32 devices in a mesh: dp: 16 (over z, x, core), tp: 2 (over y).
Axes of the slice: x: 2, y: 2, z: 4, core: 2. Of those that a mesh axis runs over, the one named last changes fastest.
Arguments:
- tokens: bfloat16 [8192, 1152], P('dp'), may hold values from -6 to 6
- condition: float32 [32, 1152], P('dp'), may hold values from -6 to 6
- noise_times: float32 [32], P('dp'), may hold values from 0 to 1
- cotangent: bfloat16 [8192, 1152], P('dp'), may hold values from -6 to 6
- ada_weight: bfloat16 [1152, 6912], P(None, 'tp'), may hold values from -0.1875 to 0.1875
- ada_bias: float32 [6912], P('tp'), may hold values from -3 to 3
- qkv_weight: bfloat16 [1152, 3, 1152], P(None, None, 'tp'), may hold values from -0.1875 to 0.1875
- qv_bias: float32 [2, 1152], P(None, 'tp'), may hold values from -3 to 3
- out_weight: bfloat16 [1152, 1152], P('tp'), may hold values from -1.5 to 1.5
- out_bias: float32 [1152], replicated, may hold values from -3 to 3
- fc1_weight: bfloat16 [1152, 4608], P(None, 'tp'), may hold values from -0.1875 to 0.1875
- fc1_bias: float32 [4608], P('tp'), may hold values from -3 to 3
- fc2_weight: bfloat16 [4608, 1152], P('tp'), may hold values from -0.09375 to 0.09375
- fc2_bias: float32 [1152], replicated, may hold values from -3 to 3
Outputs:
- output: bfloat16 [8192, 1152], P('dp')
- grad_tokens: bfloat16 [8192, 1152], P('dp')
- grad_condition: float32 [32, 1152], P('dp')
- grad_ada_weight: float32 [1152, 6912], P('dp', 'tp')
- grad_ada_bias: float32 [6912], P('tp')
- grad_qkv_weight: float32 [1152, 3, 1152], P('dp', None, 'tp')
- grad_qv_bias: float32 [2, 1152], P(None, 'tp')
- grad_out_weight: float32 [1152, 1152], P('tp', 'dp')
- grad_out_bias: float32 [1152], replicated
- grad_fc1_weight: float32 [1152, 4608], P('dp', 'tp')
- grad_fc1_bias: float32 [4608], P('tp')
- grad_fc2_weight: float32 [4608, 1152], P('tp', 'dp')
- grad_fc2_bias: float32 [1152], replicated
The draws below stay inside these ranges and needn't reach their ends.
All inputs are finite; a program needn't handle non-finite values.
Results may differ from the reference program's by a relative error of at most 0.02.
The reference program's roundings to bfloat16 on the way count: a program that leaves them out, or rounds other values in their place, can miss the bound.
Values may be sent and summed in bfloat16 or wider, within the bound.
A program may use at most 192 MiB of HBM per device.

```python
import math
import jax
import jax.numpy as jnp
from jax import lax

D = 1152
HEADS = 16
HEAD_DIM = 72
FF = 4608
SEQ = 256
IMG_DEV = 2
IMAGES = 32
TOKENS = 8192
N_DP = 16


def raised(array, own_key, source, target, shards_of, factor):
    def block_of(dim):
        return (jnp.arange(array.shape[dim]) // (array.shape[dim] // shards_of)).reshape((-1,) + (1,) * (array.ndim - 1 - dim))

    one_side = jax.random.permutation(own_key, shards_of)[block_of(target)]
    second = (block_of(target) + shards_of // 2) % shards_of
    return jnp.where((block_of(source) == one_side) | (block_of(source) == second), factor * array, array)


def block_scale(stream_key, shape, cuts, low, high):
    def one(dim, shards_of):
        heights = jax.random.uniform(jax.random.fold_in(jax.random.fold_in(stream_key, 6), dim), (shards_of,), jnp.float32, low / len(cuts), high / len(cuts))
        return jnp.repeat(jnp.exp(heights), shape[dim] // shards_of).reshape((-1,) + (1,) * (len(shape) - dim - 1))

    level = one(*cuts[0])
    for cut in cuts[1:]:
        level = level * one(*cut)
    return level


def noise(own_key, shape, width, reach, cuts=(), dtype=jnp.bfloat16):
    values = width * jax.random.normal(own_key, shape, jnp.float32)
    if cuts:
        values = values * block_scale(own_key, shape, cuts, -0.22, 0.18)
    return jnp.clip(values, -reach, reach).astype(dtype)


def bell_draw_with(key, shape, deviation, reach, split, heavy, kind=jnp.bfloat16):
    values = deviation * jax.random.normal(key, shape, jnp.float32)
    if split:
        values = values * block_scale(key, shape, split, -0.22, 0.18)
    return jnp.clip(raised(values, jax.random.fold_in(key, 3), *heavy), -reach, reach).astype(kind)


def setup_inputs(seed: int = 0) -> dict:
    streams_of = jax.random.split(jax.random.key(seed), 15)
    return {
        "tokens": bell_draw_with(streams_of[0], (TOKENS, D), 1.0, 6.0, ((0, 16),), (0, 1, 16, 2.0)),
        "condition": noise(streams_of[1], (IMAGES, D), 1.0, 6.0, ((0, 16),), jnp.float32),
        "noise_times": jnp.clip(1.0 * jax.random.uniform(streams_of[2], (IMAGES,), jnp.float32) ** block_scale(streams_of[2], (IMAGES,), ((0, 16),), -0.2, 0.2), 0.0, 1.0),
        "cotangent": bell_draw_with(streams_of[3], (TOKENS, D), 1.0, 6.0, ((0, 16),), (0, 1, 16, 2.0)),
        "ada_weight": noise(streams_of[4], (D, 6 * D), D ** -0.5, 0.1875, ((1, 2),)),
        "ada_bias": noise(streams_of[5], (6 * D,), 0.5, 3.0, ((0, 2),), jnp.float32),
        "qkv_weight": noise(streams_of[6], (D, 3, D), D ** -0.5, 0.1875, ((2, 2),)),
        "qv_bias": noise(streams_of[7], (2, D), 0.5, 3.0, ((1, 2),), jnp.float32),
        "out_weight": noise(streams_of[8], (D, D), (D // 64) ** -0.5, 1.5, ((0, 2),)),
        "out_bias": noise(streams_of[9], (D,), 0.5, 3.0, (), jnp.float32),
        "fc1_weight": noise(streams_of[10], (D, FF), D ** -0.5, 0.1875, ((1, 2),)),
        "fc1_bias": noise(streams_of[11], (FF,), 0.5, 3.0, ((0, 2),), jnp.float32),
        "fc2_weight": noise(streams_of[12], (FF, D), FF ** -0.5, 0.09375, ((0, 2),)),
        "fc2_bias": noise(streams_of[13], (D,), 0.5, 3.0, (), jnp.float32),
    }


@jax.custom_vjp
def low(v):
    return lax.optimization_barrier(v.astype(jnp.bfloat16)).astype(jnp.float32)

@jax.custom_vjp
def low_back(v):
    return v

def low_keep(v):
    return (low(v), None)

def low_pass(kept, grad):
    return (grad,)

def back_keep(v):
    return (v, None)

def back_low(kept, grad):
    return (low(grad),)
low.defvjp(low_keep, low_pass)
low_back.defvjp(back_keep, back_low)
norm_eps = 1e-06
gelu_coef = 0.7978845608028654

def matmul(former, latter):
    return jnp.dot(former, latter, precision=lax.Precision.HIGHEST, preferred_element_type=jnp.float32)

def layer_norm(values):
    center = values - lax.optimization_barrier(jnp.mean(values, axis=-1, keepdims=True))
    variance = lax.optimization_barrier(jnp.mean(center * center, axis=-1, keepdims=True))
    return center * lax.rsqrt(variance + norm_eps)

def gelu_tanh(values):
    return 0.5 * values * (1.0 + jnp.tanh(gelu_coef * (values + 0.044715 * values * values * values)))

def time_features(noise_times):
    half_width = D // 2
    ladder = jnp.arange(half_width).astype(jnp.float32)
    frequency = jnp.exp(-math.log(10000.0) * ladder / half_width)
    angles = 1000.0 * noise_times[:, None] * frequency[None, :]
    return jnp.concatenate([jnp.cos(angles), jnp.sin(angles)], axis=1)

def sit_block(params, tokens, condition, features):
    ada_weight, ada_bias, qkv_weight, qv_bias, out_weight, out_bias, fc1_weight, fc1_bias, fc2_weight, fc2_bias = params
    images = condition.shape[0]
    silu_cond = low(jax.nn.silu(condition + features))
    modulation = matmul(silu_cond, ada_weight) + ada_bias
    pieces = modulation.reshape(images, 6, 1, D)
    residual = tokens.reshape(images, SEQ, D)
    input_a = low(layer_norm(residual) * (1.0 + pieces[:, 1]) + pieces[:, 0]).reshape(images * SEQ, D)
    projected = matmul(input_a, qkv_weight.reshape(D, 3 * D)).reshape(images, SEQ, 3, HEADS, HEAD_DIM)
    queries = low(low_back(projected[:, :, 0] + qv_bias[0].reshape(HEADS, HEAD_DIM)))
    key_rows = low(low_back(projected[:, :, 1]))
    value_rows = low(low_back(projected[:, :, 2] + qv_bias[1].reshape(HEADS, HEAD_DIM)))
    scores = low_back(jnp.einsum('nqhd,nkhd->nhqk', queries, key_rows, precision=lax.Precision.HIGHEST) * (1.0 / math.sqrt(HEAD_DIM)))
    weights = low(jnp.exp(scores - jax.nn.logsumexp(scores, axis=-1, keepdims=True)))
    attended = low(low_back(jnp.einsum('nhqk,nkhd->nqhd', weights, value_rows, precision=lax.Precision.HIGHEST))).reshape(images * SEQ, D)
    attention = low_back(matmul(attended, out_weight) + out_bias).reshape(images, SEQ, D)
    middle = residual + pieces[:, 2] * attention
    input_b = low(layer_norm(middle) * (1.0 + pieces[:, 4]) + pieces[:, 3]).reshape(images * SEQ, D)
    hidden_pre = low_back(matmul(input_b, fc1_weight) + fc1_bias)
    hidden = low(gelu_tanh(hidden_pre))
    branch = low_back(matmul(hidden, fc2_weight) + fc2_bias).reshape(images, SEQ, D)
    return (middle + pieces[:, 5] * branch).reshape(images * SEQ, D)

def reference(tokens, condition, noise_times, cotangent, ada_weight, ada_bias, qkv_weight, qv_bias, out_weight, out_bias, fc1_weight, fc1_bias, fc2_weight, fc2_bias):
    params = tuple((member.astype(jnp.float32) for member in (ada_weight, ada_bias, qkv_weight, qv_bias, out_weight, out_bias, fc1_weight, fc1_bias, fc2_weight, fc2_bias)))
    features = time_features(noise_times.astype(jnp.float32))
    group_tokens = IMG_DEV * SEQ
    stacked = (tokens.astype(jnp.float32).reshape(N_DP, group_tokens, D), condition.astype(jnp.float32).reshape(N_DP, IMG_DEV, D), features.reshape(N_DP, IMG_DEV, D), cotangent.astype(jnp.float32).reshape(N_DP, group_tokens, D))

    def one_group(totals, member):
        group_tok, group_cond, group_feat, group_cot = member

        def forward(all_params, inputs, cond_in):
            return sit_block(all_params, inputs, cond_in, group_feat)
        result, pullback = jax.vjp(forward, params, group_tok, group_cond)
        grad_params, grad_tok, grad_cond = pullback(group_cot)
        totals = jax.tree.map(lambda former, latter: former + latter, totals, grad_params)
        return (totals, (result.astype(jnp.bfloat16), grad_tok.astype(jnp.bfloat16), grad_cond))
    zeros = jax.tree.map(jnp.zeros_like, params)
    totals, (outputs, grad_toks, grad_conds) = lax.scan(one_group, zeros, stacked)
    factor = 1.0 / math.sqrt(TOKENS)
    g_ada, g_ada_bias, g_qkv, g_qv_bias, g_out, g_out_bias, g_fc1, g_fc1_bias, g_fc2, g_fc2_bias = totals
    return (outputs.reshape(TOKENS, D), grad_toks.reshape(TOKENS, D), grad_conds.reshape(IMAGES, D), g_ada * factor, g_ada_bias * factor, g_qkv * factor, g_qv_bias * factor, g_out * factor, g_out_bias * factor, g_fc1 * factor, g_fc1_bias * factor, g_fc2 * factor, g_fc2_bias * factor)
```

```python
import functools
import math

import jax
import jax.numpy as jnp
from jax import lax
from jax.experimental import pallas as pl
from jax.experimental.pallas import tpu as pltpu
from jax.sharding import PartitionSpec as P

D = 1152
HEAD_DIM = 72
SEQ = 256


norm_eps = 1e-06
gelu_coef = 0.7978845608028654


def layer_norm(values):
    center = values - jnp.mean(values, axis=-1, keepdims=True)
    variance = jnp.mean(center * center, axis=-1, keepdims=True)
    return center * lax.rsqrt(variance + norm_eps)


def gelu_tanh(values):
    return (
        0.5 * values * (1.0 + jnp.tanh(gelu_coef * (values + 0.044715 * values * values * values)))
    )


def time_features(noise_times):
    half_width = D // 2
    ladder = jnp.arange(half_width).astype(jnp.float32)
    frequency = jnp.exp(-math.log(10000.0) * ladder / half_width)
    angles = 1000.0 * noise_times[:, None] * frequency[None, :]
    return jnp.concatenate([jnp.cos(angles), jnp.sin(angles)], axis=1)


def contract_rows(former, latter):
    return lax.dot_general(
        former, latter, (((0,), (0,)), ((), ())), preferred_element_type=jnp.float32
    )


def contract_cols(former, latter):
    return lax.dot_general(
        former, latter, (((1,), (1,)), ((), ())), preferred_element_type=jnp.float32
    )


def feed_up(input_b, fc1_weight, fc1_bias, fc2_weight):
    hidden_pre = jnp.dot(input_b, fc1_weight, preferred_element_type=jnp.float32) + fc1_bias
    hidden_act, gelu_pull = jax.vjp(gelu_tanh, hidden_pre)
    hidden = hidden_act.astype(jnp.bfloat16)
    return (hidden, gelu_pull, jnp.dot(hidden, fc2_weight, preferred_element_type=jnp.float32))


def plain(
    tokens,
    condition,
    noise_times,
    cotangent,
    ada_weight,
    ada_bias,
    qkv_weight,
    qv_bias,
    out_weight,
    out_bias,
    fc1_weight,
    fc1_bias,
    fc2_weight,
    fc2_bias,
):
    images = condition.shape[0]
    row_count = tokens.shape[0]
    local_width = qkv_weight.shape[2]
    local_heads = local_width // HEAD_DIM
    ada_cols = ada_weight.shape[1]
    score_scale = 1.0 / math.sqrt(HEAD_DIM)
    cond_total = condition + time_features(noise_times)
    silu_cond, silu_pull = jax.vjp(jax.nn.silu, cond_total)
    silu_low = silu_cond.astype(jnp.bfloat16)
    mod_part = jnp.dot(silu_low, ada_weight, preferred_element_type=jnp.float32) + ada_bias
    modulation = lax.all_gather(mod_part, "tp", axis=1, tiled=True)
    pieces = modulation.reshape(images, 6, 1, D)
    residual = tokens.astype(jnp.float32).reshape(images, SEQ, D)
    normed_one, norm_one_pull = jax.vjp(layer_norm, residual)
    input_a = (
        (normed_one * (1.0 + pieces[:, 1]) + pieces[:, 0])
        .astype(jnp.bfloat16)
        .reshape(row_count, D)
    )
    qkv_flat = qkv_weight.reshape(D, 3 * local_width)
    projected = jnp.dot(input_a, qkv_flat, preferred_element_type=jnp.float32).reshape(
        images, SEQ, 3, local_heads, HEAD_DIM
    )
    queries = (projected[:, :, 0] + qv_bias[0].reshape(local_heads, HEAD_DIM)).astype(jnp.bfloat16)
    key_rows = projected[:, :, 1].astype(jnp.bfloat16)
    value_rows = (projected[:, :, 2] + qv_bias[1].reshape(local_heads, HEAD_DIM)).astype(
        jnp.bfloat16
    )
    scores = (
        jnp.einsum("nqhd,nkhd->nhqk", queries, key_rows, preferred_element_type=jnp.float32)
        * score_scale
    )
    log_total = jax.nn.logsumexp(scores, axis=-1, keepdims=True)
    weights = jnp.exp(scores - log_total)
    weights_low = weights.astype(jnp.bfloat16)
    attended = (
        jnp.einsum("nhqk,nkhd->nqhd", weights_low, value_rows, preferred_element_type=jnp.float32)
        .astype(jnp.bfloat16)
        .reshape(row_count, local_width)
    )
    attn_part = jnp.dot(attended, out_weight, preferred_element_type=jnp.float32)
    attention = lax.psum(attn_part, "tp") + out_bias
    attention = attention.reshape(images, SEQ, D)
    middle = residual + pieces[:, 2] * attention
    normed_two, norm_two_pull = jax.vjp(layer_norm, middle)
    input_b = (
        (normed_two * (1.0 + pieces[:, 4]) + pieces[:, 3])
        .astype(jnp.bfloat16)
        .reshape(row_count, D)
    )
    hidden, gelu_pull, mlp_part = feed_up(input_b, fc1_weight, fc1_bias, fc2_weight)
    branch = lax.psum(mlp_part.astype(jnp.bfloat16), "tp").astype(jnp.float32) + fc2_bias
    branch = branch.reshape(images, SEQ, D)
    output = (middle + pieces[:, 5] * branch).reshape(row_count, D).astype(jnp.bfloat16)
    grad_out = cotangent.astype(jnp.float32).reshape(images, SEQ, D)
    grad_gate_two = jnp.sum(grad_out * branch, axis=1)
    grad_branch = (grad_out * pieces[:, 5]).astype(jnp.bfloat16).reshape(row_count, D)
    bias_fc2 = jnp.sum(grad_branch.astype(jnp.float32), axis=0)
    weight_fc2 = contract_rows(hidden, grad_branch)
    grad_hidden = contract_cols(grad_branch, fc2_weight)
    grad_pre = gelu_pull(grad_hidden)[0].astype(jnp.bfloat16)
    bias_fc1 = jnp.sum(grad_pre.astype(jnp.float32), axis=0)
    weight_fc1 = contract_rows(input_b, grad_pre)
    grad_input_b = lax.psum(contract_cols(grad_pre, fc1_weight), "tp").reshape(images, SEQ, D)
    grad_shift_two = jnp.sum(grad_input_b, axis=1)
    grad_scale_two = jnp.sum(grad_input_b * normed_two, axis=1)
    grad_middle = grad_out + norm_two_pull(grad_input_b * (1.0 + pieces[:, 4]))[0]
    grad_gate_one = jnp.sum(grad_middle * attention, axis=1)
    grad_attention = (grad_middle * pieces[:, 2]).astype(jnp.bfloat16).reshape(row_count, D)
    bias_out = jnp.sum(grad_attention.astype(jnp.float32), axis=0)
    weight_out = contract_rows(attended, grad_attention)
    grad_attended = (
        contract_cols(grad_attention, out_weight)
        .astype(jnp.bfloat16)
        .reshape(images, SEQ, local_heads, HEAD_DIM)
    )
    scores_again = (
        jnp.einsum("nqhd,nkhd->nhqk", queries, key_rows, preferred_element_type=jnp.float32)
        * score_scale
    )
    soft_rows = jnp.exp(scores_again - log_total)
    soft_low = soft_rows.astype(jnp.bfloat16)
    grad_values = jnp.einsum(
        "nhqk,nqhd->nkhd", soft_low, grad_attended, preferred_element_type=jnp.float32
    ).astype(jnp.bfloat16)
    grad_soft = jnp.einsum(
        "nqhd,nkhd->nhqk", grad_attended, value_rows, preferred_element_type=jnp.float32
    )
    row_dot = jnp.sum(soft_rows * grad_soft, axis=-1, keepdims=True)
    grad_scores = (soft_rows * (grad_soft - row_dot)).astype(jnp.bfloat16)
    grad_queries = (
        jnp.einsum("nhqk,nkhd->nqhd", grad_scores, key_rows, preferred_element_type=jnp.float32)
        * score_scale
    ).astype(jnp.bfloat16)
    grad_keys = (
        jnp.einsum("nhqk,nqhd->nkhd", grad_scores, queries, preferred_element_type=jnp.float32)
        * score_scale
    ).astype(jnp.bfloat16)
    grad_projected = jnp.stack([grad_queries, grad_keys, grad_values], axis=2).reshape(
        row_count, 3 * local_width
    )
    bias_qv = jnp.stack(
        [
            jnp.sum(grad_queries.astype(jnp.float32), axis=(0, 1)).reshape(local_width),
            jnp.sum(grad_values.astype(jnp.float32), axis=(0, 1)).reshape(local_width),
        ]
    )
    weight_qkv = contract_rows(input_a, grad_projected).reshape(D, 3, local_width)
    grad_input_a = lax.psum(contract_cols(grad_projected, qkv_flat), "tp").reshape(images, SEQ, D)
    grad_shift_one = jnp.sum(grad_input_a, axis=1)
    grad_scale_one = jnp.sum(grad_input_a * normed_one, axis=1)
    grad_tokens = (
        (grad_middle + norm_one_pull(grad_input_a * (1.0 + pieces[:, 1]))[0])
        .reshape(row_count, D)
        .astype(jnp.bfloat16)
    )
    grad_mod = jnp.stack(
        [
            grad_shift_one,
            grad_scale_one,
            grad_gate_one,
            grad_shift_two,
            grad_scale_two,
            grad_gate_two,
        ],
        axis=1,
    ).reshape(images, 6 * D)
    grad_mod_mine = lax.dynamic_slice_in_dim(grad_mod, lax.axis_index("tp") * ada_cols, ada_cols, 1)
    bias_ada = jnp.sum(grad_mod_mine, axis=0)
    weight_ada = lax.dot_general(
        silu_low.astype(jnp.float32),
        grad_mod_mine,
        (((0,), (0,)), ((), ())),
        precision=lax.Precision.HIGHEST,
        preferred_element_type=jnp.float32,
    )
    silu_part = lax.dot_general(
        grad_mod_mine,
        ada_weight.astype(jnp.float32),
        (((1,), (1,)), ((), ())),
        precision=lax.Precision.HIGHEST,
        preferred_element_type=jnp.float32,
    )
    grad_silu = lax.psum(silu_part, "tp")
    grad_condition = silu_pull(grad_silu)[0]
    factor = 1.0 / math.sqrt(row_count * lax.axis_size("dp"))
    sum_ada, sum_qkv, sum_out, sum_fc1, sum_fc2 = (
        lax.psum_scatter(
            weight_ada.astype(jnp.bfloat16), "dp", scatter_dimension=0, tiled=True
        ).astype(jnp.float32),
        lax.psum_scatter(
            weight_qkv.astype(jnp.bfloat16), "dp", scatter_dimension=0, tiled=True
        ).astype(jnp.float32),
        lax.psum_scatter(
            weight_out.astype(jnp.bfloat16), "dp", scatter_dimension=1, tiled=True
        ).astype(jnp.float32),
        lax.psum_scatter(
            weight_fc1.astype(jnp.bfloat16), "dp", scatter_dimension=0, tiled=True
        ).astype(jnp.float32),
        lax.psum_scatter(
            weight_fc2.astype(jnp.bfloat16), "dp", scatter_dimension=1, tiled=True
        ).astype(jnp.float32),
    )
    total_ada, total_qv, total_out, total_fc1, total_fc2 = lax.psum(
        (bias_ada, bias_qv, bias_out, bias_fc1, bias_fc2), "dp"
    )
    return (
        output,
        grad_tokens,
        grad_condition,
        sum_ada * factor,
        total_ada * factor,
        sum_qkv * factor,
        total_qv * factor,
        sum_out * factor,
        total_out * factor,
        sum_fc1 * factor,
        total_fc1 * factor,
        sum_fc2 * factor,
        total_fc2 * factor,
    )


NORM_EPS = 1e-06
GELU_COEF = 0.7978845608028654
GELU_CUBE = 0.044715
MESH = pl.DeviceIdType.MESH
F32 = jnp.float32
BF16 = jnp.bfloat16


def dot_nn(a, b):
    return lax.dot_general(a, b, (((1,), (0,)), ((), ())), preferred_element_type=F32)


def dot_nt(a, b):
    return lax.dot_general(a, b, (((1,), (1,)), ((), ())), preferred_element_type=F32)


def dot_tn(a, b):
    return lax.dot_general(a, b, (((0,), (0,)), ((), ())), preferred_element_type=F32)


def norm_parts(values):
    center = values - jnp.mean(values, axis=-1, keepdims=True)
    scale = lax.rsqrt(jnp.mean(center * center, axis=-1, keepdims=True) + NORM_EPS)
    return center * scale, scale


def fold_rows(values):
    rows, cols = values.shape
    return jnp.sum(values.reshape(rows // 8, 8, cols), axis=0)


def al(index, unit):
    return pl.multiple_of(index, unit)


RC = 16
PW = 384
NP = 3


def block_kernel(
    factor,
    tok_h, cot_h, ada_h, w3_h, wo_h, w1_h, w2_h, silu_r, adab_r, qvb_r, ob_r, b1_r, b2_r,
    out_h, gt_h, g2_h, g1_h, g3_h, gmod_o, bfc1_o, brow_o, bqv_o,
    big, w3, wo, w1, w2, tok, cot, ia, ib, gb, qkv, prob, att, attn, mid, hid, gpre,
    gibs, gibr, g4, at1, rx, rx3, rz, rz3, ry, ry3, fin, fin3, modb, gmod,
    ld_sem, out_sem, ss, rs, cred,
):
    dp, tp = lax.axis_index("dp"), lax.axis_index("tp")
    z, x, c = dp // 4, (dp // 2) % 2, dp % 2
    zp, zh = z % 2, z // 2
    dev_y = (dp, 1 - tp)
    dev_c = (z * 4 + x * 2 + 1 - c, tp)
    dev_x = (z * 4 + (1 - x) * 2 + c, tp)
    dev_z = ((z + 1 - 2 * zp) * 4 + x * 2 + c, tp)
    dev_w = (((z + 2) % 4) * 4 + x * 2 + c, tp)

    T, D = tok.shape
    SEQ = T // 2
    L = wo_h.shape[0]
    LP = qkv.shape[2]
    F = w1.shape[1]
    A = modb.shape[2]
    scale = 1.0 / math.sqrt(72)
    blk = D // 8

    barrier = pltpu.get_barrier_semaphore()
    for dev in (dev_y, dev_c, dev_x, dev_z, dev_w):
        pl.semaphore_signal(barrier, inc=1, device_id=dev, device_id_type=MESH)

    counter = [0]

    def remote(src, dst, dev):
        k = counter[0]
        counter[0] += 1
        return pltpu.make_async_remote_copy(
            src_ref=src, dst_ref=dst, send_sem=ss.at[k], recv_sem=rs.at[k],
            device_id=dev, device_id_type=MESH,
        )

    lcount = [0]

    def load(src, dst):
        k = lcount[0]
        lcount[0] += 1
        cp = pltpu.make_async_copy(src, dst, ld_sem.at[k])
        cp.start()
        return cp

    ocount = [0]

    def store(src, dst):
        k = ocount[0]
        ocount[0] += 1
        cp = pltpu.make_async_copy(src, dst, out_sem.at[k])
        cp.start()
        return cp

    NA = A // PW
    ld_ada = [load(ada_h.at[:, PW * k : PW * (k + 1)], big.at[k]) for k in range(NA)]
    ld_tok = load(tok_h, tok)
    ld_w3 = [load(w3_h.at[j], w3.at[j, 0:L]) for j in range(3)]
    for j in range(3):
        w3[j, L:LP, :] = jnp.zeros((LP - L, D), BF16)
    for j in range(2):
        wo[j, L:LP, :] = jnp.zeros((LP - L, D), BF16)

    silu = silu_r[...].astype(BF16)
    for k in range(NA):
        ld_ada[k].wait()
        part = dot_nn(silu, big[k])[0:2] + adab_r[:, PW * k : PW * (k + 1)]
        modb[tp, :, PW * k : PW * (k + 1)] = part
    pl.semaphore_wait(barrier, 5)
    pl.semaphore_signal(cred.at[0], inc=1, device_id=dev_c, device_id_type=MESH)
    cp_mod = remote(modb.at[tp], modb.at[tp], dev_y)
    cp_mod.start()
    half = L // 2
    cp_wo = remote(
        wo_h.at[pl.ds(al(c * half, 16), half)], wo.at[tp, pl.ds(al(c * half, 16), half)], dev_y
    )
    cp_wo.start()
    ld_wo = load(wo_h, wo.at[tp, 0:L])
    ld_cot = load(cot_h, cot)
    ld_w1 = load(w1_h, w1)
    ld_w2 = load(w2_h, w2)
    ld_tok.wait()
    cp_mod.wait()

    def mvec(which, img):
        return modb[which // 3, img : img + 1, (which % 3) * D : (which % 3 + 1) * D]

    def rows_loop(img, body, init=None, step=RC):
        base = img * SEQ

        def one(r, carry):
            return body(pl.ds(al(base + r * step, step), step), carry)

        return lax.fori_loop(0, SEQ // step, one, init)

    def zeros8(n):
        return tuple(jnp.zeros((8, D), F32) for _ in range(n))

    def total(part):
        return jnp.sum(part, axis=0, keepdims=True)

    for img in range(2):
        shift, sc = mvec(0, img), 1.0 + mvec(1, img)

        def body(rows, carry):
            normed, _ = norm_parts(tok[rows, :].astype(F32))
            ia[rows, :] = (normed * sc + shift).astype(BF16)
            return carry

        rows_loop(img, body, 0)

    for j in range(3):
        ld_w3[j].wait()

    def qkv_body(j, carry):
        qkv[j] = (dot_nt(ia[...], w3[j]) + qvb_r[j]).astype(BF16)
        return carry

    lax.fori_loop(0, 3, qkv_body, 0)

    lane = lax.broadcasted_iota(jnp.int32, (1, 256), 1)

    def head_mask(j, e):
        lo = 16 * j + 72 * e
        return jnp.where((lane >= lo) & (lane < lo + 72), 1.0, 0.0).astype(BF16)

    def keep_low(j, old, new):
        full = lax.broadcasted_iota(jnp.int32, new.shape, 1)
        return jnp.where(full < 16 * j, old.astype(F32), new).astype(BF16)

    def attend(img):
        rows = slice(img * SEQ, (img + 1) * SEQ)

        def pair(j, carry):
            win = pl.ds(al(j * 128, 128), 256)
            q, k, v = qkv[0, rows, win], qkv[1, rows, win], qkv[2, rows, win]
            mixed = None
            for e in range(2):
                mask = head_mask(j, e)
                s = dot_nt(q * mask, k) * scale
                p = jnp.exp(s - jnp.max(s, axis=-1, keepdims=True))
                p = p * (1.0 / jnp.sum(p, axis=-1, keepdims=True))
                low = p.astype(BF16)
                prob[img * 8 + 2 * j + e] = low
                part = dot_nn(low, v * mask)
                mixed = part if mixed is None else mixed + part
            merged = keep_low(j, att[tp, rows, win], mixed)
            att[tp, rows, win] = merged
            g4[3, rows, win] = merged
            return carry

        lax.fori_loop(0, 4, pair, 0)
        cp = remote(att.at[tp, rows], att.at[tp, rows], dev_y)
        cp.start()
        return cp

    cp_att = [attend(0)]
    cp_wo.wait()
    cp_wf = remote(
        wo.at[1 - tp, pl.ds(al(c * half, 16), half)],
        wo.at[1 - tp, pl.ds(al(c * half, 16), half)],
        dev_c,
    )
    cp_wf.start()
    cp_att.append(attend(1))

    ld_cot.wait()
    acc = zeros8(1)
    for img in range(2):
        gate_b = mvec(5, img)

        def body(rows, carry):
            low = (cot[rows, :].astype(F32) * gate_b).astype(BF16)
            gb[rows, :] = low
            return (carry[0] + fold_rows(low.astype(F32)),)

        acc = rows_loop(img, body, acc)
    brow_o[1:2, :] = total(acc[0])

    def transpose_to(src, dst, base):
        def body(t, carry):
            cols = pl.ds(al(t * 128, 128), 128)
            dst[cols, base : base + T] = src[:, cols].T
            return carry

        lax.fori_loop(0, D // 128, body, 0)

    transpose_to(gb, at1, 0)

    ld_wo.wait()
    cp_wf.wait()
    ld_w1.wait()
    ld_w2.wait()

    def feed(img):
        rows = slice(img * SEQ, (img + 1) * SEQ)
        cp_att[img].wait()

        def proj(n, carry):
            cols = pl.ds(al(n * PW, 128), PW)
            attn[rows, cols] = (
                dot_nn(att[0, rows, :], wo[0, :, cols])
                + dot_nn(att[1, rows, :], wo[1, :, cols])
                + ob_r[:, cols]
            )
            return carry

        lax.fori_loop(0, D // PW, proj, 0)
        gate_a, shift_b, sc_b = mvec(2, img), mvec(3, img), 1.0 + mvec(4, img)

        def body(r, carry):
            m = tok[r, :].astype(F32) + gate_a * attn[r, :]
            mid[r, :] = m
            normed, _ = norm_parts(m)
            ib[r, :] = (normed * sc_b + shift_b).astype(BF16)
            return carry

        rows_loop(img, body, 0)

        def hidden(f, carry):
            cols = pl.ds(al(f * 256, 128), 256)
            pre = dot_nn(ib[rows, :], w1[:, cols]) + b1_r[:, cols]
            gh = dot_nt(gb[rows, :], w2[cols, :])
            sq = pre * pre
            th = jnp.tanh(GELU_COEF * pre * (1.0 + GELU_CUBE * sq))
            hp = 0.5 + 0.5 * th
            hid[rows, cols] = (pre * hp).astype(BF16)
            slope = hp + (0.5 * GELU_COEF) * pre * (1.0 - th * th) * (
                1.0 + (3.0 * GELU_CUBE) * sq
            )
            low = (gh * slope).astype(BF16)
            gpre[rows, cols] = low
            col_sum = jnp.sum(low.astype(F32), axis=0, keepdims=True)
            if img == 0:
                bfc1_o[:, cols] = col_sum
            else:
                bfc1_o[:, cols] = bfc1_o[:, cols] + col_sum
            return carry

        lax.fori_loop(0, F // 256, hidden, 0)

        def back(n, carry):
            cols = pl.ds(al(n * PW, 128), PW)
            gibs[rows, cols] = dot_nt(gpre[rows, :], w1[cols, :]).astype(BF16)
            return carry

        lax.fori_loop(0, D // PW, back, 0)
        cp = remote(gibs.at[rows], gibr.at[rows], dev_y)
        cp.start()
        return cp

    cp_gib = [feed(0), feed(1)]


    LO1, LO2 = 2 * LP, 2 * LP + T
    pl.semaphore_signal(cred.at[1], inc=1, device_id=dev_c, device_id_type=MESH)
    pl.semaphore_wait(cred.at[0], 1)
    cp_c, cp_x, cp_z, cp_w, cp_f, cp_o = {}, {}, {}, {}, {}, {}

    def place(s):
        zz, xx = s // 2, s % 2
        return (xx * 4 + (zz % 2) * 2 + zz // 2) * blk

    def product(p, h):
        if p < 2 * NP:
            cols = pl.ds(al(h * (F // 2) + PW * (p % NP), 128), PW)
            return dot_nn(at1[...], (hid if p < NP else gpre)[:, cols])
        q = p - 2 * NP
        base = LO1 if q == 0 else al(LO1 + h * T, 128)
        return dot_nn(w1[:, pl.ds(base, T)], g4[2 * h + q])

    def land_c(p):
        if p < 2 * NP:
            return big.at[p]
        return w1.at[:, (p - 2 * NP) * LP : (p - 2 * NP + 1) * LP]

    def land(plain, wide, p):
        return plain.at[p] if p < 2 * NP else wide.at[p - 2 * NP]

    def theirs(p):
        res = product(p, 1 - c)
        if p < 2 * NP:
            slot = big.at[6 + p % NP]
            if p >= NP:
                cp_c[p - NP].wait_send()
        else:
            slot = w2.at[0:D, 0:LP]
            if p == 2 * NP:
                pl.semaphore_wait(cred.at[1], 1)
            else:
                cp_c[p - 1].wait_send()
        for s in range(8):
            slot[place(s) : place(s) + blk, :] = res[s * blk : (s + 1) * blk].astype(BF16)
        cp_c[p] = remote(slot, land_c(p), dev_c)
        cp_c[p].start()

    def mine(p):
        res = product(p, c)
        cp_c[p].wait_recv()
        ref = land_c(p)
        for s in range(8):
            rows = slice(place(s), place(s) + blk)
            ref[rows, :] = (res[s * blk : (s + 1) * blk] + ref[rows, :].astype(F32)).astype(BF16)
        rows = pl.ds(al((1 - x) * 4 * blk, 16), 4 * blk)
        cp_x[p] = remote(ref.at[rows], land(rx, rx3, p), dev_x)
        cp_x[p].start()

    def merge(p, base, arrived, count):
        ref = land_c(p)

        def body(i, carry):
            rows = pl.ds(al(base + i * blk, 16), blk)
            got = arrived[pl.ds(al(i * blk, 16), blk), :].astype(F32)
            ref[rows, :] = (ref[rows, :].astype(F32) + got).astype(BF16)
            return carry

        lax.fori_loop(0, count, body, 0)

    base_x = x * 4 * blk
    base_z = base_x + zp * 2 * blk
    base_w = base_z + zh * blk

    def step_x(p):
        cp_x[p].wait_recv()
        merge(p, base_x, land(rx, rx3, p), 4)
        rows = pl.ds(al(base_x + (1 - zp) * 2 * blk, 16), 2 * blk)
        cp_z[p] = remote(land_c(p).at[rows], land(rz, rz3, p), dev_z)
        cp_z[p].start()

    def step_z(p):
        cp_z[p].wait_recv()
        merge(p, base_z, land(rz, rz3, p), 2)
        rows = pl.ds(al(base_z + (1 - zh) * blk, 16), blk)
        cp_w[p] = remote(land_c(p).at[rows], land(ry, ry3, p), dev_w)
        cp_w[p].start()

    def drain(p):
        cp_o[p].wait()
        cp_f[p].wait_send()

    def step_w(p):
        cp_w[p].wait_recv()
        both = land_c(p)[pl.ds(al(base_w, 16), blk), :].astype(F32)
        both = (both + land(ry, ry3, p)[...].astype(F32)) * factor
        keep, give = pl.ds(al(c * (blk // 2), 8), blk // 2), pl.ds(al((1 - c) * (blk // 2), 8), blk // 2)
        if p < 2 * NP:
            if p >= 2:
                drain(p - 2)
            stage = fin.at[p % 2]
            stage[...] = both
            cols = pl.ds(al(c * (F // 2) + PW * (p % NP), 128), PW)
            dst = (g2_h if p < NP else g1_h).at[:, cols]
        else:
            stage = fin3.at[p - 2 * NP]
            stage[...] = both[:, 0:L]
            dst = g3_h.at[2 * c + p - 2 * NP]
        cp_o[p] = store(stage.at[keep], dst)
        cp_f[p] = remote(stage.at[give], dst, dev_c)
        cp_f[p].start()

    def branch(img):
        rows = slice(img * SEQ, (img + 1) * SEQ)

        def body(n, carry):
            cols = pl.ds(al(n * PW, 128), PW)
            ib[rows, cols] = dot_nn(hid[rows, :], w2[:, cols]).astype(BF16)
            return carry

        lax.fori_loop(0, D // PW, body, 0)

    def send_branch():
        pl.semaphore_signal(cred.at[4], inc=1, device_id=dev_y, device_id_type=MESH)
        pl.semaphore_wait(cred.at[4], 1)
        cp = remote(ib, w2.at[D : D + T], dev_y)
        cp.start()
        return cp

    bo_acc = [zeros8(1)[0]]
    tails = []

    def norm_b_back(img):
        cp_gib[img].wait()
        gate_a, sc_b = mvec(2, img), 1.0 + mvec(4, img)

        def body(r, carry):
            s_shift, s_scale, s_gate, s_bias = carry
            g = gibs[r, :].astype(F32) + gibr[r, :].astype(F32)
            normed, inv = norm_parts(mid[r, :])
            s_shift += fold_rows(g)
            s_scale += fold_rows(g * normed)
            u = g * sc_b
            m1 = jnp.mean(u, axis=-1, keepdims=True)
            m2 = jnp.mean(u * normed, axis=-1, keepdims=True)
            gm = cot[r, :].astype(F32) + inv * (u - m1 - normed * m2)
            s_gate += fold_rows(gm * attn[r, :])
            low = (gm * gate_a).astype(BF16)
            gb[r, :] = low
            s_bias += fold_rows(low.astype(F32))
            attn[r, :] = gm
            return (s_shift, s_scale, s_gate, s_bias)

        sums = rows_loop(img, body, zeros8(3) + (bo_acc[0],))
        pl.semaphore_signal(cred.at[2 + img], inc=1, device_id=dev_y, device_id_type=MESH)
        gmod[1, img : img + 1, 0:D] = total(sums[0])
        gmod[1, img : img + 1, D : 2 * D] = total(sums[1])
        gmod[0, img : img + 1, 2 * D : 3 * D] = total(sums[2])
        bo_acc[0] = sums[3]
        if img == 1:
            brow_o[0:1, :] = total(bo_acc[0])

    def attend_back(img):
        rows = slice(img * SEQ, (img + 1) * SEQ)
        att[1 - tp, rows, :] = dot_nt(gb[rows, :], wo[tp]).astype(BF16)

        def pair(j, carry):
            win = pl.ds(al(j * 128, 128), 256)
            q, k, v = qkv[0, rows, win], qkv[1, rows, win], qkv[2, rows, win]
            g = att[1 - tp, rows, win]
            gq = gk = gv = None
            for e in range(2):
                mask = head_mask(j, e)
                gm = g * mask
                low = prob[img * 8 + 2 * j + e]
                p = low.astype(F32)
                gp = dot_nt(gm, v)
                ds = (p * (gp - jnp.sum(p * gp, axis=-1, keepdims=True))).astype(BF16)
                parts = dot_nn(ds, k * mask), dot_tn(ds, q * mask), dot_tn(low, gm)
                if gq is None:
                    gq, gk, gv = parts
                else:
                    gq, gk, gv = gq + parts[0], gk + parts[1], gv + parts[2]
            g4[0, rows, win] = keep_low(j, g4[0, rows, win], gq * scale)
            g4[1, rows, win] = keep_low(j, g4[1, rows, win], gk * scale)
            g4[2, rows, win] = keep_low(j, g4[2, rows, win], gv)
            return carry

        lax.fori_loop(0, 4, pair, 0)
        for n, which in enumerate((0, 2)):
            cur = jnp.sum(g4[which, rows, :].astype(F32), axis=0, keepdims=True)
            bqv_o[n : n + 1, :] = cur if img == 0 else bqv_o[n : n + 1, :] + cur

        def body(n, carry):
            cols = pl.ds(al(n * PW, 128), PW)
            part = dot_nn(g4[0, rows, :], w3[0, :, cols])
            part += dot_nn(g4[1, rows, :], w3[1, :, cols])
            part += dot_nn(g4[2, rows, :], w3[2, :, cols])
            gibs[rows, cols] = part.astype(BF16)
            return carry

        lax.fori_loop(0, D // PW, body, 0)
        pl.semaphore_wait(cred.at[2 + img], 1)
        cp = remote(gibs.at[rows], gibr.at[rows], dev_y)
        cp.start()
        return cp

    def norm_a_back(img, cp):
        cp.wait()
        sc_a = 1.0 + mvec(1, img)

        def body(r, carry):
            s_shift, s_scale = carry
            g = gibs[r, :].astype(F32) + gibr[r, :].astype(F32)
            normed, inv = norm_parts(tok[r, :].astype(F32))
            s_shift += fold_rows(g)
            s_scale += fold_rows(g * normed)
            u = g * sc_a
            m1 = jnp.mean(u, axis=-1, keepdims=True)
            m2 = jnp.mean(u * normed, axis=-1, keepdims=True)
            gb[r, :] = (attn[r, :] + inv * (u - m1 - normed * m2)).astype(BF16)
            return (s_shift, s_scale)

        sums = rows_loop(img, body, zeros8(2))
        gmod[0, img : img + 1, 0:D] = total(sums[0])
        gmod[0, img : img + 1, D : 2 * D] = total(sums[1])
        rows = slice(img * SEQ, (img + 1) * SEQ)
        tails.append(store(gb.at[rows], gt_h.at[rows]))

    def finish(img):
        gate_b = mvec(5, img)

        def body(r, carry):
            br = ib[r, :].astype(F32) + w2[pl.ds(al(D + r.start, RC), RC), :].astype(F32) + b2_r[...]
            ia[r, :] = (mid[r, :] + gate_b * br).astype(BF16)
            return (carry[0] + fold_rows(cot[r, :].astype(F32) * br),)

        sums = rows_loop(img, body, zeros8(1))
        gmod[1, img : img + 1, 2 * D : 3 * D] = total(sums[0])
        rows = slice(img * SEQ, (img + 1) * SEQ)
        tails.append(store(ia.at[rows], out_h.at[rows]))

    theirs(0)
    theirs(1)
    mine(0)
    theirs(2)
    mine(1)
    mine(2)
    transpose_to(ib, at1, 0)
    transpose_to(ia, w1, LO1)
    norm_b_back(0)
    cp_gia = [attend_back(0)]
    branch(0)
    branch(1)
    step_x(0)
    theirs(3)
    theirs(4)
    mine(3)
    norm_b_back(1)
    transpose_to(gb, w1, LO2)
    cp_gia.append(attend_back(1))
    cp_br = send_branch()
    step_x(1)
    step_z(0)
    mine(4)
    theirs(5)
    mine(5)
    theirs(6)
    mine(6)
    theirs(7)
    mine(7)
    step_w(0)
    step_x(2)
    step_z(1)
    step_w(1)
    step_x(3)
    step_z(2)
    step_w(2)
    norm_a_back(0, cp_gia[0])
    norm_a_back(1, cp_gia[1])
    step_x(4)
    step_z(3)
    step_w(3)
    cp_br.wait()
    finish(0)
    finish(1)
    gmod_o[...] = gmod[tp]
    step_x(5)
    step_z(4)
    step_w(4)
    step_x(6)
    step_z(5)
    step_w(5)
    step_x(7)
    step_z(6)
    step_w(6)
    step_z(7)
    step_w(7)

    for p in range(2 * NP + 2):
        if p >= NP and p != 2 * NP:
            cp_c[p].wait_send()
        cp_x[p].wait_send()
        cp_z[p].wait_send()
        cp_w[p].wait_send()
        if p >= 2 * NP - 2:
            drain(p)
        cp_f[p].wait_recv()
    for cp in tails:
        cp.wait()


def fused(
    tokens, condition, noise_times, cotangent, ada_weight, ada_bias, qkv_weight, qv_bias,
    out_weight, out_bias, fc1_weight, fc1_bias, fc2_weight, fc2_bias,
):
    T, width = tokens.shape
    L, F, A = qkv_weight.shape[2], fc1_weight.shape[1], ada_weight.shape[1]
    LP = -(-L // 128) * 128
    n_dp = lax.axis_size("dp")
    blk = width // 8
    factor = 1.0 / math.sqrt(T * n_dp)
    cond_total = condition + time_features(noise_times)
    silu_cond, silu_pull = jax.vjp(jax.nn.silu, cond_total)
    silu_low = silu_cond.astype(BF16)
    silu_rows = jnp.pad(silu_low.astype(F32), ((0, 6), (0, 0)))
    pad = ((0, 0), (0, LP - L))
    qvb = jnp.pad(qv_bias, pad)
    qvb = jnp.stack([qvb[0:1], jnp.zeros((1, LP), F32), qvb[1:2]])
    w3 = jnp.transpose(qkv_weight, (1, 2, 0))
    hbm, vmem = pl.BlockSpec(memory_space=pl.ANY), pl.BlockSpec(memory_space=pltpu.VMEM)
    sds = jax.ShapeDtypeStruct
    results = pl.pallas_call(
        functools.partial(block_kernel, factor),
        out_shape=(
            sds((T, width), BF16), sds((T, width), BF16),
            sds((width // n_dp, F), F32), sds((width // n_dp, F), F32),
            sds((4, width // n_dp, L), F32),
            sds((2, A), F32), sds((1, F), F32), sds((2, width), F32), sds((2, LP), F32),
        ),
        in_specs=[hbm] * 7 + [vmem] * 6,
        out_specs=(hbm,) * 5 + (vmem,) * 4,
        scratch_shapes=[
            pltpu.VMEM((A // PW, width, PW), BF16),
            pltpu.VMEM((3, LP, width), BF16),
            pltpu.VMEM((2, LP, width), BF16),
            pltpu.VMEM((width, F), BF16),
            pltpu.VMEM((F, width), BF16),
            pltpu.VMEM((T, width), BF16),
            pltpu.VMEM((T, width), BF16),
            pltpu.VMEM((T, width), BF16),
            pltpu.VMEM((T, width), BF16),
            pltpu.VMEM((T, width), BF16),
            pltpu.VMEM((3, T, LP), BF16),
            pltpu.VMEM((16, T // 2, T // 2), BF16),
            pltpu.VMEM((2, T, LP), BF16),
            pltpu.VMEM((T, width), F32),
            pltpu.VMEM((T, width), F32),
            pltpu.VMEM((T, F), BF16),
            pltpu.VMEM((T, F), BF16),
            pltpu.VMEM((T, width), BF16),
            pltpu.VMEM((T, width), BF16),
            pltpu.VMEM((4, T, LP), BF16),
            pltpu.VMEM((width, T), BF16),
            pltpu.VMEM((6, 4 * blk, PW), BF16),
            pltpu.VMEM((2, 4 * blk, LP), BF16),
            pltpu.VMEM((6, 2 * blk, PW), BF16),
            pltpu.VMEM((2, 2 * blk, LP), BF16),
            pltpu.VMEM((6, blk, PW), BF16),
            pltpu.VMEM((2, blk, LP), BF16),
            pltpu.VMEM((2, blk, PW), F32),
            pltpu.VMEM((2, blk, L), F32),
            pltpu.VMEM((2, 2, A), F32),
            pltpu.VMEM((2, 2, A), F32),
            pltpu.SemaphoreType.DMA((24,)),
            pltpu.SemaphoreType.DMA((16,)),
            pltpu.SemaphoreType.DMA((64,)),
            pltpu.SemaphoreType.DMA((64,)),
            pltpu.SemaphoreType.REGULAR((8,)),
        ],
        compiler_params=pltpu.CompilerParams(
            collective_id=0, has_side_effects=True, vmem_limit_bytes=63 * 2**20
        ),
        name="block",
    )(
        tokens, cotangent, ada_weight, w3, out_weight, fc1_weight, fc2_weight,
        silu_rows, ada_bias[None], qvb, out_bias[None], fc1_bias[None], fc2_bias[None],
    )
    output, grad_tokens, g2, g1, g4, grad_mod, b_fc1, b_row, b_qv = results
    sizes = jnp.concatenate([b_fc1[0], b_row.reshape(-1), b_qv.reshape(-1)])
    mine = jnp.concatenate([grad_mod.reshape(-1), silu_low.astype(F32).reshape(-1), sizes])
    every = lax.all_gather(mine, "dp", axis=0)
    mod_all = every[:, : 2 * A].reshape(2 * n_dp, A)
    silu_all = every[:, 2 * A : 2 * A + 2 * width].reshape(2 * n_dp, width)
    sums = jnp.sum(every[:, 2 * A + 2 * width :], axis=0) * factor
    rows = width // n_dp
    silu_cols = lax.dynamic_slice_in_dim(silu_all, lax.axis_index("dp") * rows, rows, 1)
    grad_ada = (
        lax.dot_general(
            silu_cols, mod_all, (((0,), (0,)), ((), ())),
            precision=lax.Precision.HIGHEST, preferred_element_type=F32,
        )
        * factor
    )
    ada_sum = jnp.sum(mod_all, axis=0) * factor
    silu_part = lax.dot_general(
        grad_mod, ada_weight.astype(F32), (((1,), (1,)), ((), ())),
        precision=lax.Precision.HIGHEST, preferred_element_type=F32,
    )
    grad_condition = silu_pull(lax.psum(silu_part, "tp"))[0]
    s_fc1, s_row, s_qv = sums[:F], sums[F : F + 2 * width].reshape(2, width), sums[F + 2 * width :].reshape(2, LP)
    return (
        output, grad_tokens, grad_condition, grad_ada, ada_sum,
        jnp.transpose(g4[0:3], (1, 0, 2)), s_qv[:, :L],
        g4[3].T, s_row[0], g1, s_fc1, g2.T, s_row[1],
    )


def local(*args):
    tokens, condition, qkv_weight, fc1_weight = args[0], args[1], args[6], args[10]
    fits = (
        lax.axis_size("tp") == 2 and lax.axis_size("dp") == 16
        and condition.shape[0] == 2 and tokens.shape[0] == 2 * SEQ
        and qkv_weight.shape[2] == D // 2 and fc1_weight.shape[1] == 2 * D
    )
    return fused(*args) if fits else plain(*args)


def solution(mesh):
    return jax.shard_map(
        local,
        mesh=mesh,
        in_specs=(
            P("dp", None),
            P("dp", None),
            P("dp"),
            P("dp", None),
            P(None, "tp"),
            P("tp"),
            P(None, None, "tp"),
            P(None, "tp"),
            P("tp", None),
            P(),
            P(None, "tp"),
            P("tp"),
            P("tp", None),
            P(),
        ),
        out_specs=(
            P("dp", None),
            P("dp", None),
            P("dp", None),
            P("dp", "tp"),
            P("tp"),
            P("dp", None, "tp"),
            P(None, "tp"),
            P("tp", "dp"),
            P(),
            P("dp", "tp"),
            P("tp"),
            P("tp", "dp"),
            P(),
        ),
        check_vma=False,
    )
```

```python
import functools
import math

import jax
import jax.numpy as jnp
from jax import lax
from jax.experimental import pallas as pl
from jax.experimental.pallas import tpu as pltpu
from jax.sharding import PartitionSpec as P

D = 1152
HEAD_DIM = 72
SEQ = 256


norm_eps = 1e-06
gelu_coef = 0.7978845608028654


def layer_norm(values):
    center = values - jnp.mean(values, axis=-1, keepdims=True)
    variance = jnp.mean(center * center, axis=-1, keepdims=True)
    return center * lax.rsqrt(variance + norm_eps)


def gelu_tanh(values):
    return (
        0.5 * values * (1.0 + jnp.tanh(gelu_coef * (values + 0.044715 * values * values * values)))
    )


def time_features(noise_times):
    half_width = D // 2
    ladder = jnp.arange(half_width).astype(jnp.float32)
    frequency = jnp.exp(-math.log(10000.0) * ladder / half_width)
    angles = 1000.0 * noise_times[:, None] * frequency[None, :]
    return jnp.concatenate([jnp.cos(angles), jnp.sin(angles)], axis=1)


def contract_rows(former, latter):
    return lax.dot_general(
        former, latter, (((0,), (0,)), ((), ())), preferred_element_type=jnp.float32
    )


def contract_cols(former, latter):
    return lax.dot_general(
        former, latter, (((1,), (1,)), ((), ())), preferred_element_type=jnp.float32
    )


def feed_up(input_b, fc1_weight, fc1_bias, fc2_weight):
    hidden_pre = jnp.dot(input_b, fc1_weight, preferred_element_type=jnp.float32) + fc1_bias
    hidden_act, gelu_pull = jax.vjp(gelu_tanh, hidden_pre)
    hidden = hidden_act.astype(jnp.bfloat16)
    return (hidden, gelu_pull, jnp.dot(hidden, fc2_weight, preferred_element_type=jnp.float32))


def plain(
    tokens,
    condition,
    noise_times,
    cotangent,
    ada_weight,
    ada_bias,
    qkv_weight,
    qv_bias,
    out_weight,
    out_bias,
    fc1_weight,
    fc1_bias,
    fc2_weight,
    fc2_bias,
):
    images = condition.shape[0]
    row_count = tokens.shape[0]
    local_width = qkv_weight.shape[2]
    local_heads = local_width // HEAD_DIM
    ada_cols = ada_weight.shape[1]
    score_scale = 1.0 / math.sqrt(HEAD_DIM)
    cond_total = condition + time_features(noise_times)
    silu_cond, silu_pull = jax.vjp(jax.nn.silu, cond_total)
    silu_low = silu_cond.astype(jnp.bfloat16)
    mod_part = jnp.dot(silu_low, ada_weight, preferred_element_type=jnp.float32) + ada_bias
    modulation = lax.all_gather(mod_part, "tp", axis=1, tiled=True)
    pieces = modulation.reshape(images, 6, 1, D)
    residual = tokens.astype(jnp.float32).reshape(images, SEQ, D)
    normed_one, norm_one_pull = jax.vjp(layer_norm, residual)
    input_a = (
        (normed_one * (1.0 + pieces[:, 1]) + pieces[:, 0])
        .astype(jnp.bfloat16)
        .reshape(row_count, D)
    )
    qkv_flat = qkv_weight.reshape(D, 3 * local_width)
    projected = jnp.dot(input_a, qkv_flat, preferred_element_type=jnp.float32).reshape(
        images, SEQ, 3, local_heads, HEAD_DIM
    )
    queries = (projected[:, :, 0] + qv_bias[0].reshape(local_heads, HEAD_DIM)).astype(jnp.bfloat16)
    key_rows = projected[:, :, 1].astype(jnp.bfloat16)
    value_rows = (projected[:, :, 2] + qv_bias[1].reshape(local_heads, HEAD_DIM)).astype(
        jnp.bfloat16
    )
    scores = (
        jnp.einsum("nqhd,nkhd->nhqk", queries, key_rows, preferred_element_type=jnp.float32)
        * score_scale
    )
    log_total = jax.nn.logsumexp(scores, axis=-1, keepdims=True)
    weights = jnp.exp(scores - log_total)
    weights_low = weights.astype(jnp.bfloat16)
    attended = (
        jnp.einsum("nhqk,nkhd->nqhd", weights_low, value_rows, preferred_element_type=jnp.float32)
        .astype(jnp.bfloat16)
        .reshape(row_count, local_width)
    )
    attn_part = jnp.dot(attended, out_weight, preferred_element_type=jnp.float32)
    attention = lax.psum(attn_part, "tp") + out_bias
    attention = attention.reshape(images, SEQ, D)
    middle = residual + pieces[:, 2] * attention
    normed_two, norm_two_pull = jax.vjp(layer_norm, middle)
    input_b = (
        (normed_two * (1.0 + pieces[:, 4]) + pieces[:, 3])
        .astype(jnp.bfloat16)
        .reshape(row_count, D)
    )
    hidden, gelu_pull, mlp_part = feed_up(input_b, fc1_weight, fc1_bias, fc2_weight)
    branch = lax.psum(mlp_part.astype(jnp.bfloat16), "tp").astype(jnp.float32) + fc2_bias
    branch = branch.reshape(images, SEQ, D)
    output = (middle + pieces[:, 5] * branch).reshape(row_count, D).astype(jnp.bfloat16)
    grad_out = cotangent.astype(jnp.float32).reshape(images, SEQ, D)
    grad_gate_two = jnp.sum(grad_out * branch, axis=1)
    grad_branch = (grad_out * pieces[:, 5]).astype(jnp.bfloat16).reshape(row_count, D)
    bias_fc2 = jnp.sum(grad_branch.astype(jnp.float32), axis=0)
    weight_fc2 = contract_rows(hidden, grad_branch)
    grad_hidden = contract_cols(grad_branch, fc2_weight)
    grad_pre = gelu_pull(grad_hidden)[0].astype(jnp.bfloat16)
    bias_fc1 = jnp.sum(grad_pre.astype(jnp.float32), axis=0)
    weight_fc1 = contract_rows(input_b, grad_pre)
    grad_input_b = lax.psum(contract_cols(grad_pre, fc1_weight), "tp").reshape(images, SEQ, D)
    grad_shift_two = jnp.sum(grad_input_b, axis=1)
    grad_scale_two = jnp.sum(grad_input_b * normed_two, axis=1)
    grad_middle = grad_out + norm_two_pull(grad_input_b * (1.0 + pieces[:, 4]))[0]
    grad_gate_one = jnp.sum(grad_middle * attention, axis=1)
    grad_attention = (grad_middle * pieces[:, 2]).astype(jnp.bfloat16).reshape(row_count, D)
    bias_out = jnp.sum(grad_attention.astype(jnp.float32), axis=0)
    weight_out = contract_rows(attended, grad_attention)
    grad_attended = (
        contract_cols(grad_attention, out_weight)
        .astype(jnp.bfloat16)
        .reshape(images, SEQ, local_heads, HEAD_DIM)
    )
    scores_again = (
        jnp.einsum("nqhd,nkhd->nhqk", queries, key_rows, preferred_element_type=jnp.float32)
        * score_scale
    )
    soft_rows = jnp.exp(scores_again - log_total)
    soft_low = soft_rows.astype(jnp.bfloat16)
    grad_values = jnp.einsum(
        "nhqk,nqhd->nkhd", soft_low, grad_attended, preferred_element_type=jnp.float32
    ).astype(jnp.bfloat16)
    grad_soft = jnp.einsum(
        "nqhd,nkhd->nhqk", grad_attended, value_rows, preferred_element_type=jnp.float32
    )
    row_dot = jnp.sum(soft_rows * grad_soft, axis=-1, keepdims=True)
    grad_scores = (soft_rows * (grad_soft - row_dot)).astype(jnp.bfloat16)
    grad_queries = (
        jnp.einsum("nhqk,nkhd->nqhd", grad_scores, key_rows, preferred_element_type=jnp.float32)
        * score_scale
    ).astype(jnp.bfloat16)
    grad_keys = (
        jnp.einsum("nhqk,nqhd->nkhd", grad_scores, queries, preferred_element_type=jnp.float32)
        * score_scale
    ).astype(jnp.bfloat16)
    grad_projected = jnp.stack([grad_queries, grad_keys, grad_values], axis=2).reshape(
        row_count, 3 * local_width
    )
    bias_qv = jnp.stack(
        [
            jnp.sum(grad_queries.astype(jnp.float32), axis=(0, 1)).reshape(local_width),
            jnp.sum(grad_values.astype(jnp.float32), axis=(0, 1)).reshape(local_width),
        ]
    )
    weight_qkv = contract_rows(input_a, grad_projected).reshape(D, 3, local_width)
    grad_input_a = lax.psum(contract_cols(grad_projected, qkv_flat), "tp").reshape(images, SEQ, D)
    grad_shift_one = jnp.sum(grad_input_a, axis=1)
    grad_scale_one = jnp.sum(grad_input_a * normed_one, axis=1)
    grad_tokens = (
        (grad_middle + norm_one_pull(grad_input_a * (1.0 + pieces[:, 1]))[0])
        .reshape(row_count, D)
        .astype(jnp.bfloat16)
    )
    grad_mod = jnp.stack(
        [
            grad_shift_one,
            grad_scale_one,
            grad_gate_one,
            grad_shift_two,
            grad_scale_two,
            grad_gate_two,
        ],
        axis=1,
    ).reshape(images, 6 * D)
    grad_mod_mine = lax.dynamic_slice_in_dim(grad_mod, lax.axis_index("tp") * ada_cols, ada_cols, 1)
    bias_ada = jnp.sum(grad_mod_mine, axis=0)
    weight_ada = lax.dot_general(
        silu_low.astype(jnp.float32),
        grad_mod_mine,
        (((0,), (0,)), ((), ())),
        precision=lax.Precision.HIGHEST,
        preferred_element_type=jnp.float32,
    )
    silu_part = lax.dot_general(
        grad_mod_mine,
        ada_weight.astype(jnp.float32),
        (((1,), (1,)), ((), ())),
        precision=lax.Precision.HIGHEST,
        preferred_element_type=jnp.float32,
    )
    grad_silu = lax.psum(silu_part, "tp")
    grad_condition = silu_pull(grad_silu)[0]
    factor = 1.0 / math.sqrt(row_count * lax.axis_size("dp"))
    sum_ada, sum_qkv, sum_out, sum_fc1, sum_fc2 = (
        lax.psum_scatter(
            weight_ada.astype(jnp.bfloat16), "dp", scatter_dimension=0, tiled=True
        ).astype(jnp.float32),
        lax.psum_scatter(
            weight_qkv.astype(jnp.bfloat16), "dp", scatter_dimension=0, tiled=True
        ).astype(jnp.float32),
        lax.psum_scatter(
            weight_out.astype(jnp.bfloat16), "dp", scatter_dimension=1, tiled=True
        ).astype(jnp.float32),
        lax.psum_scatter(
            weight_fc1.astype(jnp.bfloat16), "dp", scatter_dimension=0, tiled=True
        ).astype(jnp.float32),
        lax.psum_scatter(
            weight_fc2.astype(jnp.bfloat16), "dp", scatter_dimension=1, tiled=True
        ).astype(jnp.float32),
    )
    total_ada, total_qv, total_out, total_fc1, total_fc2 = lax.psum(
        (bias_ada, bias_qv, bias_out, bias_fc1, bias_fc2), "dp"
    )
    return (
        output,
        grad_tokens,
        grad_condition,
        sum_ada * factor,
        total_ada * factor,
        sum_qkv * factor,
        total_qv * factor,
        sum_out * factor,
        total_out * factor,
        sum_fc1 * factor,
        total_fc1 * factor,
        sum_fc2 * factor,
        total_fc2 * factor,
    )

GELU_CUBE = 0.044715
MESH = pl.DeviceIdType.MESH
F32 = jnp.float32
BF16 = jnp.bfloat16


def dot_nn(a, b):
    return lax.dot_general(a, b, (((1,), (0,)), ((), ())), preferred_element_type=F32)


def dot_nt(a, b):
    return lax.dot_general(a, b, (((1,), (1,)), ((), ())), preferred_element_type=F32)


def dot_tn(a, b):
    return lax.dot_general(a, b, (((0,), (0,)), ((), ())), preferred_element_type=F32)


def norm_parts(values):
    center = values - jnp.mean(values, axis=-1, keepdims=True)
    scale = lax.rsqrt(jnp.mean(center * center, axis=-1, keepdims=True) + norm_eps)
    return center * scale, scale


def fold_rows(values):
    rows, cols = values.shape
    return jnp.sum(values.reshape(rows // 8, 8, cols), axis=0)


def total(part):
    return jnp.sum(part, axis=0, keepdims=True)


def al(index, unit):
    return pl.multiple_of(index, unit)


RC = 128
PW = 384
NP = 3
MR = 384
MODES = ("xzw", "zxw", "xzw", "xzw", "zxw", "xzw", "zxw", "xzw")
GROUPS = {0: 2, 2: 1, 3: 2, 5: 1, 6: 1, 7: 1}
SCHEDULE = (
    "T0", "back1", "T2", "M0", "T3", "M2", "nb0", "ab0", "A0", "M3",
    "nb1", "ab1", "A2", "branch", "T6", "A3", "na0", "B2", "A4", "A1",
    "T5", "M6", "B3", "gmod", "silu", "W2", "sp1", "M5", "T7", "sp2",
    "B4", "na1", "B1", "B0", "M7", "A5", "A6", "W3", "sp3", "fin",
    "W4", "gc", "W1", "W0", "A7", "B5", "B6", "ada", "B7", "W5",
    "W6", "W7",
)


def block_kernel(
    factor,
    tok_h, cot_h, ada_h, w3_h, wo_h, w1_h, w2_h,
    cond_r, adab_r, qvb_r, ob_r, b1_r, b2_r,
    out_h, gt_h, g2_h, g1_h, gq_h, go_h, gada_h,
    gcond_o, gadab_o, gqvb_o, gob_o, gb1_o, gb2_o,
    big, w3, wo, w1, w2, tok, cot, act, ib, qkv, prob, att, attn, mid, hid, gpre,
    gibs, gibr, g4, rx, rz, ry, ry3, fin, fin3, modb, gmod, dysum, part_s, part_r,
    silu_all, silu_2d, mod_all, mod_2d, bias, bias_r, cpart,
    ld_sem, out_sem, ss, rs, cred,
):
    dp, tp = lax.axis_index("dp"), lax.axis_index("tp")
    z, x, c = dp // 4, (dp // 2) % 2, dp % 2
    zp, zh = z % 2, z // 2
    dev_y = (dp, 1 - tp)
    dev_c = (z * 4 + x * 2 + 1 - c, tp)
    dev_x = (z * 4 + (1 - x) * 2 + c, tp)
    dev_z = ((z + 1 - 2 * zp) * 4 + x * 2 + c, tp)
    dev_w = ((3 - z) * 4 + x * 2 + c, tp)
    dp_devs = (dev_c, dev_x, dev_z, dev_w)

    ia, gb = act.at[0], act.at[1]
    T, D = tok.shape
    SEQ = T // 2
    L = wo_h.shape[0]
    LP = qkv.shape[2]
    F = w1.shape[1]
    FH = F // 2
    A = modb.shape[2]
    score_scale = 1.0 / math.sqrt(HEAD_DIM)
    blk = D // 8

    barrier = pltpu.get_barrier_semaphore()
    for dev in (dev_y,) + dp_devs:
        pl.semaphore_signal(barrier, inc=1, device_id=dev, device_id_type=MESH)

    counter = [0]

    def remote(src, dst, dev):
        k = counter[0]
        counter[0] += 1
        return pltpu.make_async_remote_copy(
            src_ref=src, dst_ref=dst, send_sem=ss.at[k], recv_sem=rs.at[k],
            device_id=dev, device_id_type=MESH,
        )

    def credit(k, dev):
        pl.semaphore_signal(cred.at[k], inc=1, device_id=dev, device_id_type=MESH)

    def await_credit(k):
        pl.semaphore_wait(cred.at[k], 1)

    lcount = [0]

    def load(src, dst):
        k = lcount[0]
        lcount[0] += 1
        cp = pltpu.make_async_copy(src, dst, ld_sem.at[k])
        cp.start()
        return cp

    ocount = [0]

    def store(src, dst):
        k = ocount[0]
        ocount[0] += 1
        cp = pltpu.make_async_copy(src, dst, out_sem.at[k])
        cp.start()
        return cp

    NA = A // PW
    ld_ada = [load(ada_h.at[:, PW * k : PW * (k + 1)], big.at[k]) for k in range(NA)]
    ld_tok = load(tok_h, tok)
    ld_w3 = [load(w3_h.at[j], w3.at[j, 0:L]) for j in range(3)]
    for j in range(3):
        w3[j, L:LP, :] = jnp.zeros((LP - L, D), BF16)
    for j in range(2):
        wo[j, L:LP, :] = jnp.zeros((LP - L, D), BF16)

    quart = L // 4
    cut = (quart // 2 + 15) // 16 * 16

    def wo_part(xx, first, count):
        return pl.ds(al((xx * 2 + c) * quart + first, 16), count)

    wo_cuts = ((0, cut), (cut, quart - cut))
    pl.semaphore_wait(barrier, 5)
    cp_wo, cp_wx = [], []

    def send_wo(n):
        rows = wo_part(x, *wo_cuts[n])
        cp_wo.append(remote(wo_h.at[rows], wo.at[tp, rows], dev_y))
        cp_wo[n].start()

    def pass_wo(n):
        cp_wo[n].wait()
        ref = wo.at[1 - tp, wo_part(x, *wo_cuts[n])]
        cp_wx.append(remote(ref, ref, dev_x))
        cp_wx[n].start()

    send_wo(0)

    cond = cond_r[...]
    gate = 1.0 / (1.0 + jnp.exp(-cond))
    silu = cond * gate
    silu_all[dp] = silu.astype(BF16).astype(F32)
    silu_low = jnp.concatenate([silu, jnp.zeros((6, D), F32)], axis=0).astype(BF16)
    for k in range(NA):
        ld_ada[k].wait()
        part = dot_nn(silu_low, big[k])[0:2] + adab_r[pl.ds(PW * k, PW)].reshape(1, PW)
        modb[tp, :, PW * k : PW * (k + 1)] = part
    cp_mod = remote(modb.at[tp], modb.at[tp], dev_y)
    cp_mod.start()
    send_wo(1)
    credit(0, dev_c)

    def spread(ref, k):
        width = 1 << k
        span = pl.ds((dp // width) * width, width)
        cp = remote(ref.at[span], ref.at[span], dp_devs[k])
        cp.start()
        return cp

    cp_silu = spread(silu_all, 0)
    ld_cot = load(cot_h, cot)
    ld_wo = load(wo_h, wo.at[tp, 0:L])
    ld_w1 = load(w1_h, w1)
    ld_w2 = load(w2_h, w2)
    ld_tok.wait()
    cp_mod.wait()

    def mvec(which, img):
        return modb[which // 3, img : img + 1, (which % 3) * D : (which % 3 + 1) * D]

    def rows_loop(img, body, init=None, step=RC):
        base = img * SEQ

        def one(r, carry):
            return body(pl.ds(al(base + r * step, step), step), carry)

        return lax.fori_loop(0, SEQ // step, one, init)

    def zeros8(n):
        return tuple(jnp.zeros((8, D), F32) for _ in range(n))

    def image(img):
        return slice(img * SEQ, (img + 1) * SEQ)

    for img in range(2):
        shift, sc = mvec(0, img), 1.0 + mvec(1, img)

        def body(rows, carry):
            normed, _ = norm_parts(tok[rows, :].astype(F32))
            ia[rows, :] = (normed * sc + shift).astype(BF16)
            return carry

        rows_loop(img, body, 0, 16)
    cp_silu.wait()
    cp_silu = spread(silu_all, 1)

    for j in range(3):
        ld_w3[j].wait()

    def project_in(img):
        rows = image(img)
        for j in range(3):
            out = dot_nt(ia[rows, :], w3[j])
            if j != 1:
                bias_j = qvb_r[j // 2 : j // 2 + 1, :]
                qkv[j, rows, 0:L] = (out[:, 0:L] + bias_j).astype(BF16)
                qkv[j, rows, L:LP] = jnp.zeros((SEQ, LP - L), BF16)
            else:
                qkv[j, rows, :] = out.astype(BF16)

    lane = lax.broadcasted_iota(jnp.int32, (1, 256), 1)

    def head_mask(j, e):
        lo = 16 * j + HEAD_DIM * e
        return jnp.where((lane >= lo) & (lane < lo + HEAD_DIM), 1.0, 0.0).astype(BF16)

    def keep_low(j, old, new):
        full = lax.broadcasted_iota(jnp.int32, new.shape, 1)
        return jnp.where(full < 16 * j, old.astype(F32), new).astype(BF16)

    def attend(img):
        rows = image(img)
        for j in range(4):
            win = slice(128 * j, 128 * j + 256)
            q, k, v = qkv[0, rows, win], qkv[1, rows, win], qkv[2, rows, win]
            mixed = None
            for e in range(2):
                mask = head_mask(j, e)
                s = dot_nt(q * mask, k) * score_scale
                p = jnp.exp(s - jnp.max(s, axis=-1, keepdims=True))
                p = p * (1.0 / jnp.sum(p, axis=-1, keepdims=True))
                low = p.astype(BF16)
                prob[img * 8 + 2 * j + e] = low
                part = dot_nn(low, v * mask)
                mixed = part if mixed is None else mixed + part
            if j:
                mixed = keep_low(j, g4[3, rows, win], mixed)
            g4[3, rows, win] = mixed.astype(BF16)
        att[tp, rows, :] = g4[3, rows, :]
        cp = remote(att.at[tp, rows], att.at[tp, rows], dev_y)
        cp.start()
        return cp

    project_in(0)
    pass_wo(0)
    cp_silu.wait()
    cp_silu = spread(silu_all, 2)
    cp_att = [attend(0)]
    pass_wo(1)
    own_rows = wo.at[1 - tp, wo_part(x, 0, quart)]
    cp_wc = [remote(own_rows, own_rows, dev_c)]
    cp_wc[0].start()
    project_in(1)
    cp_silu.wait()
    cp_silu = spread(silu_all, 3)
    cp_att.append(attend(1))

    ld_cot.wait()
    acc = zeros8(1)[0]
    for img in range(2):
        gate_b = mvec(5, img)

        def body(rows, carry):
            dy = cot[rows, :].astype(F32)
            low = (dy * gate_b).astype(BF16)
            gb[rows, :] = low
            return (carry[0] + fold_rows(low.astype(F32)), carry[1] + fold_rows(dy))

        acc, dy_sum = rows_loop(img, body, (acc, zeros8(1)[0]), 16)
        dysum[img : img + 1, :] = total(dy_sum)

    O1, OO, O2, OQ = 0, F, F + D, F + 2 * D
    bias[0, :, O2 : O2 + D] = total(acc)

    cp_silu.wait()
    for i in range(16):
        silu_2d[2 * i : 2 * i + 2, :] = silu_all[i]
    ld_wo.wait()
    for cp in cp_wx:
        cp.wait()
    far_rows = wo.at[1 - tp, wo_part(1 - x, 0, quart)]
    cp_wc.append(remote(far_rows, far_rows, dev_c))
    cp_wc[1].start()
    ld_w1.wait()
    ld_w2.wait()

    def project(img):
        rows = image(img)
        cp_att[img].wait()
        attn[rows, :] = (
            dot_nn(att[0, rows, :], wo[0]) + dot_nn(att[1, rows, :], wo[1])
        ) + ob_r[...].reshape(1, D)
        gate_a, shift_b, sc_b = mvec(2, img), mvec(3, img), 1.0 + mvec(4, img)

        def body(r, carry):
            m = tok[r, :].astype(F32) + gate_a * attn[r, :]
            mid[r, :] = m
            normed, _ = norm_parts(m)
            ib[r, :] = (normed * sc_b + shift_b).astype(BF16)
            return carry

        rows_loop(img, body, 0)

    def hidden(img):
        rows = image(img)
        width = F // 3
        for n in range(3):
            cols = slice(n * width, (n + 1) * width)
            pre = dot_nn(ib[rows, :], w1[:, cols]) + b1_r[pl.ds(n * width, width)].reshape(1, width)
            gh = dot_nt(gb[rows, :], w2[cols, :])
            sq = pre * pre
            th = jnp.tanh(gelu_coef * pre * (1.0 + GELU_CUBE * sq))
            hp = 0.5 + 0.5 * th
            hid[rows, cols] = (pre * hp).astype(BF16)
            slope = hp + (0.5 * gelu_coef) * pre * (1.0 - th * th) * (1.0 + (3.0 * GELU_CUBE) * sq)
            low = (gh * slope).astype(BF16)
            gpre[rows, cols] = low
            cur = jnp.sum(low.astype(F32), axis=0, keepdims=True)
            bias[0, :, cols] = cur if img == 0 else bias[0, :, cols] + cur

    def back(img):
        rows = image(img)
        gibs[rows, :] = dot_nt(gpre[rows, :], w1[...]).astype(BF16)
        cp = remote(gibs.at[rows], gibr.at[rows], dev_y)
        cp.start()
        return cp

    cp_c, cp_a, cp_b, cp_w, cp_f, cp_o = {}, {}, {}, {}, {}, {}
    sent, staged = set(), []

    devs = {"x": dev_x, "z": dev_z, "w": dev_w}

    def bits(mode, zz, xx):
        def one(axis):
            if axis == "x":
                return xx
            if axis == "w":
                return zz // 2
            return ((zz + 1) // 2) % 2 if mode.index("z") < mode.index("w") else zz % 2

        return [one(axis) for axis in mode]

    def place(p, s):
        b = bits(MODES[p], s // 2, s % 2)
        return (b[0] * 4 + b[1] * 2 + b[2]) * blk

    def product(p, count, h, m):
        feats = slice(m * MR, (m + 1) * MR)
        if p < 2 * NP:
            cols = pl.ds(al(h * FH + PW * (p % NP), 128), PW * count)
            return dot_tn((gb if p < NP else ib)[:, feats], (hid if p < NP else gpre)[:, cols])
        if p == 2 * NP:
            return dot_tn(ia[:, feats], g4[2 * h])
        return dot_tn(act[h, :, feats], g4[2 * h + 1])

    def product_blocks(p, count, h, put):
        for m in range(D // MR):
            res = product(p, count, h, m)
            for s in range(8):
                lo, hi = max(m * MR, s * blk), min((m + 1) * MR, (s + 1) * blk)
                if lo < hi:
                    for i in range(count):
                        width = res.shape[1] // count
                        base = place(p + i, s) + lo - s * blk
                        put(
                            p + i, slice(base, base + hi - lo),
                            res[lo - m * MR : hi - m * MR, i * width : (i + 1) * width],
                        )

    def land_c(p):
        if p < 2 * NP:
            return big.at[p]
        return w1.at[:, (p - 2 * NP) * LP : (p - 2 * NP + 1) * LP]

    def land_a(p):
        if p < 2 * NP:
            return rx.at[p]
        q = p - 2 * NP
        return w1.at[q * 4 * blk : (q + 1) * 4 * blk, 2 * LP : 3 * LP]

    def land_b(p):
        if p < 2 * NP:
            return rz.at[p]
        q = D + T + (p - 2 * NP) * 2 * blk
        return w2.at[q : q + 2 * blk, 0:LP]

    def land_w(p):
        return ry.at[p] if p < 2 * NP else ry3.at[p - 2 * NP]

    def slot_c(p):
        return big.at[6 + p % NP] if p < 2 * NP else w2.at[0:D, 0:LP]

    def theirs(p, count=1):
        for cur in range(p, p + count):
            old = cur - NP if NP <= cur < 2 * NP else cur - 1 if cur > 2 * NP else None
            if old is not None:
                cp_c[old].wait_send()
                sent.add(old)

        def put(cur, rows, values):
            slot_c(cur)[rows, :] = values.astype(BF16)

        product_blocks(p, count, 1 - c, put)
        for cur in range(p, p + count):
            if len(cp_c) == 0:
                await_credit(0)
            if cur == 2 * NP:
                await_credit(1)
            cp_c[cur] = remote(slot_c(cur), land_c(cur), dev_c)
            cp_c[cur].start()

    def mine(p, count=1):
        for cur in range(p, p + count):
            cp_c[cur].wait_recv()

        def put(cur, rows, values):
            ref = land_c(cur)
            ref[rows, :] = (values + ref[rows, :].astype(F32)).astype(BF16)

        product_blocks(p, count, c, put)
        for cur in range(p, p + count):
            mode = MODES[cur]
            b = bits(mode, z, x)
            rows = pl.ds(al((1 - b[0]) * 4 * blk, 16), 4 * blk)
            cp_a[cur] = remote(land_c(cur).at[rows], land_a(cur), devs[mode[0]])
            if cur >= 2 * NP:
                await_credit(cur - 2 * NP + 2)
            cp_a[cur].start()

    def merge(p, base, arrived, count):
        ref = land_c(p)

        def body(i, carry):
            rows = pl.ds(al(base + i * blk, 16), blk)
            got = arrived[pl.ds(al(i * blk, 16), blk), :].astype(F32)
            ref[rows, :] = (ref[rows, :].astype(F32) + got).astype(BF16)
            return carry

        lax.fori_loop(0, count, body, 0)

    def step_a(p):
        cp_a[p].wait_recv()
        b = bits(MODES[p], z, x)
        base = b[0] * 4 * blk
        merge(p, base, land_a(p), 4)
        rows = pl.ds(al(base + (1 - b[1]) * 2 * blk, 16), 2 * blk)
        cp_b[p] = remote(land_c(p).at[rows], land_b(p), devs[MODES[p][1]])
        if p >= 2 * NP:
            await_credit(p - 2 * NP + 4)
        cp_b[p].start()

    def step_b(p):
        cp_b[p].wait_recv()
        b = bits(MODES[p], z, x)
        base = (b[0] * 4 + b[1] * 2) * blk
        merge(p, base, land_b(p), 2)
        rows = pl.ds(al(base + (1 - b[2]) * blk, 16), blk)
        cp_w[p] = remote(land_c(p).at[rows], land_w(p), devs[MODES[p][2]])
        cp_w[p].start()

    def drain(p):
        cp_o[p].wait()
        cp_f[p].wait_send()

    hb = blk // 2
    keep, give = pl.ds(al(c * hb, 8), hb), pl.ds(al((1 - c) * hb, 8), hb)

    def step_w(p):
        cp_w[p].wait_recv()
        b = bits(MODES[p], z, x)
        base = (b[0] * 4 + b[1] * 2 + b[2]) * blk
        both = land_c(p)[pl.ds(al(base, 16), blk), :].astype(F32)
        both = (both + land_w(p)[...].astype(F32)) * factor
        if p < 2 * NP:
            n = len(staged)
            if n >= 2:
                drain(staged[n - 2])
            staged.append(p)
            stage = fin.at[n % 2]
            stage[...] = both
            cols = pl.ds(al(c * FH + PW * (p % NP), 128), PW)
            targets = [(g2_h if p < NP else g1_h).at[:, cols]]
        else:
            stage = fin3.at[p - 2 * NP]
            stage[...] = both[:, 0:L]
            targets = [gq_h.at[2 * c]] if p == 2 * NP else [gq_h.at[1], go_h]
        k = counter[0]
        for n, dst in enumerate(targets):
            counter[0] = k
            cp_o[p] = pltpu.make_async_copy(stage.at[keep], dst, out_sem.at[8 + p])
            cp_f[p] = remote(stage.at[give], dst, dev_c)

            def go(local=cp_o[p], far=cp_f[p]):
                local.start()
                far.start()

            if len(targets) == 1:
                go()
            else:
                pl.when(c == n)(go)

    def branch():
        out = dot_nn(hid[...], w2[...])
        for img in range(2):
            rows = image(img)
            dy = cot[rows, :].astype(F32)
            part_s[img, 2:3, :] = jnp.sum(dy * out[rows], axis=0, keepdims=True)
        hid[:, 0:D] = out.astype(BF16)

    def norm_b_back(img):
        cp_gib[img].wait()
        gate_a, sc_b = mvec(2, img), 1.0 + mvec(4, img)

        def body(r, carry):
            s_shift, s_scale, s_gate, s_bias = carry
            g = gibs[r, :].astype(F32) + gibr[r, :].astype(F32)
            normed, inv = norm_parts(mid[r, :])
            s_shift += fold_rows(g)
            s_scale += fold_rows(g * normed)
            u = g * sc_b
            m1 = jnp.mean(u, axis=-1, keepdims=True)
            m2 = jnp.mean(u * normed, axis=-1, keepdims=True)
            gm = cot[r, :].astype(F32) + inv * (u - m1 - normed * m2)
            s_gate += fold_rows(gm * attn[r, :])
            low = (gm * gate_a).astype(BF16)
            gb[r, :] = low
            s_bias += fold_rows(low.astype(F32))
            attn[r, :] = gm
            return (s_shift, s_scale, s_gate, s_bias)

        sums = rows_loop(img, body, zeros8(4))
        credit(6 + img, dev_y)
        gmod[1, img : img + 1, 0:D] = total(sums[0])
        gmod[1, img : img + 1, D : 2 * D] = total(sums[1])
        gmod[0, img : img + 1, 2 * D : 3 * D] = total(sums[2])
        cur = total(sums[3])
        bias[0, :, OO : OO + D] = cur if img == 0 else bias[0, :, OO : OO + D] + cur

    def attend_back(img):
        rows = image(img)
        g_all = dot_nt(gb[rows, :], wo[tp]).astype(BF16)
        for j in range(4):
            win = slice(128 * j, 128 * j + 256)
            q, k, v = qkv[0, rows, win], qkv[1, rows, win], qkv[2, rows, win]
            g = g_all[:, win]
            gq = gk = gv = None
            for e in range(2):
                mask = head_mask(j, e)
                gm = g * mask
                low = prob[img * 8 + 2 * j + e]
                p = low.astype(F32)
                gp = dot_nt(gm, v)
                ds = (p * (gp - jnp.sum(p * gp, axis=-1, keepdims=True))).astype(BF16)
                parts = dot_nn(ds, k * mask), dot_tn(ds, q * mask), dot_tn(low, gm)
                if gq is None:
                    gq, gk, gv = parts
                else:
                    gq, gk, gv = gq + parts[0], gk + parts[1], gv + parts[2]
            for i, got in enumerate((gq * score_scale, gk * score_scale, gv)):
                if j:
                    got = keep_low(j, g4[i, rows, win], got)
                g4[i, rows, win] = got.astype(BF16)
        for n, which in enumerate((0, 2)):
            cur = jnp.sum(g4[which, rows, :].astype(F32), axis=0, keepdims=True)
            at = slice(OQ + n * LP, OQ + (n + 1) * LP)
            bias[0, :, at] = cur if img == 0 else bias[0, :, at] + cur
        part = dot_nn(g4[0, rows, :], w3[0])
        part += dot_nn(g4[1, rows, :], w3[1])
        part += dot_nn(g4[2, rows, :], w3[2])
        gibs[rows, :] = part.astype(BF16)
        await_credit(6 + img)
        cp = remote(gibs.at[rows], gibr.at[rows], dev_y)
        cp.start()

        def body(r, carry):
            g = gibs[r, :].astype(F32)
            normed, _ = norm_parts(tok[r, :].astype(F32))
            return (carry[0] + fold_rows(g), carry[1] + fold_rows(g * normed))

        sums = rows_loop(img, body, zeros8(2), 32)
        part_s[img, 0:1, :] = total(sums[0])
        part_s[img, 1:2, :] = total(sums[1])
        return cp

    tails = []

    def norm_a_back(img, cp):
        cp.wait()
        sc_a = 1.0 + mvec(1, img)

        def body(r, carry):
            u = (gibs[r, :].astype(F32) + gibr[r, :].astype(F32)) * sc_a
            normed, inv = norm_parts(tok[r, :].astype(F32))
            m1 = jnp.mean(u, axis=-1, keepdims=True)
            m2 = jnp.mean(u * normed, axis=-1, keepdims=True)
            gibr[r, :] = (attn[r, :] + inv * (u - m1 - normed * m2)).astype(BF16)
            return carry

        rows_loop(img, body, 0)
        rows = image(img)
        tails.append(store(gibr.at[rows], gt_h.at[rows]))

    def finish(img):
        gate_b = mvec(5, img)
        base2 = b2_r[...].reshape(1, D)

        def body(r, carry):
            br = hid[r, 0:D].astype(F32) + w2[pl.ds(al(D + r.start, 16), RC), :].astype(F32)
            ia[r, :] = (mid[r, :] + gate_b * (br + base2)).astype(BF16)
            return carry

        rows_loop(img, body, 0)
        rows = image(img)
        tails.append(store(ia.at[rows], out_h.at[rows]))

    mod_cp = []

    def spread_mod(k):
        if k:
            for cp in mod_cp[-1]:
                cp.wait()
            bias[k] = bias[k - 1] + bias_r[k - 1]
        if k < 4:
            cp = remote(bias.at[k], bias_r.at[k], dp_devs[k])
            cp.start()
            mod_cp.append((spread(mod_all, k), cp))

    def ada_out():
        for i in range(16):
            mod_2d[2 * i : 2 * i + 2, :] = mod_all[i]
        row = lax.broadcasted_iota(jnp.int32, (hb, D), 0)
        col = lax.broadcasted_iota(jnp.int32, (hb, D), 1)
        chosen = jnp.where(col == dp * hb + row, 1.0, 0.0).astype(BF16)
        picked = dot_nt(chosen, silu_2d[...].astype(BF16)).astype(BF16)
        for t in range(3):
            cols = slice(D * t, D * (t + 1))
            whole = mod_2d[:, cols]
            coarse = whole.astype(BF16)
            fine = (whole - coarse.astype(F32)).astype(BF16)
            rows = slice(hb * t, hb * (t + 1))
            mid[rows, :] = (dot_nn(picked, coarse) + dot_nn(picked, fine)) * factor
            tails.append(store(mid.at[rows], gada_h.at[:, cols]))
        gadab_o[...] = (total(mod_2d[...]) * factor).reshape(A)
        sums = bias[4] * factor
        gb1_o[...] = sums[:, O1 : O1 + F].reshape(F)
        gob_o[...] = sums[:, OO : OO + D].reshape(D)
        gb2_o[...] = sums[:, O2 : O2 + D].reshape(D)
        gqvb_o[0:1, :] = sums[:, OQ : OQ + L]
        gqvb_o[1:2, :] = sums[:, OQ + LP : OQ + LP + L]

    for cp in cp_wc:
        cp.wait()
    project(0)
    hidden(0)
    cp_gib = [back(0)]
    project(1)
    hidden(1)
    cp_gia, cp_later, done = {}, {}, set()
    back_refs = [wo.at[0, 0:T], wo.at[1, 0:T], hid.at[:, D : 2 * D]]

    def do_back():
        cp_gib.append(back(1))
        credit(1, dev_c)
        credit(2, devs[MODES[6][0]])
        credit(3, devs[MODES[7][0]])

    def do_branch():
        branch()
        credit(4, devs[MODES[6][1]])
        credit(5, devs[MODES[7][1]])
        credit(8, dev_y)
        await_credit(8)
        cp_later["br"] = remote(hid.at[:, 0:D], w2.at[D : D + T], dev_y)
        cp_later["br"].start()

    def do_gmod():
        cp_later["part"].wait()
        for img in range(2):
            both = part_s[img] + part_r[img]
            gmod[0, img : img + 1, 0:D] = both[0:1]
            gmod[0, img : img + 1, D : 2 * D] = both[1:2]
            gmod[1, img : img + 1, 2 * D : 3 * D] = (
                both[2:3] + dysum[img : img + 1, :] * b2_r[...].reshape(1, D)
            )
        mod_all[dp] = gmod[tp]
        spread_mod(0)

    def do_silu():
        for cp in cp_later["ada"]:
            cp.wait()
        gm = gmod[tp]
        gm_hi = gm.astype(BF16).astype(F32)
        gm_two = jnp.concatenate([gm_hi, gm - gm_hi, jnp.zeros((4, A), F32)], axis=0)
        gm_two = gm_two.astype(BF16)
        top = sum(dot_nt(gm_two[:, D * t : D * (t + 1)], w3[t]) for t in range(3))
        rest = sum(dot_nt(gm_two[:, D * t : D * (t + 1)], back_refs[t][...]) for t in range(3))
        cpart[tp, :, 0:LP] = top[0:2] + top[2:4]
        cpart[tp, :, LP:D] = rest[0:2] + rest[2:4]
        cp_later["cond"] = remote(cpart.at[tp], cpart.at[tp], dev_y)
        cp_later["cond"].start()

    def do_cond():
        cp_later["cond"].wait()
        gcond_o[...] = (cpart[0] + cpart[1]) * (gate * (1.0 + cond * (1.0 - gate)))

    def do_finish():
        cp_later["br"].wait()
        finish(0)
        finish(1)

    def do_ada():
        spread_mod(4)
        ada_out()

    def attend_back_of(img):
        cp_gia[img] = attend_back(img)

    steps = {
        "back1": do_back, "branch": do_branch, "gmod": do_gmod, "silu": do_silu,
        "gc": do_cond, "fin": do_finish, "ada": do_ada,
    }
    for n in range(2):
        steps[f"nb{n}"] = functools.partial(norm_b_back, n)
        steps[f"ab{n}"] = functools.partial(attend_back_of, n)
        steps[f"na{n}"] = lambda n=n: norm_a_back(n, cp_gia[n])
    for n in range(1, 4):
        steps[f"sp{n}"] = functools.partial(spread_mod, n)
    for p in range(2 * NP + 2):
        steps[f"T{p}"] = functools.partial(theirs, p, GROUPS.get(p))
        steps[f"M{p}"] = functools.partial(mine, p, GROUPS.get(p))
        steps[f"A{p}"] = functools.partial(step_a, p)
        steps[f"B{p}"] = functools.partial(step_b, p)
        steps[f"W{p}"] = functools.partial(step_w, p)
    for name in SCHEDULE:
        steps[name]()
        done.add(name)
        if {"ab1", "branch"} <= done and "part" not in cp_later:
            cp_later["ada"] = [
                load(ada_h.at[0:LP, D * t : D * (t + 1)], w3.at[t]) for t in range(3)
            ] + [load(ada_h.at[LP:D, D * t : D * (t + 1)], back_refs[t]) for t in range(3)]
            cp_later["part"] = remote(part_s, part_r, dev_y)
            cp_later["part"].start()
    for p in range(2 * NP + 2):
        if p not in sent:
            cp_c[p].wait_send()
        cp_a[p].wait_send()
        cp_b[p].wait_send()
        cp_w[p].wait_send()
        if p >= 2 * NP or p in staged[-2:]:
            drain(p)
        cp_f[p].wait_recv()
    for cp in tails:
        cp.wait()


VMEM_BYTES = 66977792

def fused(
    tokens, condition, noise_times, cotangent, ada_weight, ada_bias, qkv_weight, qv_bias,
    out_weight, out_bias, fc1_weight, fc1_bias, fc2_weight, fc2_bias,
):
    T, width = tokens.shape
    L, F, A = qkv_weight.shape[2], fc1_weight.shape[1], ada_weight.shape[1]
    LP = -(-L // 128) * 128
    n_dp = lax.axis_size("dp")
    blk = width // 8
    rows = width // n_dp
    sums = F + 2 * width + 2 * LP
    factor = 1.0 / math.sqrt(T * n_dp)
    cond_total = condition + time_features(noise_times)
    w3 = jnp.transpose(qkv_weight, (1, 2, 0))
    hbm, vmem = pl.BlockSpec(memory_space=pl.ANY), pl.BlockSpec(memory_space=pltpu.VMEM)
    sds = jax.ShapeDtypeStruct
    low, full = lambda *shape: pltpu.VMEM(shape, BF16), lambda *shape: pltpu.VMEM(shape, F32)
    results = pl.pallas_call(
        functools.partial(block_kernel, factor),
        out_shape=(
            sds((T, width), BF16), sds((T, width), BF16),
            sds((rows, F), F32), sds((rows, F), F32),
            sds((3, rows, L), F32), sds((rows, L), F32), sds((rows, A), F32),
            sds((2, width), F32), sds((A,), F32), sds((2, L), F32), sds((width,), F32),
            sds((F,), F32), sds((width,), F32),
        ),
        in_specs=[hbm] * 7 + [vmem] * 6,
        out_specs=(hbm,) * 7 + (vmem,) * 6,
        scratch_shapes=[
            low(A // PW, width, PW),
            low(3, LP, width),
            low(2, LP, width),
            low(width, F),
            low(F, width),
            low(T, width),
            low(T, width),
            low(2, T, width),
            low(T, width),
            low(3, T, LP),
            low(16, T // 2, T // 2),
            low(2, T, LP),
            full(T, width),
            full(T, width),
            low(T, F),
            low(T, F),
            low(T, width),
            low(T, width),
            low(4, T, LP),
            low(6, 4 * blk, PW),
            low(6, 2 * blk, PW),
            low(6, blk, PW),
            low(2, blk, LP),
            full(2, blk, PW),
            full(2, blk, L),
            full(2, 2, A),
            full(2, 2, A),
            full(2, width),
            full(2, 3, width),
            full(2, 3, width),
            full(16, 2, width),
            full(32, width),
            full(16, 2, A),
            full(32, A),
            full(5, 1, sums),
            full(4, 1, sums),
            full(2, 2, width),
            pltpu.SemaphoreType.DMA((24,)),
            pltpu.SemaphoreType.DMA((16,)),
            pltpu.SemaphoreType.DMA((72,)),
            pltpu.SemaphoreType.DMA((72,)),
            pltpu.SemaphoreType.REGULAR((9,)),
        ],
        compiler_params=pltpu.CompilerParams(
            collective_id=0, has_side_effects=True, vmem_limit_bytes=VMEM_BYTES
        ),
        name="block",
    )(
        tokens, cotangent, ada_weight, w3, out_weight, fc1_weight, fc2_weight,
        cond_total, ada_bias, qv_bias, out_bias, fc1_bias, fc2_bias,
    )
    (
        output, grad_tokens, g2, g1, gqkv, gout, gada, gcond, gada_b, gqv_b, gout_b, g1_b, g2_b,
    ) = results
    return (
        output, grad_tokens, gcond, gada, gada_b, jnp.transpose(gqkv, (1, 0, 2)), gqv_b,
        gout.T, gout_b, g1, g1_b, g2.T, g2_b,
    )


def local(*args):
    tokens, condition, qkv_weight, fc1_weight = args[0], args[1], args[6], args[10]
    fits = (
        lax.axis_size("tp") == 2 and lax.axis_size("dp") == 16
        and condition.shape[0] == 2 and tokens.shape[0] == 2 * SEQ
        and qkv_weight.shape[2] == D // 2 and fc1_weight.shape[1] == 2 * D
    )
    return fused(*args) if fits else plain(*args)


def solution(mesh):
    return jax.shard_map(
        local,
        mesh=mesh,
        in_specs=(
            P("dp", None),
            P("dp", None),
            P("dp"),
            P("dp", None),
            P(None, "tp"),
            P("tp"),
            P(None, None, "tp"),
            P(None, "tp"),
            P("tp", None),
            P(),
            P(None, "tp"),
            P("tp"),
            P("tp", None),
            P(),
        ),
        out_specs=(
            P("dp", None),
            P("dp", None),
            P("dp", None),
            P("dp", "tp"),
            P("tp"),
            P("dp", None, "tp"),
            P(None, "tp"),
            P("tp", "dp"),
            P(),
            P("dp", "tp"),
            P("tp"),
            P("tp", "dp"),
            P(),
        ),
        check_vma=False,
    )
```

```python
import functools
import math

import jax
import jax.numpy as jnp
from jax import lax
from jax.experimental import pallas as pl
from jax.experimental.pallas import tpu as pltpu
from jax.sharding import PartitionSpec as P

D = 1152
HEAD_DIM = 72
SEQ = 256


norm_eps = 1e-06
gelu_coef = 0.7978845608028654


def layer_norm(values):
    center = values - jnp.mean(values, axis=-1, keepdims=True)
    variance = jnp.mean(center * center, axis=-1, keepdims=True)
    return center * lax.rsqrt(variance + norm_eps)


def gelu_tanh(values):
    return (
        0.5 * values * (1.0 + jnp.tanh(gelu_coef * (values + 0.044715 * values * values * values)))
    )


def time_features(noise_times):
    half_width = D // 2
    ladder = jnp.arange(half_width).astype(jnp.float32)
    frequency = jnp.exp(-math.log(10000.0) * ladder / half_width)
    angles = 1000.0 * noise_times[:, None] * frequency[None, :]
    return jnp.concatenate([jnp.cos(angles), jnp.sin(angles)], axis=1)


def contract_rows(former, latter):
    return lax.dot_general(
        former, latter, (((0,), (0,)), ((), ())), preferred_element_type=jnp.float32
    )


def contract_cols(former, latter):
    return lax.dot_general(
        former, latter, (((1,), (1,)), ((), ())), preferred_element_type=jnp.float32
    )


def feed_up(input_b, fc1_weight, fc1_bias, fc2_weight):
    hidden_pre = jnp.dot(input_b, fc1_weight, preferred_element_type=jnp.float32) + fc1_bias
    hidden_act, gelu_pull = jax.vjp(gelu_tanh, hidden_pre)
    hidden = hidden_act.astype(jnp.bfloat16)
    return (hidden, gelu_pull, jnp.dot(hidden, fc2_weight, preferred_element_type=jnp.float32))


def plain(
    tokens,
    condition,
    noise_times,
    cotangent,
    ada_weight,
    ada_bias,
    qkv_weight,
    qv_bias,
    out_weight,
    out_bias,
    fc1_weight,
    fc1_bias,
    fc2_weight,
    fc2_bias,
):
    images = condition.shape[0]
    row_count = tokens.shape[0]
    local_width = qkv_weight.shape[2]
    local_heads = local_width // HEAD_DIM
    ada_cols = ada_weight.shape[1]
    score_scale = 1.0 / math.sqrt(HEAD_DIM)
    cond_total = condition + time_features(noise_times)
    silu_cond, silu_pull = jax.vjp(jax.nn.silu, cond_total)
    silu_low = silu_cond.astype(jnp.bfloat16)
    mod_part = jnp.dot(silu_low, ada_weight, preferred_element_type=jnp.float32) + ada_bias
    modulation = lax.all_gather(mod_part, "tp", axis=1, tiled=True)
    pieces = modulation.reshape(images, 6, 1, D)
    residual = tokens.astype(jnp.float32).reshape(images, SEQ, D)
    normed_one, norm_one_pull = jax.vjp(layer_norm, residual)
    input_a = (
        (normed_one * (1.0 + pieces[:, 1]) + pieces[:, 0])
        .astype(jnp.bfloat16)
        .reshape(row_count, D)
    )
    qkv_flat = qkv_weight.reshape(D, 3 * local_width)
    projected = jnp.dot(input_a, qkv_flat, preferred_element_type=jnp.float32).reshape(
        images, SEQ, 3, local_heads, HEAD_DIM
    )
    queries = (projected[:, :, 0] + qv_bias[0].reshape(local_heads, HEAD_DIM)).astype(jnp.bfloat16)
    key_rows = projected[:, :, 1].astype(jnp.bfloat16)
    value_rows = (projected[:, :, 2] + qv_bias[1].reshape(local_heads, HEAD_DIM)).astype(
        jnp.bfloat16
    )
    scores = (
        jnp.einsum("nqhd,nkhd->nhqk", queries, key_rows, preferred_element_type=jnp.float32)
        * score_scale
    )
    log_total = jax.nn.logsumexp(scores, axis=-1, keepdims=True)
    weights = jnp.exp(scores - log_total)
    weights_low = weights.astype(jnp.bfloat16)
    attended = (
        jnp.einsum("nhqk,nkhd->nqhd", weights_low, value_rows, preferred_element_type=jnp.float32)
        .astype(jnp.bfloat16)
        .reshape(row_count, local_width)
    )
    attn_part = jnp.dot(attended, out_weight, preferred_element_type=jnp.float32)
    attention = lax.psum(attn_part, "tp") + out_bias
    attention = attention.reshape(images, SEQ, D)
    middle = residual + pieces[:, 2] * attention
    normed_two, norm_two_pull = jax.vjp(layer_norm, middle)
    input_b = (
        (normed_two * (1.0 + pieces[:, 4]) + pieces[:, 3])
        .astype(jnp.bfloat16)
        .reshape(row_count, D)
    )
    hidden, gelu_pull, mlp_part = feed_up(input_b, fc1_weight, fc1_bias, fc2_weight)
    branch = lax.psum(mlp_part.astype(jnp.bfloat16), "tp").astype(jnp.float32) + fc2_bias
    branch = branch.reshape(images, SEQ, D)
    output = (middle + pieces[:, 5] * branch).reshape(row_count, D).astype(jnp.bfloat16)
    grad_out = cotangent.astype(jnp.float32).reshape(images, SEQ, D)
    grad_gate_two = jnp.sum(grad_out * branch, axis=1)
    grad_branch = (grad_out * pieces[:, 5]).astype(jnp.bfloat16).reshape(row_count, D)
    bias_fc2 = jnp.sum(grad_branch.astype(jnp.float32), axis=0)
    weight_fc2 = contract_rows(hidden, grad_branch)
    grad_hidden = contract_cols(grad_branch, fc2_weight)
    grad_pre = gelu_pull(grad_hidden)[0].astype(jnp.bfloat16)
    bias_fc1 = jnp.sum(grad_pre.astype(jnp.float32), axis=0)
    weight_fc1 = contract_rows(input_b, grad_pre)
    grad_input_b = lax.psum(contract_cols(grad_pre, fc1_weight), "tp").reshape(images, SEQ, D)
    grad_shift_two = jnp.sum(grad_input_b, axis=1)
    grad_scale_two = jnp.sum(grad_input_b * normed_two, axis=1)
    grad_middle = grad_out + norm_two_pull(grad_input_b * (1.0 + pieces[:, 4]))[0]
    grad_gate_one = jnp.sum(grad_middle * attention, axis=1)
    grad_attention = (grad_middle * pieces[:, 2]).astype(jnp.bfloat16).reshape(row_count, D)
    bias_out = jnp.sum(grad_attention.astype(jnp.float32), axis=0)
    weight_out = contract_rows(attended, grad_attention)
    grad_attended = (
        contract_cols(grad_attention, out_weight)
        .astype(jnp.bfloat16)
        .reshape(images, SEQ, local_heads, HEAD_DIM)
    )
    scores_again = (
        jnp.einsum("nqhd,nkhd->nhqk", queries, key_rows, preferred_element_type=jnp.float32)
        * score_scale
    )
    soft_rows = jnp.exp(scores_again - log_total)
    soft_low = soft_rows.astype(jnp.bfloat16)
    grad_values = jnp.einsum(
        "nhqk,nqhd->nkhd", soft_low, grad_attended, preferred_element_type=jnp.float32
    ).astype(jnp.bfloat16)
    grad_soft = jnp.einsum(
        "nqhd,nkhd->nhqk", grad_attended, value_rows, preferred_element_type=jnp.float32
    )
    row_dot = jnp.sum(soft_rows * grad_soft, axis=-1, keepdims=True)
    grad_scores = (soft_rows * (grad_soft - row_dot)).astype(jnp.bfloat16)
    grad_queries = (
        jnp.einsum("nhqk,nkhd->nqhd", grad_scores, key_rows, preferred_element_type=jnp.float32)
        * score_scale
    ).astype(jnp.bfloat16)
    grad_keys = (
        jnp.einsum("nhqk,nqhd->nkhd", grad_scores, queries, preferred_element_type=jnp.float32)
        * score_scale
    ).astype(jnp.bfloat16)
    grad_projected = jnp.stack([grad_queries, grad_keys, grad_values], axis=2).reshape(
        row_count, 3 * local_width
    )
    bias_qv = jnp.stack(
        [
            jnp.sum(grad_queries.astype(jnp.float32), axis=(0, 1)).reshape(local_width),
            jnp.sum(grad_values.astype(jnp.float32), axis=(0, 1)).reshape(local_width),
        ]
    )
    weight_qkv = contract_rows(input_a, grad_projected).reshape(D, 3, local_width)
    grad_input_a = lax.psum(contract_cols(grad_projected, qkv_flat), "tp").reshape(images, SEQ, D)
    grad_shift_one = jnp.sum(grad_input_a, axis=1)
    grad_scale_one = jnp.sum(grad_input_a * normed_one, axis=1)
    grad_tokens = (
        (grad_middle + norm_one_pull(grad_input_a * (1.0 + pieces[:, 1]))[0])
        .reshape(row_count, D)
        .astype(jnp.bfloat16)
    )
    grad_mod = jnp.stack(
        [
            grad_shift_one,
            grad_scale_one,
            grad_gate_one,
            grad_shift_two,
            grad_scale_two,
            grad_gate_two,
        ],
        axis=1,
    ).reshape(images, 6 * D)
    grad_mod_mine = lax.dynamic_slice_in_dim(grad_mod, lax.axis_index("tp") * ada_cols, ada_cols, 1)
    bias_ada = jnp.sum(grad_mod_mine, axis=0)
    weight_ada = lax.dot_general(
        silu_low.astype(jnp.float32),
        grad_mod_mine,
        (((0,), (0,)), ((), ())),
        precision=lax.Precision.HIGHEST,
        preferred_element_type=jnp.float32,
    )
    silu_part = lax.dot_general(
        grad_mod_mine,
        ada_weight.astype(jnp.float32),
        (((1,), (1,)), ((), ())),
        precision=lax.Precision.HIGHEST,
        preferred_element_type=jnp.float32,
    )
    grad_silu = lax.psum(silu_part, "tp")
    grad_condition = silu_pull(grad_silu)[0]
    factor = 1.0 / math.sqrt(row_count * lax.axis_size("dp"))
    sum_ada, sum_qkv, sum_out, sum_fc1, sum_fc2 = (
        lax.psum_scatter(
            weight_ada.astype(jnp.bfloat16), "dp", scatter_dimension=0, tiled=True
        ).astype(jnp.float32),
        lax.psum_scatter(
            weight_qkv.astype(jnp.bfloat16), "dp", scatter_dimension=0, tiled=True
        ).astype(jnp.float32),
        lax.psum_scatter(
            weight_out.astype(jnp.bfloat16), "dp", scatter_dimension=1, tiled=True
        ).astype(jnp.float32),
        lax.psum_scatter(
            weight_fc1.astype(jnp.bfloat16), "dp", scatter_dimension=0, tiled=True
        ).astype(jnp.float32),
        lax.psum_scatter(
            weight_fc2.astype(jnp.bfloat16), "dp", scatter_dimension=1, tiled=True
        ).astype(jnp.float32),
    )
    total_ada, total_qv, total_out, total_fc1, total_fc2 = lax.psum(
        (bias_ada, bias_qv, bias_out, bias_fc1, bias_fc2), "dp"
    )
    return (
        output,
        grad_tokens,
        grad_condition,
        sum_ada * factor,
        total_ada * factor,
        sum_qkv * factor,
        total_qv * factor,
        sum_out * factor,
        total_out * factor,
        sum_fc1 * factor,
        total_fc1 * factor,
        sum_fc2 * factor,
        total_fc2 * factor,
    )

GELU_CUBE = 0.044715
MESH = pl.DeviceIdType.MESH
F32 = jnp.float32
BF16 = jnp.bfloat16


def dot_nn(a, b):
    return lax.dot_general(a, b, (((1,), (0,)), ((), ())), preferred_element_type=F32)


def dot_nt(a, b):
    return lax.dot_general(a, b, (((1,), (1,)), ((), ())), preferred_element_type=F32)


def dot_tn(a, b):
    return lax.dot_general(a, b, (((0,), (0,)), ((), ())), preferred_element_type=F32)


def norm_parts(values):
    center = values - jnp.mean(values, axis=-1, keepdims=True)
    scale = lax.rsqrt(jnp.mean(center * center, axis=-1, keepdims=True) + norm_eps)
    return center * scale, scale


def fold_rows(values):
    rows, cols = values.shape
    return jnp.sum(values.reshape(rows // 8, 8, cols), axis=0)


def total(part):
    return jnp.sum(part, axis=0, keepdims=True)


def al(index, unit):
    return pl.multiple_of(index, unit)


RC = 128
PW = 384
NP = 3
MR = 384
MODES = ("zxw", "xzw", "zxw", "xzw", "zxw", "xzw", "xzw", "xzw")
GROUPS = {0: 2, 2: 1, 3: 2, 5: 1, 6: 1, 7: 1}
SCHEDULE = (
    "T0", "hidB", "back0", "M0", "T2", "T3", "back1", "M2", "T5", "M3",
    "A0", "A1", "nb0", "ab0", "M5", "A2", "A3", "nb1", "ab1", "branch",
    "T6", "B1", "B0", "na0", "A4", "B3", "A5", "B2", "M6", "T7",
    "B4", "W1", "W0", "na1", "gmod", "silu", "B5", "W3", "sp1", "M7",
    "W2", "A6", "W4", "sp2", "W5", "B6", "sp3", "fin", "gc", "A7",
    "W6", "ada", "B7", "W7",
)


def block_kernel(
    factor,
    tok_h, cot_h, ada_h, w3_h, wo_h, w1_h, w2_h,
    cond_r, adab_r, qvb_r, ob_r, b1_r, b2_r,
    out_h, gt_h, g2_h, g1_h, gq_h, go_h, gada_h,
    gcond_o, gadab_o, gqvb_o, gob_o, gb1_o, gb2_o,
    big, w3, wo, w1, w2, tok, cot, act, ib, qkv, prob, att, attn, mid, hid, gpre,
    gibs, gibr, g4, rx, rz, ry, ry3, fin, fin3, modb, gmod, dysum, part_s, part_r,
    silu_all, silu_2d, mod_all, mod_2d, bias, bias_r, cpart,
    ld_sem, out_sem, ss, rs, cred,
):
    dp, tp = lax.axis_index("dp"), lax.axis_index("tp")
    z, x, c = dp // 4, (dp // 2) % 2, dp % 2
    zp, zh = z % 2, z // 2
    dev_y = (dp, 1 - tp)
    dev_c = (z * 4 + x * 2 + 1 - c, tp)
    dev_x = (z * 4 + (1 - x) * 2 + c, tp)
    dev_z = ((z + 1 - 2 * zp) * 4 + x * 2 + c, tp)
    dev_w = (((z + 2) % 4) * 4 + x * 2 + c, tp)
    dp_devs = (dev_c, dev_x, dev_z, dev_w)

    ia, gb = act.at[0], act.at[1]
    T, D = tok.shape
    SEQ = T // 2
    L = wo_h.shape[0]
    LP = qkv.shape[2]
    F = w1.shape[1]
    FH = F // 2
    A = modb.shape[2]
    score_scale = 1.0 / math.sqrt(HEAD_DIM)
    blk = D // 8

    barrier = pltpu.get_barrier_semaphore()
    for dev in (dev_y,) + dp_devs:
        pl.semaphore_signal(barrier, inc=1, device_id=dev, device_id_type=MESH)

    counter = [0]

    def remote(src, dst, dev):
        k = counter[0]
        counter[0] += 1
        return pltpu.make_async_remote_copy(
            src_ref=src, dst_ref=dst, send_sem=ss.at[k], recv_sem=rs.at[k],
            device_id=dev, device_id_type=MESH,
        )

    def credit(k, dev):
        pl.semaphore_signal(cred.at[k], inc=1, device_id=dev, device_id_type=MESH)

    def await_credit(k):
        pl.semaphore_wait(cred.at[k], 1)

    lcount = [0]

    def load(src, dst):
        k = lcount[0]
        lcount[0] += 1
        cp = pltpu.make_async_copy(src, dst, ld_sem.at[k])
        cp.start()
        return cp

    ocount = [0]

    def store(src, dst):
        k = ocount[0]
        ocount[0] += 1
        cp = pltpu.make_async_copy(src, dst, out_sem.at[k])
        cp.start()
        return cp

    NA = A // PW
    ld_ada = [load(ada_h.at[:, PW * k : PW * (k + 1)], big.at[k]) for k in range(NA)]
    ld_tok = load(tok_h, tok)
    ld_w3 = [load(w3_h.at[j], w3.at[j, 0:L]) for j in range(3)]
    for j in range(3):
        w3[j, L:LP, :] = jnp.zeros((LP - L, D), BF16)
    for j in range(2):
        wo[j, L:LP, :] = jnp.zeros((LP - L, D), BF16)

    cond = cond_r[...]
    gate = 1.0 / (1.0 + jnp.exp(-cond))

    quart = L // 4
    cut = (quart // 2 + 15) // 16 * 16

    def wo_part(xx, first, count):
        return pl.ds(al((xx * 2 + c) * quart + first, 16), count)

    wo_cuts = ((0, cut), (cut, quart - cut))
    pl.semaphore_wait(barrier, 5)
    cp_wo, cp_wx = [], []

    def send_wo(n):
        rows = wo_part(x, *wo_cuts[n])
        cp_wo.append(remote(wo_h.at[rows], wo.at[tp, rows], dev_y))
        cp_wo[n].start()

    def pass_wo(n):
        cp_wo[n].wait()
        ref = wo.at[1 - tp, wo_part(x, *wo_cuts[n])]
        cp_wx.append(remote(ref, ref, dev_x))
        cp_wx[n].start()

    send_wo(0)

    silu = cond * gate
    silu_all[dp] = silu.astype(BF16).astype(F32)
    silu_low = jnp.concatenate([silu, jnp.zeros((6, D), F32)], axis=0).astype(BF16)
    for k in range(NA):
        ld_ada[k].wait()
        part = dot_nn(silu_low, big[k])[0:2] + adab_r[pl.ds(PW * k, PW)].reshape(1, PW)
        modb[tp, :, PW * k : PW * (k + 1)] = part
    cp_mod = remote(modb.at[tp], modb.at[tp], dev_y)
    cp_mod.start()
    send_wo(1)
    credit(0, dev_c)

    def spread(ref, k):
        width = 1 << k
        span = pl.ds((dp // width) * width, width)
        cp = remote(ref.at[span], ref.at[span], dp_devs[k])
        cp.start()
        return cp

    cp_silu = spread(silu_all, 0)
    ld_cot = load(cot_h, cot)
    ld_wo = load(wo_h, wo.at[tp, 0:L])
    ld_w1 = load(w1_h, w1)
    ld_w2 = load(w2_h, w2)
    ld_tok.wait()
    cp_mod.wait()

    def mvec(which, img):
        return modb[which // 3, img : img + 1, (which % 3) * D : (which % 3 + 1) * D]

    def rows_loop(img, body, init=None, step=RC):
        base = img * SEQ

        def one(r, carry):
            return body(pl.ds(al(base + r * step, step), step), carry)

        return lax.fori_loop(0, SEQ // step, one, init)

    def zeros8(n):
        return tuple(jnp.zeros((8, D), F32) for _ in range(n))

    def image(img):
        return slice(img * SEQ, (img + 1) * SEQ)

    for img in range(2):
        shift, sc = mvec(0, img), 1.0 + mvec(1, img)

        def body(rows, carry):
            normed, _ = norm_parts(tok[rows, :].astype(F32))
            ia[rows, :] = (normed * sc + shift).astype(BF16)
            return carry

        rows_loop(img, body, 0, 16)
    cp_silu.wait()
    cp_silu = spread(silu_all, 1)

    for j in range(3):
        ld_w3[j].wait()

    def project_in(img):
        rows = image(img)
        for j in range(3):
            out = dot_nt(ia[rows, :], w3[j])
            if j != 1:
                bias_j = qvb_r[j // 2 : j // 2 + 1, :]
                qkv[j, rows, 0:L] = (out[:, 0:L] + bias_j).astype(BF16)
                qkv[j, rows, L:LP] = jnp.zeros((SEQ, LP - L), BF16)
            else:
                qkv[j, rows, :] = out.astype(BF16)

    lane = lax.broadcasted_iota(jnp.int32, (1, 256), 1)

    def head_mask(j, e):
        lo = 16 * j + HEAD_DIM * e
        return jnp.where((lane >= lo) & (lane < lo + HEAD_DIM), 1.0, 0.0).astype(BF16)

    def keep_low(j, old, new):
        full = lax.broadcasted_iota(jnp.int32, new.shape, 1)
        return jnp.where(full < 16 * j, old.astype(F32), new).astype(BF16)

    def attend(img):
        rows = image(img)
        for j in range(4):
            win = slice(128 * j, 128 * j + 256)
            q, k, v = qkv[0, rows, win], qkv[1, rows, win], qkv[2, rows, win]
            mixed = None
            for e in range(2):
                mask = head_mask(j, e)
                s = dot_nt(q * mask, k) * score_scale
                p = jnp.exp(s - jnp.max(s, axis=-1, keepdims=True))
                p = p * (1.0 / jnp.sum(p, axis=-1, keepdims=True))
                low = p.astype(BF16)
                prob[img * 8 + 2 * j + e] = low
                part = dot_nn(low, v * mask)
                mixed = part if mixed is None else mixed + part
            if j:
                mixed = keep_low(j, g4[3, rows, win], mixed)
            g4[3, rows, win] = mixed.astype(BF16)
        att[tp, rows, :] = g4[3, rows, :]
        cp = remote(att.at[tp, rows], att.at[tp, rows], dev_y)
        cp.start()
        return cp

    project_in(0)
    pass_wo(0)
    cp_silu.wait()
    cp_silu = spread(silu_all, 2)
    cp_att = [attend(0)]
    pass_wo(1)
    own_rows = wo.at[1 - tp, wo_part(x, 0, quart)]
    cp_wc = [remote(own_rows, own_rows, dev_c)]
    cp_wc[0].start()
    project_in(1)
    cp_silu.wait()
    cp_silu = spread(silu_all, 3)
    cp_att.append(attend(1))

    ld_cot.wait()
    acc = zeros8(1)[0]
    for img in range(2):
        gate_b = mvec(5, img)

        def body(rows, carry):
            dy = cot[rows, :].astype(F32)
            low = (dy * gate_b).astype(BF16)
            gb[rows, :] = low
            return (carry[0] + fold_rows(low.astype(F32)), carry[1] + fold_rows(dy))

        acc, dy_sum = rows_loop(img, body, (acc, zeros8(1)[0]), 16)
        dysum[img : img + 1, :] = total(dy_sum)

    O1, OO, O2, OQ = 0, F, F + D, F + 2 * D
    bias[0, :, O2 : O2 + D] = total(acc)

    cp_silu.wait()
    for i in range(16):
        silu_2d[2 * i : 2 * i + 2, :] = silu_all[i]
    ld_wo.wait()
    for cp in cp_wx:
        cp.wait()
    far_rows = wo.at[1 - tp, wo_part(1 - x, 0, quart)]
    cp_wc.append(remote(far_rows, far_rows, dev_c))
    cp_wc[1].start()
    ld_w1.wait()
    ld_w2.wait()

    def project(img):
        rows = image(img)
        cp_att[img].wait()
        attn[rows, :] = (
            dot_nn(att[0, rows, :], wo[0]) + dot_nn(att[1, rows, :], wo[1])
        ) + ob_r[...].reshape(1, D)
        gate_a, shift_b, sc_b = mvec(2, img), mvec(3, img), 1.0 + mvec(4, img)

        def body(r, carry):
            m = tok[r, :].astype(F32) + gate_a * attn[r, :]
            mid[r, :] = m
            normed, _ = norm_parts(m)
            ib[r, :] = (normed * sc_b + shift_b).astype(BF16)
            return carry

        rows_loop(img, body, 0)

    def hidden(h):
        def one(n, carry):
            cols = pl.ds(al(h * FH + n * PW, 128), PW)
            pre = dot_nn(ib[...], w1[:, cols]) + b1_r[cols].reshape(1, PW)
            gh = dot_nt(gb[...], w2[cols, :])
            sq = pre * pre
            th = jnp.tanh(gelu_coef * pre * (1.0 + GELU_CUBE * sq))
            hp = 0.5 + 0.5 * th
            hid[:, cols] = (pre * hp).astype(BF16)
            bend = (0.5 * gelu_coef) * pre * (1.0 - th * th) * (1.0 + (3.0 * GELU_CUBE) * sq)
            low = (gh * (hp + bend)).astype(BF16)
            gpre[:, cols] = low
            bias[0, :, cols] = jnp.sum(low.astype(F32), axis=0, keepdims=True)
            return carry

        lax.fori_loop(0, FH // PW, one, 0)

    def back(img):
        rows = image(img)
        gibs[rows, :] = dot_nt(gpre[rows, :], w1[...]).astype(BF16)
        cp = remote(gibs.at[rows], gibr.at[rows], dev_y)
        cp.start()
        return cp

    cp_c, cp_a, cp_b, cp_w, cp_f, cp_o = {}, {}, {}, {}, {}, {}
    sent, staged = set(), []

    devs = {"x": dev_x, "z": dev_z, "w": dev_w}

    def bits(mode, zz, xx):
        def one(axis):
            if axis == "x":
                return xx
            if axis == "w":
                return zz // 2
            return zz % 2

        return [one(axis) for axis in mode]

    def place(p, s):
        b = bits(MODES[p], s // 2, s % 2)
        return (b[0] * 4 + b[1] * 2 + b[2]) * blk

    def product(p, count, h, m):
        feats = slice(m * MR, (m + 1) * MR)
        if p < 2 * NP:
            cols = pl.ds(al(h * FH + PW * (p % NP), 128), PW * count)
            return dot_tn((gb if p < NP else ib)[:, feats], (hid if p < NP else gpre)[:, cols])
        if p == 2 * NP:
            return dot_tn(ia[:, feats], g4[2 * h])
        return dot_tn(act[h, :, feats], g4[2 * h + 1])

    def product_blocks(p, count, h, put):
        for m in range(D // MR):
            res = product(p, count, h, m)
            for s in range(8):
                lo, hi = max(m * MR, s * blk), min((m + 1) * MR, (s + 1) * blk)
                if lo < hi:
                    for i in range(count):
                        width = res.shape[1] // count
                        base = place(p + i, s) + lo - s * blk
                        put(
                            p + i, slice(base, base + hi - lo),
                            res[lo - m * MR : hi - m * MR, i * width : (i + 1) * width],
                        )

    def land_c(p):
        if p < 2 * NP:
            return big.at[p]
        return w1.at[:, (p - 2 * NP) * LP : (p - 2 * NP + 1) * LP]

    def land_a(p):
        if p < 2 * NP:
            return rx.at[p]
        q = p - 2 * NP
        return w1.at[q * 4 * blk : (q + 1) * 4 * blk, 2 * LP : 3 * LP]

    def land_b(p):
        if p < 2 * NP:
            return rz.at[p]
        q = D + T + (p - 2 * NP) * 2 * blk
        return w2.at[q : q + 2 * blk, 0:LP]

    def land_w(p):
        return ry.at[p] if p < 2 * NP else ry3.at[p - 2 * NP]

    def slot_c(p):
        return big.at[6 + p % NP] if p < 2 * NP else w2.at[0:D, 0:LP]

    def theirs(p, count=1):
        for cur in range(p, p + count):
            old = cur - NP if NP <= cur < 2 * NP else cur - 1 if cur > 2 * NP else None
            if old is not None:
                cp_c[old].wait_send()
                sent.add(old)

        def put(cur, rows, values):
            slot_c(cur)[rows, :] = values.astype(BF16)

        product_blocks(p, count, 1 - c, put)
        for cur in range(p, p + count):
            if len(cp_c) == 0:
                await_credit(0)
            if cur == 2 * NP:
                await_credit(1)
            cp_c[cur] = remote(slot_c(cur), land_c(cur), dev_c)
            cp_c[cur].start()

    def mine(p, count=1):
        for cur in range(p, p + count):
            cp_c[cur].wait_recv()

        def put(cur, rows, values):
            ref = land_c(cur)
            ref[rows, :] = (values + ref[rows, :].astype(F32)).astype(BF16)

        product_blocks(p, count, c, put)
        for cur in range(p, p + count):
            mode = MODES[cur]
            b = bits(mode, z, x)
            rows = pl.ds(al((1 - b[0]) * 4 * blk, 16), 4 * blk)
            cp_a[cur] = remote(land_c(cur).at[rows], land_a(cur), devs[mode[0]])
            if cur >= 2 * NP:
                await_credit(cur - 2 * NP + 2)
            cp_a[cur].start()

    def merge(p, base, arrived, count):
        ref = land_c(p)

        def body(i, carry):
            rows = pl.ds(al(base + i * blk, 16), blk)
            got = arrived[pl.ds(al(i * blk, 16), blk), :].astype(F32)
            ref[rows, :] = (ref[rows, :].astype(F32) + got).astype(BF16)
            return carry

        lax.fori_loop(0, count, body, 0)

    def step_a(p):
        cp_a[p].wait_recv()
        b = bits(MODES[p], z, x)
        base = b[0] * 4 * blk
        merge(p, base, land_a(p), 4)
        rows = pl.ds(al(base + (1 - b[1]) * 2 * blk, 16), 2 * blk)
        cp_b[p] = remote(land_c(p).at[rows], land_b(p), devs[MODES[p][1]])
        if p >= 2 * NP:
            await_credit(p - 2 * NP + 4)
        cp_b[p].start()

    def step_b(p):
        cp_b[p].wait_recv()
        b = bits(MODES[p], z, x)
        base = (b[0] * 4 + b[1] * 2) * blk
        merge(p, base, land_b(p), 2)
        rows = pl.ds(al(base + (1 - b[2]) * blk, 16), blk)
        cp_w[p] = remote(land_c(p).at[rows], land_w(p), devs[MODES[p][2]])
        cp_w[p].start()

    def drain(p):
        cp_o[p].wait()
        cp_f[p].wait_send()

    hb = blk // 2
    keep, give = pl.ds(al(c * hb, 8), hb), pl.ds(al((1 - c) * hb, 8), hb)

    def step_w(p):
        cp_w[p].wait_recv()
        b = bits(MODES[p], z, x)
        base = (b[0] * 4 + b[1] * 2 + b[2]) * blk
        both = land_c(p)[pl.ds(al(base, 16), blk), :].astype(F32)
        both = (both + land_w(p)[...].astype(F32)) * factor
        if p < 2 * NP:
            n = len(staged)
            if n >= 2:
                drain(staged[n - 2])
            staged.append(p)
            stage = fin.at[n % 2]
            stage[...] = both
            cols = pl.ds(al(c * FH + PW * (p % NP), 128), PW)
            targets = [(g2_h if p < NP else g1_h).at[:, cols]]
        else:
            stage = fin3.at[p - 2 * NP]
            stage[...] = both[:, 0:L]
            targets = [gq_h.at[2 * c]] if p == 2 * NP else [gq_h.at[1], go_h]
        k = counter[0]
        for n, dst in enumerate(targets):
            counter[0] = k
            cp_o[p] = pltpu.make_async_copy(stage.at[keep], dst, out_sem.at[8 + p])
            cp_f[p] = remote(stage.at[give], dst, dev_c)

            def go(local=cp_o[p], far=cp_f[p]):
                local.start()
                far.start()

            if len(targets) == 1:
                go()
            else:
                pl.when(c == n)(go)

    def branch():
        out = dot_nn(hid[...], w2[...])
        for img in range(2):
            rows = image(img)
            dy = cot[rows, :].astype(F32)
            part_s[img, 2:3, :] = jnp.sum(dy * out[rows], axis=0, keepdims=True)
        hid[:, 0:D] = out.astype(BF16)

    def norm_b_back(img):
        cp_gib[img].wait()
        gate_a, sc_b = mvec(2, img), 1.0 + mvec(4, img)

        def body(r, carry):
            s_shift, s_scale, s_gate, s_bias = carry
            g = gibs[r, :].astype(F32) + gibr[r, :].astype(F32)
            normed, inv = norm_parts(mid[r, :])
            s_shift += fold_rows(g)
            s_scale += fold_rows(g * normed)
            u = g * sc_b
            m1 = jnp.mean(u, axis=-1, keepdims=True)
            m2 = jnp.mean(u * normed, axis=-1, keepdims=True)
            gm = cot[r, :].astype(F32) + inv * (u - m1 - normed * m2)
            s_gate += fold_rows(gm * attn[r, :])
            low = (gm * gate_a).astype(BF16)
            gb[r, :] = low
            s_bias += fold_rows(low.astype(F32))
            attn[r, :] = gm
            return (s_shift, s_scale, s_gate, s_bias)

        sums = rows_loop(img, body, zeros8(4))
        credit(6 + img, dev_y)
        gmod[1, img : img + 1, 0:D] = total(sums[0])
        gmod[1, img : img + 1, D : 2 * D] = total(sums[1])
        gmod[0, img : img + 1, 2 * D : 3 * D] = total(sums[2])
        cur = total(sums[3])
        bias[0, :, OO : OO + D] = cur if img == 0 else bias[0, :, OO : OO + D] + cur

    def attend_back(img):
        rows = image(img)
        g_all = dot_nt(gb[rows, :], wo[tp]).astype(BF16)
        for j in range(4):
            win = slice(128 * j, 128 * j + 256)
            q, k, v = qkv[0, rows, win], qkv[1, rows, win], qkv[2, rows, win]
            g = g_all[:, win]
            gq = gk = gv = None
            for e in range(2):
                mask = head_mask(j, e)
                gm = g * mask
                low = prob[img * 8 + 2 * j + e]
                p = low.astype(F32)
                gp = dot_nt(gm, v)
                ds = (p * (gp - jnp.sum(p * gp, axis=-1, keepdims=True))).astype(BF16)
                parts = dot_nn(ds, k * mask), dot_tn(ds, q * mask), dot_tn(low, gm)
                if gq is None:
                    gq, gk, gv = parts
                else:
                    gq, gk, gv = gq + parts[0], gk + parts[1], gv + parts[2]
            for i, got in enumerate((gq * score_scale, gk * score_scale, gv)):
                if j:
                    got = keep_low(j, g4[i, rows, win], got)
                g4[i, rows, win] = got.astype(BF16)
        for n, which in enumerate((0, 2)):
            cur = jnp.sum(g4[which, rows, :].astype(F32), axis=0, keepdims=True)
            at = slice(OQ + n * LP, OQ + (n + 1) * LP)
            bias[0, :, at] = cur if img == 0 else bias[0, :, at] + cur
        part = dot_nn(g4[0, rows, :], w3[0])
        part += dot_nn(g4[1, rows, :], w3[1])
        part += dot_nn(g4[2, rows, :], w3[2])
        gibs[rows, :] = part.astype(BF16)
        await_credit(6 + img)
        cp = remote(gibs.at[rows], gibr.at[rows], dev_y)
        cp.start()

        def body(r, carry):
            g = gibs[r, :].astype(F32)
            normed, _ = norm_parts(tok[r, :].astype(F32))
            return (carry[0] + fold_rows(g), carry[1] + fold_rows(g * normed))

        sums = rows_loop(img, body, zeros8(2), 32)
        part_s[img, 0:1, :] = total(sums[0])
        part_s[img, 1:2, :] = total(sums[1])
        return cp

    tails = []

    def norm_a_back(img, cp):
        cp.wait()
        sc_a = 1.0 + mvec(1, img)

        def body(r, carry):
            u = (gibs[r, :].astype(F32) + gibr[r, :].astype(F32)) * sc_a
            normed, inv = norm_parts(tok[r, :].astype(F32))
            m1 = jnp.mean(u, axis=-1, keepdims=True)
            m2 = jnp.mean(u * normed, axis=-1, keepdims=True)
            gibr[r, :] = (attn[r, :] + inv * (u - m1 - normed * m2)).astype(BF16)
            return carry

        rows_loop(img, body, 0)
        rows = image(img)
        tails.append(store(gibr.at[rows], gt_h.at[rows]))

    def finish(img):
        gate_b = mvec(5, img)
        base2 = b2_r[...].reshape(1, D)

        def body(r, carry):
            br = hid[r, 0:D].astype(F32) + w2[pl.ds(al(D + r.start, 16), RC), :].astype(F32)
            ia[r, :] = (mid[r, :] + gate_b * (br + base2)).astype(BF16)
            return carry

        rows_loop(img, body, 0)
        rows = image(img)
        tails.append(store(ia.at[rows], out_h.at[rows]))

    mod_cp = []

    def spread_mod(k):
        if k:
            for cp in mod_cp[-1]:
                cp.wait()
            bias[k] = bias[k - 1] + bias_r[k - 1]
        if k < 4:
            cp = remote(bias.at[k], bias_r.at[k], dp_devs[k])
            cp.start()
            mod_cp.append((spread(mod_all, k), cp))

    def ada_out():
        for i in range(16):
            mod_2d[2 * i : 2 * i + 2, :] = mod_all[i]
        row = lax.broadcasted_iota(jnp.int32, (hb, D), 0)
        col = lax.broadcasted_iota(jnp.int32, (hb, D), 1)
        chosen = jnp.where(col == dp * hb + row, 1.0, 0.0).astype(BF16)
        picked = dot_nt(chosen, silu_2d[...].astype(BF16)).astype(BF16)
        for t in range(3):
            cols = slice(D * t, D * (t + 1))
            whole = mod_2d[:, cols]
            coarse = whole.astype(BF16)
            fine = (whole - coarse.astype(F32)).astype(BF16)
            rows = slice(hb * t, hb * (t + 1))
            mid[rows, :] = (dot_nn(picked, coarse) + dot_nn(picked, fine)) * factor
            tails.append(store(mid.at[rows], gada_h.at[:, cols]))
        gadab_o[...] = (total(mod_2d[...]) * factor).reshape(A)
        sums = bias[4] * factor
        gb1_o[...] = sums[:, O1 : O1 + F].reshape(F)
        gob_o[...] = sums[:, OO : OO + D].reshape(D)
        gb2_o[...] = sums[:, O2 : O2 + D].reshape(D)
        gqvb_o[0:1, :] = sums[:, OQ : OQ + L]
        gqvb_o[1:2, :] = sums[:, OQ + LP : OQ + LP + L]

    for cp in cp_wc:
        cp.wait()
    project(0)
    project(1)
    hidden(1 - c)
    cp_gib, cp_gia, cp_later, done = {}, {}, {}, set()
    back_refs = [wo.at[0, 0:T], wo.at[1, 0:T], hid.at[:, D : 2 * D]]

    def do_back(img):
        cp_gib[img] = back(img)
        if img:
            credit(1, dev_c)
            credit(2, devs[MODES[6][0]])
            credit(3, devs[MODES[7][0]])

    def do_branch():
        branch()
        credit(4, devs[MODES[6][1]])
        credit(5, devs[MODES[7][1]])
        credit(8, dev_y)
        send_part("branch")
        await_credit(8)
        cp_later["br"] = remote(hid.at[:, 0:D], w2.at[D : D + T], dev_y)
        cp_later["br"].start()

    def send_part(name):
        done.add(name)
        if {"ab1", "branch"} <= done:
            cp_later["part"] = remote(part_s, part_r, dev_y)
            cp_later["part"].start()
            cp_later["ada"] = [
                load(ada_h.at[0:LP, D * t : D * (t + 1)], w3.at[t]) for t in range(3)
            ] + [load(ada_h.at[LP:D, D * t : D * (t + 1)], back_refs[t]) for t in range(3)]

    def do_gmod():
        cp_later["part"].wait()
        for img in range(2):
            both = part_s[img] + part_r[img]
            gmod[0, img : img + 1, 0:D] = both[0:1]
            gmod[0, img : img + 1, D : 2 * D] = both[1:2]
            gmod[1, img : img + 1, 2 * D : 3 * D] = (
                both[2:3] + dysum[img : img + 1, :] * b2_r[...].reshape(1, D)
            )
        mod_all[dp] = gmod[tp]
        spread_mod(0)

    def do_silu():
        for cp in cp_later["ada"]:
            cp.wait()
        gm = gmod[tp]
        gm_hi = gm.astype(BF16).astype(F32)
        gm_two = jnp.concatenate([gm_hi, gm - gm_hi, jnp.zeros((4, A), F32)], axis=0)
        gm_two = gm_two.astype(BF16)
        top = sum(dot_nt(gm_two[:, D * t : D * (t + 1)], w3[t]) for t in range(3))
        rest = sum(dot_nt(gm_two[:, D * t : D * (t + 1)], back_refs[t][...]) for t in range(3))
        cpart[tp, :, 0:LP] = top[0:2] + top[2:4]
        cpart[tp, :, LP:D] = rest[0:2] + rest[2:4]
        cp_later["cond"] = remote(cpart.at[tp], cpart.at[tp], dev_y)
        cp_later["cond"].start()

    def do_cond():
        cp_later["cond"].wait()
        gcond_o[...] = (cpart[0] + cpart[1]) * (gate * (1.0 + cond * (1.0 - gate)))

    def do_finish():
        cp_later["br"].wait()
        finish(0)
        finish(1)

    def do_ada():
        spread_mod(4)
        ada_out()

    def attend_back_of(img):
        cp_gia[img] = attend_back(img)
        if img:
            send_part("ab1")

    steps = {
        "hidB": lambda: hidden(c), "branch": do_branch, "gmod": do_gmod, "silu": do_silu,
        "gc": do_cond, "fin": do_finish, "ada": do_ada,
    }
    for n in range(2):
        steps[f"back{n}"] = functools.partial(do_back, n)
        steps[f"nb{n}"] = functools.partial(norm_b_back, n)
        steps[f"ab{n}"] = functools.partial(attend_back_of, n)
        steps[f"na{n}"] = lambda n=n: norm_a_back(n, cp_gia[n])
    for n in range(1, 4):
        steps[f"sp{n}"] = functools.partial(spread_mod, n)
    for p in range(2 * NP + 2):
        steps[f"T{p}"] = functools.partial(theirs, p, GROUPS.get(p))
        steps[f"M{p}"] = functools.partial(mine, p, GROUPS.get(p))
        steps[f"A{p}"] = functools.partial(step_a, p)
        steps[f"B{p}"] = functools.partial(step_b, p)
        steps[f"W{p}"] = functools.partial(step_w, p)
    for name in SCHEDULE:
        steps[name]()
    for p in range(2 * NP + 2):
        if p not in sent:
            cp_c[p].wait_send()
        cp_a[p].wait_send()
        cp_b[p].wait_send()
        cp_w[p].wait_send()
        if p >= 2 * NP or p in staged[-2:]:
            drain(p)
        cp_f[p].wait_recv()
    for cp in tails:
        cp.wait()


VMEM_BYTES = 66977792

def copy_kernel(count, *refs):
    source, target, held = refs[:count], refs[count : 2 * count], refs[2 * count : 3 * count]
    sems = refs[3 * count]
    into = [pltpu.make_async_copy(source[k], held[k], sems.at[0, k]) for k in range(count)]
    out = [pltpu.make_async_copy(held[k], target[k], sems.at[1, k]) for k in range(count)]
    for cp in into:
        cp.start()
    for k in range(count):
        into[k].wait()
        out[k].start()
    for cp in out:
        cp.wait()


def fused(
    tokens, condition, noise_times, cotangent, ada_weight, ada_bias, qkv_weight, qv_bias,
    out_weight, out_bias, fc1_weight, fc1_bias, fc2_weight, fc2_bias,
):
    T, width = tokens.shape
    L, F, A = qkv_weight.shape[2], fc1_weight.shape[1], ada_weight.shape[1]
    LP = -(-L // 128) * 128
    n_dp = lax.axis_size("dp")
    blk = width // 8
    rows = width // n_dp
    sums = F + 2 * width + 2 * LP
    factor = 1.0 / math.sqrt(T * n_dp)
    w3 = jnp.transpose(qkv_weight, (1, 2, 0))
    hbm, vmem = pl.BlockSpec(memory_space=pl.ANY), pl.BlockSpec(memory_space=pltpu.VMEM)
    sds = jax.ShapeDtypeStruct
    low, full = lambda *shape: pltpu.VMEM(shape, BF16), lambda *shape: pltpu.VMEM(shape, F32)
    results = pl.pallas_call(
        functools.partial(block_kernel, factor),
        out_shape=(
            sds((T, width), BF16), sds((T, width), BF16),
            sds((rows, F), F32), sds((rows, F), F32),
            sds((3, rows, L), F32), sds((rows, L), F32), sds((rows, A), F32),
            sds((2, width), F32), sds((A,), F32), sds((2, L), F32), sds((width,), F32),
            sds((F,), F32), sds((width,), F32),
        ),
        in_specs=[hbm] * 7 + [vmem] * 6,
        out_specs=(hbm,) * 7 + (vmem,) * 6,
        scratch_shapes=[
            low(A // PW, width, PW),
            low(3, LP, width),
            low(2, LP, width),
            low(width, F),
            low(F, width),
            low(T, width),
            low(T, width),
            low(2, T, width),
            low(T, width),
            low(3, T, LP),
            low(16, T // 2, T // 2),
            low(2, T, LP),
            full(T, width),
            full(T, width),
            low(T, F),
            low(T, F),
            low(T, width),
            low(T, width),
            low(4, T, LP),
            low(6, 4 * blk, PW),
            low(6, 2 * blk, PW),
            low(6, blk, PW),
            low(2, blk, LP),
            full(2, blk, PW),
            full(2, blk, L),
            full(2, 2, A),
            full(2, 2, A),
            full(2, width),
            full(2, 3, width),
            full(2, 3, width),
            full(16, 2, width),
            full(32, width),
            full(16, 2, A),
            full(32, A),
            full(5, 1, sums),
            full(4, 1, sums),
            full(2, 2, width),
            pltpu.SemaphoreType.DMA((24,)),
            pltpu.SemaphoreType.DMA((16,)),
            pltpu.SemaphoreType.DMA((72,)),
            pltpu.SemaphoreType.DMA((72,)),
            pltpu.SemaphoreType.REGULAR((9,)),
        ],
        compiler_params=pltpu.CompilerParams(
            collective_id=0, has_side_effects=True, vmem_limit_bytes=VMEM_BYTES
        ),
        name="block",
    )(
        tokens, cotangent, ada_weight, w3, out_weight, fc1_weight, fc2_weight,
        condition + time_features(noise_times), ada_bias, qv_bias, out_bias, fc1_bias, fc2_bias,
    )
    count = len(results)
    results = pl.pallas_call(
        functools.partial(copy_kernel, count),
        out_shape=tuple(sds(r.shape, r.dtype) for r in results),
        in_specs=[hbm] * count,
        out_specs=(hbm,) * count,
        scratch_shapes=[pltpu.VMEM(r.shape, r.dtype) for r in results]
        + [pltpu.SemaphoreType.DMA((2, count))],
        compiler_params=pltpu.CompilerParams(vmem_limit_bytes=VMEM_BYTES),
        name="results",
    )(*results)
    (
        output, grad_tokens, g2, g1, gqkv, gout, gada, gcond, gada_b, gqv_b, gout_b, g1_b, g2_b,
    ) = results
    return (
        output, grad_tokens, gcond, gada, gada_b, jnp.transpose(gqkv, (1, 0, 2)), gqv_b,
        gout.T, gout_b, g1, g1_b, g2.T, g2_b,
    )


def local(*args):
    tokens, condition, qkv_weight, fc1_weight = args[0], args[1], args[6], args[10]
    fits = (
        lax.axis_size("tp") == 2 and lax.axis_size("dp") == 16
        and condition.shape[0] == 2 and tokens.shape[0] == 2 * SEQ
        and qkv_weight.shape[2] == D // 2 and fc1_weight.shape[1] == 2 * D
    )
    return fused(*args) if fits else plain(*args)


def solution(mesh):
    return jax.shard_map(
        local,
        mesh=mesh,
        in_specs=(
            P("dp", None),
            P("dp", None),
            P("dp"),
            P("dp", None),
            P(None, "tp"),
            P("tp"),
            P(None, None, "tp"),
            P(None, "tp"),
            P("tp", None),
            P(),
            P(None, "tp"),
            P("tp"),
            P("tp", None),
            P(),
        ),
        out_specs=(
            P("dp", None),
            P("dp", None),
            P("dp", None),
            P("dp", "tp"),
            P("tp"),
            P("dp", None, "tp"),
            P(None, "tp"),
            P("tp", "dp"),
            P(),
            P("dp", "tp"),
            P("tp"),
            P("tp", "dp"),
            P(),
        ),
        check_vma=False,
    )
```

```python
import functools
import math

import jax
import jax.numpy as jnp
from jax import lax
from jax.experimental import pallas as pl
from jax.experimental.pallas import tpu as pltpu
from jax.sharding import PartitionSpec as P

D = 1152
HEAD_DIM = 72
SEQ = 256


norm_eps = 1e-06
gelu_coef = 0.7978845608028654


def layer_norm(values):
    center = values - jnp.mean(values, axis=-1, keepdims=True)
    variance = jnp.mean(center * center, axis=-1, keepdims=True)
    return center * lax.rsqrt(variance + norm_eps)


def gelu_tanh(values):
    return (
        0.5 * values * (1.0 + jnp.tanh(gelu_coef * (values + 0.044715 * values * values * values)))
    )


def time_features(noise_times):
    half_width = D // 2
    ladder = jnp.arange(half_width).astype(jnp.float32)
    frequency = jnp.exp(-math.log(10000.0) * ladder / half_width)
    angles = 1000.0 * noise_times[:, None] * frequency[None, :]
    return jnp.concatenate([jnp.cos(angles), jnp.sin(angles)], axis=1)


def contract_rows(former, latter):
    return lax.dot_general(
        former, latter, (((0,), (0,)), ((), ())), preferred_element_type=jnp.float32
    )


def contract_cols(former, latter):
    return lax.dot_general(
        former, latter, (((1,), (1,)), ((), ())), preferred_element_type=jnp.float32
    )


def feed_up(input_b, fc1_weight, fc1_bias, fc2_weight):
    hidden_pre = jnp.dot(input_b, fc1_weight, preferred_element_type=jnp.float32) + fc1_bias
    hidden_act, gelu_pull = jax.vjp(gelu_tanh, hidden_pre)
    hidden = hidden_act.astype(jnp.bfloat16)
    return (hidden, gelu_pull, jnp.dot(hidden, fc2_weight, preferred_element_type=jnp.float32))


def plain(
    tokens,
    condition,
    noise_times,
    cotangent,
    ada_weight,
    ada_bias,
    qkv_weight,
    qv_bias,
    out_weight,
    out_bias,
    fc1_weight,
    fc1_bias,
    fc2_weight,
    fc2_bias,
):
    images = condition.shape[0]
    row_count = tokens.shape[0]
    local_width = qkv_weight.shape[2]
    local_heads = local_width // HEAD_DIM
    ada_cols = ada_weight.shape[1]
    score_scale = 1.0 / math.sqrt(HEAD_DIM)
    cond_total = condition + time_features(noise_times)
    silu_cond, silu_pull = jax.vjp(jax.nn.silu, cond_total)
    silu_low = silu_cond.astype(jnp.bfloat16)
    mod_part = jnp.dot(silu_low, ada_weight, preferred_element_type=jnp.float32) + ada_bias
    modulation = lax.all_gather(mod_part, "tp", axis=1, tiled=True)
    pieces = modulation.reshape(images, 6, 1, D)
    residual = tokens.astype(jnp.float32).reshape(images, SEQ, D)
    normed_one, norm_one_pull = jax.vjp(layer_norm, residual)
    input_a = (
        (normed_one * (1.0 + pieces[:, 1]) + pieces[:, 0])
        .astype(jnp.bfloat16)
        .reshape(row_count, D)
    )
    qkv_flat = qkv_weight.reshape(D, 3 * local_width)
    projected = jnp.dot(input_a, qkv_flat, preferred_element_type=jnp.float32).reshape(
        images, SEQ, 3, local_heads, HEAD_DIM
    )
    queries = (projected[:, :, 0] + qv_bias[0].reshape(local_heads, HEAD_DIM)).astype(jnp.bfloat16)
    key_rows = projected[:, :, 1].astype(jnp.bfloat16)
    value_rows = (projected[:, :, 2] + qv_bias[1].reshape(local_heads, HEAD_DIM)).astype(
        jnp.bfloat16
    )
    scores = (
        jnp.einsum("nqhd,nkhd->nhqk", queries, key_rows, preferred_element_type=jnp.float32)
        * score_scale
    )
    log_total = jax.nn.logsumexp(scores, axis=-1, keepdims=True)
    weights = jnp.exp(scores - log_total)
    weights_low = weights.astype(jnp.bfloat16)
    attended = (
        jnp.einsum("nhqk,nkhd->nqhd", weights_low, value_rows, preferred_element_type=jnp.float32)
        .astype(jnp.bfloat16)
        .reshape(row_count, local_width)
    )
    attn_part = jnp.dot(attended, out_weight, preferred_element_type=jnp.float32)
    attention = lax.psum(attn_part, "tp") + out_bias
    attention = attention.reshape(images, SEQ, D)
    middle = residual + pieces[:, 2] * attention
    normed_two, norm_two_pull = jax.vjp(layer_norm, middle)
    input_b = (
        (normed_two * (1.0 + pieces[:, 4]) + pieces[:, 3])
        .astype(jnp.bfloat16)
        .reshape(row_count, D)
    )
    hidden, gelu_pull, mlp_part = feed_up(input_b, fc1_weight, fc1_bias, fc2_weight)
    branch = lax.psum(mlp_part.astype(jnp.bfloat16), "tp").astype(jnp.float32) + fc2_bias
    branch = branch.reshape(images, SEQ, D)
    output = (middle + pieces[:, 5] * branch).reshape(row_count, D).astype(jnp.bfloat16)
    grad_out = cotangent.astype(jnp.float32).reshape(images, SEQ, D)
    grad_gate_two = jnp.sum(grad_out * branch, axis=1)
    grad_branch = (grad_out * pieces[:, 5]).astype(jnp.bfloat16).reshape(row_count, D)
    bias_fc2 = jnp.sum(grad_branch.astype(jnp.float32), axis=0)
    weight_fc2 = contract_rows(hidden, grad_branch)
    grad_hidden = contract_cols(grad_branch, fc2_weight)
    grad_pre = gelu_pull(grad_hidden)[0].astype(jnp.bfloat16)
    bias_fc1 = jnp.sum(grad_pre.astype(jnp.float32), axis=0)
    weight_fc1 = contract_rows(input_b, grad_pre)
    grad_input_b = lax.psum(contract_cols(grad_pre, fc1_weight), "tp").reshape(images, SEQ, D)
    grad_shift_two = jnp.sum(grad_input_b, axis=1)
    grad_scale_two = jnp.sum(grad_input_b * normed_two, axis=1)
    grad_middle = grad_out + norm_two_pull(grad_input_b * (1.0 + pieces[:, 4]))[0]
    grad_gate_one = jnp.sum(grad_middle * attention, axis=1)
    grad_attention = (grad_middle * pieces[:, 2]).astype(jnp.bfloat16).reshape(row_count, D)
    bias_out = jnp.sum(grad_attention.astype(jnp.float32), axis=0)
    weight_out = contract_rows(attended, grad_attention)
    grad_attended = (
        contract_cols(grad_attention, out_weight)
        .astype(jnp.bfloat16)
        .reshape(images, SEQ, local_heads, HEAD_DIM)
    )
    scores_again = (
        jnp.einsum("nqhd,nkhd->nhqk", queries, key_rows, preferred_element_type=jnp.float32)
        * score_scale
    )
    soft_rows = jnp.exp(scores_again - log_total)
    soft_low = soft_rows.astype(jnp.bfloat16)
    grad_values = jnp.einsum(
        "nhqk,nqhd->nkhd", soft_low, grad_attended, preferred_element_type=jnp.float32
    ).astype(jnp.bfloat16)
    grad_soft = jnp.einsum(
        "nqhd,nkhd->nhqk", grad_attended, value_rows, preferred_element_type=jnp.float32
    )
    row_dot = jnp.sum(soft_rows * grad_soft, axis=-1, keepdims=True)
    grad_scores = (soft_rows * (grad_soft - row_dot)).astype(jnp.bfloat16)
    grad_queries = (
        jnp.einsum("nhqk,nkhd->nqhd", grad_scores, key_rows, preferred_element_type=jnp.float32)
        * score_scale
    ).astype(jnp.bfloat16)
    grad_keys = (
        jnp.einsum("nhqk,nqhd->nkhd", grad_scores, queries, preferred_element_type=jnp.float32)
        * score_scale
    ).astype(jnp.bfloat16)
    grad_projected = jnp.stack([grad_queries, grad_keys, grad_values], axis=2).reshape(
        row_count, 3 * local_width
    )
    bias_qv = jnp.stack(
        [
            jnp.sum(grad_queries.astype(jnp.float32), axis=(0, 1)).reshape(local_width),
            jnp.sum(grad_values.astype(jnp.float32), axis=(0, 1)).reshape(local_width),
        ]
    )
    weight_qkv = contract_rows(input_a, grad_projected).reshape(D, 3, local_width)
    grad_input_a = lax.psum(contract_cols(grad_projected, qkv_flat), "tp").reshape(images, SEQ, D)
    grad_shift_one = jnp.sum(grad_input_a, axis=1)
    grad_scale_one = jnp.sum(grad_input_a * normed_one, axis=1)
    grad_tokens = (
        (grad_middle + norm_one_pull(grad_input_a * (1.0 + pieces[:, 1]))[0])
        .reshape(row_count, D)
        .astype(jnp.bfloat16)
    )
    grad_mod = jnp.stack(
        [
            grad_shift_one,
            grad_scale_one,
            grad_gate_one,
            grad_shift_two,
            grad_scale_two,
            grad_gate_two,
        ],
        axis=1,
    ).reshape(images, 6 * D)
    grad_mod_mine = lax.dynamic_slice_in_dim(grad_mod, lax.axis_index("tp") * ada_cols, ada_cols, 1)
    bias_ada = jnp.sum(grad_mod_mine, axis=0)
    weight_ada = lax.dot_general(
        silu_low.astype(jnp.float32),
        grad_mod_mine,
        (((0,), (0,)), ((), ())),
        precision=lax.Precision.HIGHEST,
        preferred_element_type=jnp.float32,
    )
    silu_part = lax.dot_general(
        grad_mod_mine,
        ada_weight.astype(jnp.float32),
        (((1,), (1,)), ((), ())),
        precision=lax.Precision.HIGHEST,
        preferred_element_type=jnp.float32,
    )
    grad_silu = lax.psum(silu_part, "tp")
    grad_condition = silu_pull(grad_silu)[0]
    factor = 1.0 / math.sqrt(row_count * lax.axis_size("dp"))
    sum_ada, sum_qkv, sum_out, sum_fc1, sum_fc2 = (
        lax.psum_scatter(
            weight_ada.astype(jnp.bfloat16), "dp", scatter_dimension=0, tiled=True
        ).astype(jnp.float32),
        lax.psum_scatter(
            weight_qkv.astype(jnp.bfloat16), "dp", scatter_dimension=0, tiled=True
        ).astype(jnp.float32),
        lax.psum_scatter(
            weight_out.astype(jnp.bfloat16), "dp", scatter_dimension=1, tiled=True
        ).astype(jnp.float32),
        lax.psum_scatter(
            weight_fc1.astype(jnp.bfloat16), "dp", scatter_dimension=0, tiled=True
        ).astype(jnp.float32),
        lax.psum_scatter(
            weight_fc2.astype(jnp.bfloat16), "dp", scatter_dimension=1, tiled=True
        ).astype(jnp.float32),
    )
    total_ada, total_qv, total_out, total_fc1, total_fc2 = lax.psum(
        (bias_ada, bias_qv, bias_out, bias_fc1, bias_fc2), "dp"
    )
    return (
        output,
        grad_tokens,
        grad_condition,
        sum_ada * factor,
        total_ada * factor,
        sum_qkv * factor,
        total_qv * factor,
        sum_out * factor,
        total_out * factor,
        sum_fc1 * factor,
        total_fc1 * factor,
        sum_fc2 * factor,
        total_fc2 * factor,
    )

GELU_CUBE = 0.044715
MESH = pl.DeviceIdType.MESH
F32 = jnp.float32
BF16 = jnp.bfloat16


def dot_nn(a, b):
    return lax.dot_general(a, b, (((1,), (0,)), ((), ())), preferred_element_type=F32)


def dot_nt(a, b):
    return lax.dot_general(a, b, (((1,), (1,)), ((), ())), preferred_element_type=F32)


def dot_tn(a, b):
    return lax.dot_general(a, b, (((0,), (0,)), ((), ())), preferred_element_type=F32)


def norm_parts(values):
    center = values - jnp.mean(values, axis=-1, keepdims=True)
    scale = lax.rsqrt(jnp.mean(center * center, axis=-1, keepdims=True) + norm_eps)
    return center * scale, scale


def fold_rows(values):
    rows, cols = values.shape
    return jnp.sum(values.reshape(rows // 8, 8, cols), axis=0)


def total(part):
    return jnp.sum(part, axis=0, keepdims=True)


def al(index, unit):
    return pl.multiple_of(index, unit)


RC = 128
PW = 384
NP = 3
MR = 384
MODES = ("zxw", "xzw", "zxw", "xzw", "xzw", "xzw", "zxw", "xzw")
GROUPS = {0: 1, 1: 2, 3: 1, 4: 2, 6: 1, 7: 1}
SCHEDULE = (
    "hA1", "hB0", "T1", "hB1", "back0", "M1", "T4", "back1", "T0", "M4",
    "T3", "A2", "A1", "M0", "nb0", "M3", "ab0", "A4", "B1", "nb1",
    "ab1", "A5", "branch", "T6", "B4", "T7", "B5", "na0", "W1", "A0",
    "B2", "M6", "A3", "W4", "M7", "B0", "W5", "na1", "gmod", "silu",
    "W2", "A6", "A7", "B3", "W0", "sp1", "B6", "fin", "gc", "B7",
    "W3", "sp2", "W6", "sp3", "W7", "ada",
)


def block_kernel(
    factor,
    tok_h, cot_h, ada_h, w3_h, wo_h, w1_h, w2_h,
    cond_r, adab_r, qvb_r, ob_r, b1_r, b2_r,
    out_h, gt_h, g2_h, g1_h, gq_h, go_h, gada_h,
    gcond_o, gadab_o, gqvb_o, gob_o, gb1_o, gb2_o,
    big, w3, wo, w1, w2, tok, cot, act, ib, qkv, prob, att, attn, mid, hid, gpre,
    gibs, gibr, g4, rx, rz, ry, ry3, fin, fin3, modb, gmod, dysum, part_s, part_r,
    silu_all, silu_2d, mod_all, mod_2d, bias, bias_r, cpart,
    ld_sem, out_sem, ss, rs, cred,
):
    dp, tp = lax.axis_index("dp"), lax.axis_index("tp")
    z, x, c = dp // 4, (dp // 2) % 2, dp % 2
    zp, zh = z % 2, z // 2
    dev_y = (dp, 1 - tp)
    dev_c = (z * 4 + x * 2 + 1 - c, tp)
    dev_x = (z * 4 + (1 - x) * 2 + c, tp)
    dev_z = ((z + 1 - 2 * zp) * 4 + x * 2 + c, tp)
    dev_w = (((z + 2) % 4) * 4 + x * 2 + c, tp)
    dp_devs = (dev_w, dev_z, dev_x, dev_c)
    me = c * 8 + x * 4 + zp * 2 + zh

    ia, gb = act.at[0], act.at[1]
    T, D = tok.shape
    SEQ = T // 2
    L = wo_h.shape[0]
    LP = qkv.shape[2]
    F = w1.shape[1]
    FH = F // 2
    A = modb.shape[2]
    score_scale = 1.0 / math.sqrt(HEAD_DIM)
    blk = D // 8

    barrier = pltpu.get_barrier_semaphore()
    for dev in (dev_y,) + dp_devs:
        pl.semaphore_signal(barrier, inc=1, device_id=dev, device_id_type=MESH)

    counter = [0]

    def remote(src, dst, dev):
        k = counter[0]
        counter[0] += 1
        return pltpu.make_async_remote_copy(
            src_ref=src, dst_ref=dst, send_sem=ss.at[k], recv_sem=rs.at[k],
            device_id=dev, device_id_type=MESH,
        )

    def credit(k, dev):
        pl.semaphore_signal(cred.at[k], inc=1, device_id=dev, device_id_type=MESH)

    def await_credit(k):
        pl.semaphore_wait(cred.at[k], 1)

    lcount = [0]

    def load(src, dst):
        k = lcount[0]
        lcount[0] += 1
        cp = pltpu.make_async_copy(src, dst, ld_sem.at[k])
        cp.start()
        return cp

    ocount = [0]

    def store(src, dst):
        k = ocount[0]
        ocount[0] += 1
        cp = pltpu.make_async_copy(src, dst, out_sem.at[k])
        cp.start()
        return cp

    NA = A // PW
    ld_ada = [load(ada_h.at[:, PW * k : PW * (k + 1)], big.at[k]) for k in range(NA)]
    ld_tok = load(tok_h, tok)
    ld_w3 = [load(w3_h.at[j], w3.at[j, 0:L]) for j in range(3)]
    for j in range(3):
        w3[j, L:LP, :] = jnp.zeros((LP - L, D), BF16)
    for j in range(2):
        wo[j, L:LP, :] = jnp.zeros((LP - L, D), BF16)

    cond = cond_r[...]
    gate = 1.0 / (1.0 + jnp.exp(-cond))

    quart = L // 4
    cut = (quart // 2 + 15) // 16 * 16

    def wo_part(xx, first, count):
        return pl.ds(al((xx * 2 + c) * quart + first, 16), count)

    wo_cuts = ((0, cut), (cut, quart - cut))
    pl.semaphore_wait(barrier, 5)
    cp_wo, cp_wx = [], []

    def send_wo(n):
        rows = wo_part(x, *wo_cuts[n])
        cp_wo.append(remote(wo_h.at[rows], wo.at[tp, rows], dev_y))
        cp_wo[n].start()

    def pass_wo(n):
        cp_wo[n].wait()
        ref = wo.at[1 - tp, wo_part(x, *wo_cuts[n])]
        cp_wx.append(remote(ref, ref, dev_x))
        cp_wx[n].start()

    send_wo(0)

    silu = cond * gate
    silu_all[me] = silu.astype(BF16).astype(F32)
    silu_low = jnp.concatenate([silu, jnp.zeros((6, D), F32)], axis=0).astype(BF16)
    for k in range(NA):
        ld_ada[k].wait()
        part = dot_nn(silu_low, big[k])[0:2] + adab_r[pl.ds(PW * k, PW)].reshape(1, PW)
        modb[tp, :, PW * k : PW * (k + 1)] = part
    cp_mod = remote(modb.at[tp], modb.at[tp], dev_y)
    cp_mod.start()
    send_wo(1)
    credit(0, dev_c)

    def spread(ref, k):
        width = 1 << k
        span = pl.ds((me // width) * width, width)
        cp = remote(ref.at[span], ref.at[span], dp_devs[k])
        cp.start()
        return cp

    cp_silu = spread(silu_all, 0)
    ld_cot = load(cot_h, cot)
    ld_wo = load(wo_h, wo.at[tp, 0:L])
    ld_w1 = load(w1_h, w1)
    ld_w2 = load(w2_h, w2)
    ld_tok.wait()
    cp_mod.wait()

    def mvec(which, img):
        return modb[which // 3, img : img + 1, (which % 3) * D : (which % 3 + 1) * D]

    def rows_loop(img, body, init=None, step=RC):
        base = img * SEQ

        def one(r, carry):
            return body(pl.ds(al(base + r * step, step), step), carry)

        return lax.fori_loop(0, SEQ // step, one, init)

    def zeros8(n):
        return tuple(jnp.zeros((8, D), F32) for _ in range(n))

    def image(img):
        return slice(img * SEQ, (img + 1) * SEQ)

    for img in range(2):
        shift, sc = mvec(0, img), 1.0 + mvec(1, img)

        def body(rows, carry):
            normed, _ = norm_parts(tok[rows, :].astype(F32))
            ia[rows, :] = (normed * sc + shift).astype(BF16)
            return carry

        rows_loop(img, body, 0, 16)
    cp_silu.wait()
    cp_silu = spread(silu_all, 1)

    for j in range(3):
        ld_w3[j].wait()

    def project_in(img):
        rows = image(img)
        for j in range(3):
            out = dot_nt(ia[rows, :], w3[j])
            if j != 1:
                bias_j = qvb_r[j // 2 : j // 2 + 1, :]
                qkv[j, rows, 0:L] = (out[:, 0:L] + bias_j).astype(BF16)
                qkv[j, rows, L:LP] = jnp.zeros((SEQ, LP - L), BF16)
            else:
                qkv[j, rows, :] = out.astype(BF16)

    lane = lax.broadcasted_iota(jnp.int32, (1, 256), 1)

    def head_mask(j, e):
        lo = 16 * j + HEAD_DIM * e
        return jnp.where((lane >= lo) & (lane < lo + HEAD_DIM), 1.0, 0.0).astype(BF16)

    def keep_low(j, old, new):
        full = lax.broadcasted_iota(jnp.int32, new.shape, 1)
        return jnp.where(full < 16 * j, old.astype(F32), new).astype(BF16)

    def attend(img):
        rows = image(img)
        for j in range(4):
            win = slice(128 * j, 128 * j + 256)
            q, k, v = qkv[0, rows, win], qkv[1, rows, win], qkv[2, rows, win]
            mixed = None
            for e in range(2):
                mask = head_mask(j, e)
                s = dot_nt(q * mask, k) * score_scale
                p = jnp.exp(s - jnp.max(s, axis=-1, keepdims=True))
                p = p * (1.0 / jnp.sum(p, axis=-1, keepdims=True))
                low = p.astype(BF16)
                prob[img * 8 + 2 * j + e] = low
                part = dot_nn(low, v * mask)
                mixed = part if mixed is None else mixed + part
            if j:
                mixed = keep_low(j, g4[3, rows, win], mixed)
            g4[3, rows, win] = mixed.astype(BF16)
        att[tp, rows, :] = g4[3, rows, :]
        cp = remote(att.at[tp, rows], att.at[tp, rows], dev_y)
        cp.start()
        return cp

    project_in(0)
    pass_wo(0)
    cp_silu.wait()
    cp_silu = spread(silu_all, 2)
    cp_att = [attend(0)]
    pass_wo(1)
    own_rows = wo.at[1 - tp, wo_part(x, 0, quart)]
    cp_wc = [remote(own_rows, own_rows, dev_c)]
    cp_wc[0].start()
    project_in(1)
    cp_silu.wait()
    cp_silu = spread(silu_all, 3)
    cp_att.append(attend(1))

    for cp in cp_wx:
        cp.wait()
    far_rows = wo.at[1 - tp, wo_part(1 - x, 0, quart)]
    cp_wc.append(remote(far_rows, far_rows, dev_c))
    cp_wc[1].start()

    O1, OO, O2, OQ = 0, F, F + D, F + 2 * D

    def branch_grad():
        ld_cot.wait()
        acc = zeros8(1)[0]
        for img in range(2):
            gate_b = mvec(5, img)

            def body(rows, carry):
                dy = cot[rows, :].astype(F32)
                low = (dy * gate_b).astype(BF16)
                gb[rows, :] = low
                return (carry[0] + fold_rows(low.astype(F32)), carry[1] + fold_rows(dy))

            acc, dy_sum = rows_loop(img, body, (acc, zeros8(1)[0]), 16)
            dysum[img : img + 1, :] = total(dy_sum)
        bias[0, :, O2 : O2 + D] = total(acc)

    cp_silu.wait()
    for i in range(16):
        silu_2d[2 * i : 2 * i + 2, :] = silu_all[i]
    ld_wo.wait()
    ld_w1.wait()
    ld_w2.wait()

    def project(img):
        rows = image(img)
        cp_att[img].wait()
        attn[rows, :] = (
            dot_nn(att[0, rows, :], wo[0]) + dot_nn(att[1, rows, :], wo[1])
        ) + ob_r[...].reshape(1, D)
        gate_a, shift_b, sc_b = mvec(2, img), mvec(3, img), 1.0 + mvec(4, img)

        def body(r, carry):
            m = tok[r, :].astype(F32) + gate_a * attn[r, :]
            mid[r, :] = m
            normed, _ = norm_parts(m)
            ib[r, :] = (normed * sc_b + shift_b).astype(BF16)
            return carry

        rows_loop(img, body, 0)

    def hidden(h, first, count):
        def one(n, carry):
            cols = pl.ds(al(h * FH + n * PW, 128), PW)
            pre = dot_nn(ib[...], w1[:, cols]) + b1_r[cols].reshape(1, PW)
            gh = dot_nt(gb[...], w2[cols, :])
            sq = pre * pre
            th = jnp.tanh(gelu_coef * pre * (1.0 + GELU_CUBE * sq))
            hp = 0.5 + 0.5 * th
            hid[:, cols] = (pre * hp).astype(BF16)
            bend = (0.5 * gelu_coef) * pre * (1.0 - th * th) * (1.0 + (3.0 * GELU_CUBE) * sq)
            low = (gh * (hp + bend)).astype(BF16)
            gpre[:, cols] = low
            bias[0, :, cols] = jnp.sum(low.astype(F32), axis=0, keepdims=True)
            return carry

        lax.fori_loop(first, first + count + dp // 16, one, 0)

    def back(img):
        rows = image(img)
        gibs[rows, :] = dot_nt(gpre[rows, :], w1[...]).astype(BF16)
        cp = remote(gibs.at[rows], gibr.at[rows], dev_y)
        cp.start()
        return cp

    cp_c, cp_a, cp_b, cp_w, cp_f, cp_o = {}, {}, {}, {}, {}, {}
    sent, staged = set(), []

    devs = {"x": dev_x, "z": dev_z, "w": dev_w}

    def bits(mode, zz, xx):
        def one(axis):
            if axis == "x":
                return xx
            if axis == "w":
                return zz // 2
            return zz % 2

        return [one(axis) for axis in mode]

    def place(p, s):
        b = bits(MODES[p], s // 2, s % 2)
        return (b[0] * 4 + b[1] * 2 + b[2]) * blk

    def product(p, count, h, m):
        feats = slice(m * MR, (m + 1) * MR)
        if p < 2 * NP:
            cols = pl.ds(al(h * FH + PW * (p % NP), 128), PW * count)
            return dot_tn((gb if p < NP else ib)[:, feats], (hid if p < NP else gpre)[:, cols])
        if p == 2 * NP:
            return dot_tn(ia[:, feats], g4[2 * h])
        return dot_tn(act[h, :, feats], g4[2 * h + 1])

    def product_blocks(p, count, h, put):
        for m in range(D // MR):
            res = product(p, count, h, m)
            for s in range(8):
                lo, hi = max(m * MR, s * blk), min((m + 1) * MR, (s + 1) * blk)
                if lo < hi:
                    for i in range(count):
                        width = res.shape[1] // count
                        base = place(p + i, s) + lo - s * blk
                        put(
                            p + i, slice(base, base + hi - lo),
                            res[lo - m * MR : hi - m * MR, i * width : (i + 1) * width],
                        )

    def land_c(p):
        if p < 2 * NP:
            return big.at[p]
        return w1.at[:, (p - 2 * NP) * LP : (p - 2 * NP + 1) * LP]

    def land_a(p):
        if p < 2 * NP:
            return rx.at[p]
        q = p - 2 * NP
        return w1.at[q * 4 * blk : (q + 1) * 4 * blk, 2 * LP : 3 * LP]

    def land_b(p):
        if p < 2 * NP:
            return rz.at[p]
        q = D + T + (p - 2 * NP) * 2 * blk
        return w2.at[q : q + 2 * blk, 0:LP]

    def land_w(p):
        return ry.at[p] if p < 2 * NP else ry3.at[p - 2 * NP]

    def slot_c(p):
        if p < 2 * NP:
            return [big.at[6 + p % NP]]
        if p == 2 * NP:
            return [w2.at[0:D, 0:LP]]
        return [w2.at[0:D, LP:D], w1.at[:, 3 * LP : 4 * LP + LP - D]]

    def theirs(p, count=1):
        for cur in range(p, p + count):
            old = cur - NP if NP <= cur < 2 * NP else None
            if old is not None:
                for cp in cp_c[old]:
                    cp.wait_send()
                sent.add(old)

        def put(cur, rows, values):
            values = values.astype(BF16)
            at = 0
            for slot in slot_c(cur):
                width = slot.shape[1]
                slot[rows, :] = values[:, at : at + width]
                at += width

        product_blocks(p, count, 1 - c, put)
        for cur in range(p, p + count):
            if len(cp_c) == 0:
                await_credit(0)
            if cur >= 2 * NP and not {2 * NP, 2 * NP + 1} & set(cp_c):
                await_credit(1)
            cp_c[cur] = []
            at = 0
            for slot in slot_c(cur):
                width = slot.shape[1]
                cp = remote(slot, land_c(cur).at[:, at : at + width], dev_c)
                cp.start()
                cp_c[cur].append(cp)
                at += width

    def mine(p, count=1):
        for cur in range(p, p + count):
            for cp in cp_c[cur]:
                cp.wait_recv()

        def put(cur, rows, values):
            ref = land_c(cur)
            ref[rows, :] = (values + ref[rows, :].astype(F32)).astype(BF16)

        product_blocks(p, count, c, put)
        for cur in range(p, p + count):
            mode = MODES[cur]
            b = bits(mode, z, x)
            rows = pl.ds(al((1 - b[0]) * 4 * blk, 16), 4 * blk)
            cp_a[cur] = remote(land_c(cur).at[rows], land_a(cur), devs[mode[0]])
            if cur >= 2 * NP:
                await_credit(cur - 2 * NP + 2)
            cp_a[cur].start()

    def merge(p, base, arrived, count):
        ref = land_c(p)

        def body(i, carry):
            rows = pl.ds(al(base + i * blk, 16), blk)
            got = arrived[pl.ds(al(i * blk, 16), blk), :].astype(F32)
            ref[rows, :] = (ref[rows, :].astype(F32) + got).astype(BF16)
            return carry

        lax.fori_loop(0, count, body, 0)

    def step_a(p):
        cp_a[p].wait_recv()
        b = bits(MODES[p], z, x)
        base = b[0] * 4 * blk
        merge(p, base, land_a(p), 4)
        rows = pl.ds(al(base + (1 - b[1]) * 2 * blk, 16), 2 * blk)
        cp_b[p] = remote(land_c(p).at[rows], land_b(p), devs[MODES[p][1]])
        if p >= 2 * NP:
            await_credit(p - 2 * NP + 4)
        cp_b[p].start()

    def step_b(p):
        cp_b[p].wait_recv()
        b = bits(MODES[p], z, x)
        base = (b[0] * 4 + b[1] * 2) * blk
        merge(p, base, land_b(p), 2)
        rows = pl.ds(al(base + (1 - b[2]) * blk, 16), blk)
        cp_w[p] = remote(land_c(p).at[rows], land_w(p), devs[MODES[p][2]])
        cp_w[p].start()

    def drain(p):
        cp_o[p].wait()
        cp_f[p].wait_send()

    hb = blk // 2
    keep, give = pl.ds(al(c * hb, 8), hb), pl.ds(al((1 - c) * hb, 8), hb)

    def step_w(p):
        cp_w[p].wait_recv()
        b = bits(MODES[p], z, x)
        base = (b[0] * 4 + b[1] * 2 + b[2]) * blk
        both = land_c(p)[pl.ds(al(base, 16), blk), :].astype(F32)
        both = (both + land_w(p)[...].astype(F32)) * factor
        if p < 2 * NP:
            n = len(staged)
            if n >= 2:
                drain(staged[n - 2])
            staged.append(p)
            stage = fin.at[n % 2]
            stage[...] = both
            cols = pl.ds(al(c * FH + PW * (p % NP), 128), PW)
            targets = [(g2_h if p < NP else g1_h).at[:, cols]]
        else:
            stage = fin3.at[p - 2 * NP]
            stage[...] = both[:, 0:L]
            targets = [gq_h.at[2 * c]] if p == 2 * NP else [gq_h.at[1], go_h]
        k = counter[0]
        for n, dst in enumerate(targets):
            counter[0] = k
            cp_o[p] = pltpu.make_async_copy(stage.at[keep], dst, out_sem.at[8 + p])
            cp_f[p] = remote(stage.at[give], dst, dev_c)

            def go(local=cp_o[p], far=cp_f[p]):
                local.start()
                far.start()

            if len(targets) == 1:
                go()
            else:
                pl.when(c == n)(go)

    def branch():
        out = dot_nn(hid[...], w2[...])
        for img in range(2):
            rows = image(img)
            dy = cot[rows, :].astype(F32)
            part_s[img, 2:3, :] = jnp.sum(dy * out[rows], axis=0, keepdims=True)
        hid[:, 0:D] = out.astype(BF16)

    def norm_b_back(img):
        cp_gib[img].wait()
        gate_a, sc_b = mvec(2, img), 1.0 + mvec(4, img)

        def body(r, carry):
            s_shift, s_scale, s_gate, s_bias = carry
            g = gibs[r, :].astype(F32) + gibr[r, :].astype(F32)
            normed, inv = norm_parts(mid[r, :])
            s_shift += fold_rows(g)
            s_scale += fold_rows(g * normed)
            u = g * sc_b
            m1 = jnp.mean(u, axis=-1, keepdims=True)
            m2 = jnp.mean(u * normed, axis=-1, keepdims=True)
            gm = cot[r, :].astype(F32) + inv * (u - m1 - normed * m2)
            s_gate += fold_rows(gm * attn[r, :])
            low = (gm * gate_a).astype(BF16)
            gb[r, :] = low
            s_bias += fold_rows(low.astype(F32))
            attn[r, :] = gm
            return (s_shift, s_scale, s_gate, s_bias)

        sums = rows_loop(img, body, zeros8(4))
        credit(6 + img, dev_y)
        gmod[1, img : img + 1, 0:D] = total(sums[0])
        gmod[1, img : img + 1, D : 2 * D] = total(sums[1])
        gmod[0, img : img + 1, 2 * D : 3 * D] = total(sums[2])
        cur = total(sums[3])
        bias[0, :, OO : OO + D] = cur if img == 0 else bias[0, :, OO : OO + D] + cur

    def attend_back(img):
        rows = image(img)
        g_all = dot_nt(gb[rows, :], wo[tp]).astype(BF16)
        for j in range(4):
            win = slice(128 * j, 128 * j + 256)
            q, k, v = qkv[0, rows, win], qkv[1, rows, win], qkv[2, rows, win]
            g = g_all[:, win]
            gq = gk = gv = None
            for e in range(2):
                mask = head_mask(j, e)
                gm = g * mask
                low = prob[img * 8 + 2 * j + e]
                p = low.astype(F32)
                gp = dot_nt(gm, v)
                ds = (p * (gp - jnp.sum(p * gp, axis=-1, keepdims=True))).astype(BF16)
                parts = dot_nn(ds, k * mask), dot_tn(ds, q * mask), dot_tn(low, gm)
                if gq is None:
                    gq, gk, gv = parts
                else:
                    gq, gk, gv = gq + parts[0], gk + parts[1], gv + parts[2]
            for i, got in enumerate((gq * score_scale, gk * score_scale, gv)):
                if j:
                    got = keep_low(j, g4[i, rows, win], got)
                g4[i, rows, win] = got.astype(BF16)
        for n, which in enumerate((0, 2)):
            cur = jnp.sum(g4[which, rows, :].astype(F32), axis=0, keepdims=True)
            at = slice(OQ + n * LP, OQ + (n + 1) * LP)
            bias[0, :, at] = cur if img == 0 else bias[0, :, at] + cur
        part = dot_nn(g4[0, rows, :], w3[0])
        part += dot_nn(g4[1, rows, :], w3[1])
        part += dot_nn(g4[2, rows, :], w3[2])
        gibs[rows, :] = part.astype(BF16)
        await_credit(6 + img)
        cp = remote(gibs.at[rows], gibr.at[rows], dev_y)
        cp.start()

        def body(r, carry):
            g = gibs[r, :].astype(F32)
            normed, _ = norm_parts(tok[r, :].astype(F32))
            return (carry[0] + fold_rows(g), carry[1] + fold_rows(g * normed))

        sums = rows_loop(img, body, zeros8(2), 32)
        part_s[img, 0:1, :] = total(sums[0])
        part_s[img, 1:2, :] = total(sums[1])
        return cp

    tails = []

    def norm_a_back(img, cp):
        cp.wait()
        sc_a = 1.0 + mvec(1, img)

        def body(r, carry):
            u = (gibs[r, :].astype(F32) + gibr[r, :].astype(F32)) * sc_a
            normed, inv = norm_parts(tok[r, :].astype(F32))
            m1 = jnp.mean(u, axis=-1, keepdims=True)
            m2 = jnp.mean(u * normed, axis=-1, keepdims=True)
            gibr[r, :] = (attn[r, :] + inv * (u - m1 - normed * m2)).astype(BF16)
            return carry

        rows_loop(img, body, 0)
        rows = image(img)
        tails.append(store(gibr.at[rows], gt_h.at[rows]))

    def finish(img):
        gate_b = mvec(5, img)
        base2 = b2_r[...].reshape(1, D)

        def body(r, carry):
            br = hid[r, 0:D].astype(F32) + w2[pl.ds(al(D + r.start, 16), RC), :].astype(F32)
            ia[r, :] = (mid[r, :] + gate_b * (br + base2)).astype(BF16)
            return carry

        rows_loop(img, body, 0)
        rows = image(img)
        tails.append(store(ia.at[rows], out_h.at[rows]))

    mod_cp = []

    def spread_mod(k):
        if k:
            for cp in mod_cp[-1]:
                cp.wait()
            bias[k] = bias[k - 1] + bias_r[k - 1]
        if k < 4:
            cp = remote(bias.at[k], bias_r.at[k], dp_devs[k])
            cp.start()
            mod_cp.append((spread(mod_all, k), cp))

    def ada_out():
        for i in range(16):
            mod_2d[2 * i : 2 * i + 2, :] = mod_all[i]
        row = lax.broadcasted_iota(jnp.int32, (hb, D), 0)
        col = lax.broadcasted_iota(jnp.int32, (hb, D), 1)
        chosen = jnp.where(col == dp * hb + row, 1.0, 0.0).astype(BF16)
        picked = dot_nt(chosen, silu_2d[...].astype(BF16)).astype(BF16)
        for t in range(3):
            cols = slice(D * t, D * (t + 1))
            whole = mod_2d[:, cols]
            coarse = whole.astype(BF16)
            fine = (whole - coarse.astype(F32)).astype(BF16)
            rows = slice(hb * t, hb * (t + 1))
            mid[rows, :] = (dot_nn(picked, coarse) + dot_nn(picked, fine)) * factor
            tails.append(store(mid.at[rows], gada_h.at[:, cols]))
        gadab_o[...] = (total(mod_2d[...]) * factor).reshape(A)
        sums = bias[4] * factor
        gb1_o[...] = sums[:, O1 : O1 + F].reshape(F)
        gob_o[...] = sums[:, OO : OO + D].reshape(D)
        gb2_o[...] = sums[:, O2 : O2 + D].reshape(D)
        gqvb_o[0:1, :] = sums[:, OQ : OQ + L]
        gqvb_o[1:2, :] = sums[:, OQ + LP : OQ + LP + L]

    for cp in cp_wc:
        cp.wait()
    branch_grad()
    project(0)
    project(1)
    hidden(1 - c, 0, 1)
    cp_gib, cp_gia, cp_later, done = {}, {}, {}, set()
    back_refs = [wo.at[0, 0:T], wo.at[1, 0:T], hid.at[:, D : 2 * D]]

    def do_back(img):
        cp_gib[img] = back(img)
        if img:
            credit(1, dev_c)
            credit(2, devs[MODES[6][0]])
            credit(3, devs[MODES[7][0]])

    def do_branch():
        branch()
        credit(4, devs[MODES[6][1]])
        credit(5, devs[MODES[7][1]])
        credit(8, dev_y)
        send_part("branch")
        await_credit(8)
        cp_later["br"] = remote(hid.at[:, 0:D], w2.at[D : D + T], dev_y)
        cp_later["br"].start()

    def send_part(name):
        done.add(name)
        if {"ab1", "branch"} <= done:
            cp_later["part"] = remote(part_s, part_r, dev_y)
            cp_later["part"].start()
            cp_later["ada"] = [
                load(ada_h.at[0:LP, D * t : D * (t + 1)], w3.at[t]) for t in range(3)
            ] + [load(ada_h.at[LP:D, D * t : D * (t + 1)], back_refs[t]) for t in range(3)]

    def do_gmod():
        cp_later["part"].wait()
        for img in range(2):
            both = part_s[img] + part_r[img]
            gmod[0, img : img + 1, 0:D] = both[0:1]
            gmod[0, img : img + 1, D : 2 * D] = both[1:2]
            gmod[1, img : img + 1, 2 * D : 3 * D] = (
                both[2:3] + dysum[img : img + 1, :] * b2_r[...].reshape(1, D)
            )
        mod_all[me] = gmod[tp]
        spread_mod(0)

    def do_silu():
        for cp in cp_later["ada"]:
            cp.wait()
        gm = gmod[tp]
        gm_hi = gm.astype(BF16).astype(F32)
        gm_two = jnp.concatenate([gm_hi, gm - gm_hi, jnp.zeros((4, A), F32)], axis=0)
        gm_two = gm_two.astype(BF16)
        top = sum(dot_nt(gm_two[:, D * t : D * (t + 1)], w3[t]) for t in range(3))
        rest = sum(dot_nt(gm_two[:, D * t : D * (t + 1)], back_refs[t][...]) for t in range(3))
        cpart[tp, :, 0:LP] = top[0:2] + top[2:4]
        cpart[tp, :, LP:D] = rest[0:2] + rest[2:4]
        cp_later["cond"] = remote(cpart.at[tp], cpart.at[tp], dev_y)
        cp_later["cond"].start()

    def do_cond():
        cp_later["cond"].wait()
        gcond_o[...] = (cpart[0] + cpart[1]) * (gate * (1.0 + cond * (1.0 - gate)))

    def do_finish():
        cp_later["br"].wait()
        finish(0)
        finish(1)

    def do_ada():
        spread_mod(4)
        ada_out()

    def attend_back_of(img):
        cp_gia[img] = attend_back(img)
        if img:
            send_part("ab1")

    steps = {
        "hB0": lambda: hidden(c, 0, 1), "hA1": lambda: hidden(1 - c, 1, NP - 1),
        "hB1": lambda: hidden(c, 1, NP - 1), "branch": do_branch, "gmod": do_gmod, "silu": do_silu,
        "gc": do_cond, "fin": do_finish, "ada": do_ada,
    }
    for n in range(2):
        steps[f"back{n}"] = functools.partial(do_back, n)
        steps[f"nb{n}"] = functools.partial(norm_b_back, n)
        steps[f"ab{n}"] = functools.partial(attend_back_of, n)
        steps[f"na{n}"] = lambda n=n: norm_a_back(n, cp_gia[n])
    for n in range(1, 4):
        steps[f"sp{n}"] = functools.partial(spread_mod, n)
    for p in range(2 * NP + 2):
        steps[f"T{p}"] = functools.partial(theirs, p, GROUPS.get(p))
        steps[f"M{p}"] = functools.partial(mine, p, GROUPS.get(p))
        steps[f"A{p}"] = functools.partial(step_a, p)
        steps[f"B{p}"] = functools.partial(step_b, p)
        steps[f"W{p}"] = functools.partial(step_w, p)
    for name in SCHEDULE:
        steps[name]()
    for p in range(2 * NP + 2):
        if p not in sent:
            for cp in cp_c[p]:
                cp.wait_send()
        cp_a[p].wait_send()
        cp_b[p].wait_send()
        cp_w[p].wait_send()
        if p >= 2 * NP or p in staged[-2:]:
            drain(p)
        cp_f[p].wait_recv()
    for cp in tails:
        cp.wait()


VMEM_BYTES = 66977792

def copy_kernel(count, *refs):
    source, target, held = refs[:count], refs[count : 2 * count], refs[2 * count : 3 * count]
    sems = refs[3 * count]
    into = [pltpu.make_async_copy(source[k], held[k], sems.at[0, k]) for k in range(count)]
    out = [pltpu.make_async_copy(held[k], target[k], sems.at[1, k]) for k in range(count)]
    for cp in into:
        cp.start()
    for k in range(count):
        into[k].wait()
        out[k].start()
    for cp in out:
        cp.wait()


def fused(
    tokens, condition, noise_times, cotangent, ada_weight, ada_bias, qkv_weight, qv_bias,
    out_weight, out_bias, fc1_weight, fc1_bias, fc2_weight, fc2_bias,
):
    T, width = tokens.shape
    L, F, A = qkv_weight.shape[2], fc1_weight.shape[1], ada_weight.shape[1]
    LP = -(-L // 128) * 128
    n_dp = lax.axis_size("dp")
    blk = width // 8
    rows = width // n_dp
    sums = F + 2 * width + 2 * LP
    factor = 1.0 / math.sqrt(T * n_dp)
    w3 = jnp.transpose(qkv_weight, (1, 2, 0))
    hbm, vmem = pl.BlockSpec(memory_space=pl.ANY), pl.BlockSpec(memory_space=pltpu.VMEM)
    sds = jax.ShapeDtypeStruct
    low, full = lambda *shape: pltpu.VMEM(shape, BF16), lambda *shape: pltpu.VMEM(shape, F32)
    results = pl.pallas_call(
        functools.partial(block_kernel, factor),
        out_shape=(
            sds((T, width), BF16), sds((T, width), BF16),
            sds((rows, F), F32), sds((rows, F), F32),
            sds((3, rows, L), F32), sds((rows, L), F32), sds((rows, A), F32),
            sds((2, width), F32), sds((A,), F32), sds((2, L), F32), sds((width,), F32),
            sds((F,), F32), sds((width,), F32),
        ),
        in_specs=[hbm] * 7 + [vmem] * 6,
        out_specs=(hbm,) * 7 + (vmem,) * 6,
        scratch_shapes=[
            low(A // PW, width, PW),
            low(3, LP, width),
            low(2, LP, width),
            low(width, F),
            low(F, width),
            low(T, width),
            low(T, width),
            low(2, T, width),
            low(T, width),
            low(3, T, LP),
            low(16, T // 2, T // 2),
            low(2, T, LP),
            full(T, width),
            full(T, width),
            low(T, F),
            low(T, F),
            low(T, width),
            low(T, width),
            low(4, T, LP),
            low(6, 4 * blk, PW),
            low(6, 2 * blk, PW),
            low(6, blk, PW),
            low(2, blk, LP),
            full(2, blk, PW),
            full(2, blk, L),
            full(2, 2, A),
            full(2, 2, A),
            full(2, width),
            full(2, 3, width),
            full(2, 3, width),
            full(16, 2, width),
            full(32, width),
            full(16, 2, A),
            full(32, A),
            full(5, 1, sums),
            full(4, 1, sums),
            full(2, 2, width),
            pltpu.SemaphoreType.DMA((24,)),
            pltpu.SemaphoreType.DMA((16,)),
            pltpu.SemaphoreType.DMA((72,)),
            pltpu.SemaphoreType.DMA((72,)),
            pltpu.SemaphoreType.REGULAR((9,)),
        ],
        compiler_params=pltpu.CompilerParams(
            collective_id=0, has_side_effects=True, vmem_limit_bytes=VMEM_BYTES
        ),
        name="block",
    )(
        tokens, cotangent, ada_weight, w3, out_weight, fc1_weight, fc2_weight,
        condition + time_features(noise_times), ada_bias, qv_bias, out_bias, fc1_bias, fc2_bias,
    )
    count = len(results)
    results = pl.pallas_call(
        functools.partial(copy_kernel, count),
        out_shape=tuple(sds(r.shape, r.dtype) for r in results),
        in_specs=[hbm] * count,
        out_specs=(hbm,) * count,
        scratch_shapes=[pltpu.VMEM(r.shape, r.dtype) for r in results]
        + [pltpu.SemaphoreType.DMA((2, count))],
        compiler_params=pltpu.CompilerParams(vmem_limit_bytes=VMEM_BYTES),
        name="results",
    )(*results)
    (
        output, grad_tokens, g2, g1, gqkv, gout, gada, gcond, gada_b, gqv_b, gout_b, g1_b, g2_b,
    ) = results
    return (
        output, grad_tokens, gcond, gada, gada_b, jnp.transpose(gqkv, (1, 0, 2)), gqv_b,
        gout.T, gout_b, g1, g1_b, g2.T, g2_b,
    )


def local(*args):
    tokens, condition, qkv_weight, fc1_weight = args[0], args[1], args[6], args[10]
    fits = (
        lax.axis_size("tp") == 2 and lax.axis_size("dp") == 16
        and condition.shape[0] == 2 and tokens.shape[0] == 2 * SEQ
        and qkv_weight.shape[2] == D // 2 and fc1_weight.shape[1] == 2 * D
    )
    return fused(*args) if fits else plain(*args)


def solution(mesh):
    return jax.shard_map(
        local,
        mesh=mesh,
        in_specs=(
            P("dp", None),
            P("dp", None),
            P("dp"),
            P("dp", None),
            P(None, "tp"),
            P("tp"),
            P(None, None, "tp"),
            P(None, "tp"),
            P("tp", None),
            P(),
            P(None, "tp"),
            P("tp"),
            P("tp", None),
            P(),
        ),
        out_specs=(
            P("dp", None),
            P("dp", None),
            P("dp", None),
            P("dp", "tp"),
            P("tp"),
            P("dp", None, "tp"),
            P(None, "tp"),
            P("tp", "dp"),
            P(),
            P("dp", "tp"),
            P("tp"),
            P("tp", "dp"),
            P(),
        ),
        check_vma=False,
    )
```

```python
import functools
import math

import jax
import jax.numpy as jnp
from jax import lax
from jax.experimental import pallas as pl
from jax.experimental.pallas import tpu as pltpu
from jax.sharding import PartitionSpec as P

D = 1152
HEAD_DIM = 72
SEQ = 256


norm_eps = 1e-06
gelu_coef = 0.7978845608028654


def layer_norm(values):
    center = values - jnp.mean(values, axis=-1, keepdims=True)
    variance = jnp.mean(center * center, axis=-1, keepdims=True)
    return center * lax.rsqrt(variance + norm_eps)


def gelu_tanh(values):
    return (
        0.5 * values * (1.0 + jnp.tanh(gelu_coef * (values + 0.044715 * values * values * values)))
    )


def time_features(noise_times):
    half_width = D // 2
    ladder = jnp.arange(half_width).astype(jnp.float32)
    frequency = jnp.exp(-math.log(10000.0) * ladder / half_width)
    angles = 1000.0 * noise_times[:, None] * frequency[None, :]
    return jnp.concatenate([jnp.cos(angles), jnp.sin(angles)], axis=1)


def contract_rows(former, latter):
    return lax.dot_general(
        former, latter, (((0,), (0,)), ((), ())), preferred_element_type=jnp.float32
    )


def contract_cols(former, latter):
    return lax.dot_general(
        former, latter, (((1,), (1,)), ((), ())), preferred_element_type=jnp.float32
    )


def feed_up(input_b, fc1_weight, fc1_bias, fc2_weight):
    hidden_pre = jnp.dot(input_b, fc1_weight, preferred_element_type=jnp.float32) + fc1_bias
    hidden_act, gelu_pull = jax.vjp(gelu_tanh, hidden_pre)
    hidden = hidden_act.astype(jnp.bfloat16)
    return (hidden, gelu_pull, jnp.dot(hidden, fc2_weight, preferred_element_type=jnp.float32))


def plain(
    tokens,
    condition,
    noise_times,
    cotangent,
    ada_weight,
    ada_bias,
    qkv_weight,
    qv_bias,
    out_weight,
    out_bias,
    fc1_weight,
    fc1_bias,
    fc2_weight,
    fc2_bias,
):
    images = condition.shape[0]
    row_count = tokens.shape[0]
    local_width = qkv_weight.shape[2]
    local_heads = local_width // HEAD_DIM
    ada_cols = ada_weight.shape[1]
    score_scale = 1.0 / math.sqrt(HEAD_DIM)
    cond_total = condition + time_features(noise_times)
    silu_cond, silu_pull = jax.vjp(jax.nn.silu, cond_total)
    silu_low = silu_cond.astype(jnp.bfloat16)
    mod_part = jnp.dot(silu_low, ada_weight, preferred_element_type=jnp.float32) + ada_bias
    modulation = lax.all_gather(mod_part, "tp", axis=1, tiled=True)
    pieces = modulation.reshape(images, 6, 1, D)
    residual = tokens.astype(jnp.float32).reshape(images, SEQ, D)
    normed_one, norm_one_pull = jax.vjp(layer_norm, residual)
    input_a = (
        (normed_one * (1.0 + pieces[:, 1]) + pieces[:, 0])
        .astype(jnp.bfloat16)
        .reshape(row_count, D)
    )
    qkv_flat = qkv_weight.reshape(D, 3 * local_width)
    projected = jnp.dot(input_a, qkv_flat, preferred_element_type=jnp.float32).reshape(
        images, SEQ, 3, local_heads, HEAD_DIM
    )
    queries = (projected[:, :, 0] + qv_bias[0].reshape(local_heads, HEAD_DIM)).astype(jnp.bfloat16)
    key_rows = projected[:, :, 1].astype(jnp.bfloat16)
    value_rows = (projected[:, :, 2] + qv_bias[1].reshape(local_heads, HEAD_DIM)).astype(
        jnp.bfloat16
    )
    scores = (
        jnp.einsum("nqhd,nkhd->nhqk", queries, key_rows, preferred_element_type=jnp.float32)
        * score_scale
    )
    log_total = jax.nn.logsumexp(scores, axis=-1, keepdims=True)
    weights = jnp.exp(scores - log_total)
    weights_low = weights.astype(jnp.bfloat16)
    attended = (
        jnp.einsum("nhqk,nkhd->nqhd", weights_low, value_rows, preferred_element_type=jnp.float32)
        .astype(jnp.bfloat16)
        .reshape(row_count, local_width)
    )
    attn_part = jnp.dot(attended, out_weight, preferred_element_type=jnp.float32)
    attention = lax.psum(attn_part, "tp") + out_bias
    attention = attention.reshape(images, SEQ, D)
    middle = residual + pieces[:, 2] * attention
    normed_two, norm_two_pull = jax.vjp(layer_norm, middle)
    input_b = (
        (normed_two * (1.0 + pieces[:, 4]) + pieces[:, 3])
        .astype(jnp.bfloat16)
        .reshape(row_count, D)
    )
    hidden, gelu_pull, mlp_part = feed_up(input_b, fc1_weight, fc1_bias, fc2_weight)
    branch = lax.psum(mlp_part.astype(jnp.bfloat16), "tp").astype(jnp.float32) + fc2_bias
    branch = branch.reshape(images, SEQ, D)
    output = (middle + pieces[:, 5] * branch).reshape(row_count, D).astype(jnp.bfloat16)
    grad_out = cotangent.astype(jnp.float32).reshape(images, SEQ, D)
    grad_gate_two = jnp.sum(grad_out * branch, axis=1)
    grad_branch = (grad_out * pieces[:, 5]).astype(jnp.bfloat16).reshape(row_count, D)
    bias_fc2 = jnp.sum(grad_branch.astype(jnp.float32), axis=0)
    weight_fc2 = contract_rows(hidden, grad_branch)
    grad_hidden = contract_cols(grad_branch, fc2_weight)
    grad_pre = gelu_pull(grad_hidden)[0].astype(jnp.bfloat16)
    bias_fc1 = jnp.sum(grad_pre.astype(jnp.float32), axis=0)
    weight_fc1 = contract_rows(input_b, grad_pre)
    grad_input_b = lax.psum(contract_cols(grad_pre, fc1_weight), "tp").reshape(images, SEQ, D)
    grad_shift_two = jnp.sum(grad_input_b, axis=1)
    grad_scale_two = jnp.sum(grad_input_b * normed_two, axis=1)
    grad_middle = grad_out + norm_two_pull(grad_input_b * (1.0 + pieces[:, 4]))[0]
    grad_gate_one = jnp.sum(grad_middle * attention, axis=1)
    grad_attention = (grad_middle * pieces[:, 2]).astype(jnp.bfloat16).reshape(row_count, D)
    bias_out = jnp.sum(grad_attention.astype(jnp.float32), axis=0)
    weight_out = contract_rows(attended, grad_attention)
    grad_attended = (
        contract_cols(grad_attention, out_weight)
        .astype(jnp.bfloat16)
        .reshape(images, SEQ, local_heads, HEAD_DIM)
    )
    scores_again = (
        jnp.einsum("nqhd,nkhd->nhqk", queries, key_rows, preferred_element_type=jnp.float32)
        * score_scale
    )
    soft_rows = jnp.exp(scores_again - log_total)
    soft_low = soft_rows.astype(jnp.bfloat16)
    grad_values = jnp.einsum(
        "nhqk,nqhd->nkhd", soft_low, grad_attended, preferred_element_type=jnp.float32
    ).astype(jnp.bfloat16)
    grad_soft = jnp.einsum(
        "nqhd,nkhd->nhqk", grad_attended, value_rows, preferred_element_type=jnp.float32
    )
    row_dot = jnp.sum(soft_rows * grad_soft, axis=-1, keepdims=True)
    grad_scores = (soft_rows * (grad_soft - row_dot)).astype(jnp.bfloat16)
    grad_queries = (
        jnp.einsum("nhqk,nkhd->nqhd", grad_scores, key_rows, preferred_element_type=jnp.float32)
        * score_scale
    ).astype(jnp.bfloat16)
    grad_keys = (
        jnp.einsum("nhqk,nqhd->nkhd", grad_scores, queries, preferred_element_type=jnp.float32)
        * score_scale
    ).astype(jnp.bfloat16)
    grad_projected = jnp.stack([grad_queries, grad_keys, grad_values], axis=2).reshape(
        row_count, 3 * local_width
    )
    bias_qv = jnp.stack(
        [
            jnp.sum(grad_queries.astype(jnp.float32), axis=(0, 1)).reshape(local_width),
            jnp.sum(grad_values.astype(jnp.float32), axis=(0, 1)).reshape(local_width),
        ]
    )
    weight_qkv = contract_rows(input_a, grad_projected).reshape(D, 3, local_width)
    grad_input_a = lax.psum(contract_cols(grad_projected, qkv_flat), "tp").reshape(images, SEQ, D)
    grad_shift_one = jnp.sum(grad_input_a, axis=1)
    grad_scale_one = jnp.sum(grad_input_a * normed_one, axis=1)
    grad_tokens = (
        (grad_middle + norm_one_pull(grad_input_a * (1.0 + pieces[:, 1]))[0])
        .reshape(row_count, D)
        .astype(jnp.bfloat16)
    )
    grad_mod = jnp.stack(
        [
            grad_shift_one,
            grad_scale_one,
            grad_gate_one,
            grad_shift_two,
            grad_scale_two,
            grad_gate_two,
        ],
        axis=1,
    ).reshape(images, 6 * D)
    grad_mod_mine = lax.dynamic_slice_in_dim(grad_mod, lax.axis_index("tp") * ada_cols, ada_cols, 1)
    bias_ada = jnp.sum(grad_mod_mine, axis=0)
    weight_ada = lax.dot_general(
        silu_low.astype(jnp.float32),
        grad_mod_mine,
        (((0,), (0,)), ((), ())),
        precision=lax.Precision.HIGHEST,
        preferred_element_type=jnp.float32,
    )
    silu_part = lax.dot_general(
        grad_mod_mine,
        ada_weight.astype(jnp.float32),
        (((1,), (1,)), ((), ())),
        precision=lax.Precision.HIGHEST,
        preferred_element_type=jnp.float32,
    )
    grad_silu = lax.psum(silu_part, "tp")
    grad_condition = silu_pull(grad_silu)[0]
    factor = 1.0 / math.sqrt(row_count * lax.axis_size("dp"))
    sum_ada, sum_qkv, sum_out, sum_fc1, sum_fc2 = (
        lax.psum_scatter(
            weight_ada.astype(jnp.bfloat16), "dp", scatter_dimension=0, tiled=True
        ).astype(jnp.float32),
        lax.psum_scatter(
            weight_qkv.astype(jnp.bfloat16), "dp", scatter_dimension=0, tiled=True
        ).astype(jnp.float32),
        lax.psum_scatter(
            weight_out.astype(jnp.bfloat16), "dp", scatter_dimension=1, tiled=True
        ).astype(jnp.float32),
        lax.psum_scatter(
            weight_fc1.astype(jnp.bfloat16), "dp", scatter_dimension=0, tiled=True
        ).astype(jnp.float32),
        lax.psum_scatter(
            weight_fc2.astype(jnp.bfloat16), "dp", scatter_dimension=1, tiled=True
        ).astype(jnp.float32),
    )
    total_ada, total_qv, total_out, total_fc1, total_fc2 = lax.psum(
        (bias_ada, bias_qv, bias_out, bias_fc1, bias_fc2), "dp"
    )
    return (
        output,
        grad_tokens,
        grad_condition,
        sum_ada * factor,
        total_ada * factor,
        sum_qkv * factor,
        total_qv * factor,
        sum_out * factor,
        total_out * factor,
        sum_fc1 * factor,
        total_fc1 * factor,
        sum_fc2 * factor,
        total_fc2 * factor,
    )

GELU_CUBE = 0.044715
MESH = pl.DeviceIdType.MESH
F32 = jnp.float32
BF16 = jnp.bfloat16


def dot_nn(a, b):
    return lax.dot_general(a, b, (((1,), (0,)), ((), ())), preferred_element_type=F32)


def dot_nt(a, b):
    return lax.dot_general(a, b, (((1,), (1,)), ((), ())), preferred_element_type=F32)


def dot_tn(a, b):
    return lax.dot_general(a, b, (((0,), (0,)), ((), ())), preferred_element_type=F32)


def norm_parts(values):
    center = values - jnp.mean(values, axis=-1, keepdims=True)
    scale = lax.rsqrt(jnp.mean(center * center, axis=-1, keepdims=True) + norm_eps)
    return center * scale, scale


def fold_rows(values):
    rows, cols = values.shape
    return jnp.sum(values.reshape(rows // 8, 8, cols), axis=0)


def total(part):
    return jnp.sum(part, axis=0, keepdims=True)


def al(index, unit):
    return pl.multiple_of(index, unit)


RC = 128
PW = 384
NP = 3
MR = 384
MODES = ("zxw", "xzw", "zxw", "xzw", "xzw", "xzw", "zxw", "xzw")
GROUPS = {0: 1, 1: 2, 3: 1, 4: 2, 6: 1, 7: 1}
SCHEDULE = (
    "hA1", "hB0", "T1", "hB1", "back0", "M1", "T4", "back1", "T0", "M4",
    "T3", "A2", "A1", "M0", "nb0", "M3", "ab0", "A4", "B1", "nb1",
    "ab1", "A5", "branch", "T6", "B4", "T7", "B5", "na0", "W1", "A0",
    "B2", "M6", "A3", "W4", "M7", "B0", "W5", "na1", "gmod", "silu",
    "W2", "A6", "A7", "B3", "W0", "sp1", "B6", "fin", "gc", "B7",
    "W3", "sp2", "W6", "sp3", "W7", "ada",
)


def block_kernel(
    factor,
    tok_h, cot_h, ada_h, w3_h, wo_h, w1_h, w2_h,
    cond_r, adab_r, qvb_r, ob_r, b1_r, b2_r,
    out_h, gt_h, g2_h, g1_h, gq_h, go_h, gada_h,
    gcond_o, gadab_o, gqvb_o, gob_o, gb1_o, gb2_o,
    big, w3, wo, w1, w2, tok, cot, act, ib, qkv, prob, att, attn, mid, hid, gpre,
    gibs, gibr, g4, rx, rz, ry, ry3, fin, fin3, modb, gmod, dysum, part_s, part_r,
    silu_all, silu_2d, mod_all, mod_2d, bias, bias_r, cpart,
    ld_sem, out_sem, ss, rs, cred,
):
    dp, tp = lax.axis_index("dp"), lax.axis_index("tp")
    z, x, c = dp // 4, (dp // 2) % 2, dp % 2
    zp, zh = z % 2, z // 2
    dev_y = (dp, 1 - tp)
    dev_c = (z * 4 + x * 2 + 1 - c, tp)
    dev_x = (z * 4 + (1 - x) * 2 + c, tp)
    dev_z = ((z + 1 - 2 * zp) * 4 + x * 2 + c, tp)
    dev_w = (((z + 2) % 4) * 4 + x * 2 + c, tp)
    dp_devs = (dev_w, dev_z, dev_x, dev_c)
    me = c * 8 + x * 4 + zp * 2 + zh

    ia, gb = act.at[0], act.at[1]
    T, D = tok.shape
    SEQ = T // 2
    L = wo_h.shape[0]
    LP = qkv.shape[2]
    F = w1.shape[1]
    FH = F // 2
    A = modb.shape[2]
    score_scale = 1.0 / math.sqrt(HEAD_DIM)
    blk = D // 8

    barrier = pltpu.get_barrier_semaphore()
    for dev in (dev_y,) + dp_devs:
        pl.semaphore_signal(barrier, inc=1, device_id=dev, device_id_type=MESH)

    counter = [0]

    def remote(src, dst, dev):
        k = counter[0]
        counter[0] += 1
        return pltpu.make_async_remote_copy(
            src_ref=src, dst_ref=dst, send_sem=ss.at[k], recv_sem=rs.at[k],
            device_id=dev, device_id_type=MESH,
        )

    def credit(k, dev):
        pl.semaphore_signal(cred.at[k], inc=1, device_id=dev, device_id_type=MESH)

    def await_credit(k):
        pl.semaphore_wait(cred.at[k], 1)

    lcount = [0]

    def load(src, dst):
        k = lcount[0]
        lcount[0] += 1
        cp = pltpu.make_async_copy(src, dst, ld_sem.at[k])
        cp.start()
        return cp

    ocount = [0]

    def store(src, dst):
        k = ocount[0]
        ocount[0] += 1
        cp = pltpu.make_async_copy(src, dst, out_sem.at[k])
        cp.start()
        return cp

    NA = A // PW
    ld_ada = [load(ada_h.at[:, PW * k : PW * (k + 1)], big.at[k]) for k in range(NA)]
    ld_tok = load(tok_h, tok)
    ld_w3 = [load(w3_h.at[j], w3.at[j, 0:L]) for j in range(3)]
    for j in range(3):
        w3[j, L:LP, :] = jnp.zeros((LP - L, D), BF16)
    for j in range(2):
        wo[j, L:LP, :] = jnp.zeros((LP - L, D), BF16)

    cond = cond_r[...]
    gate = 1.0 / (1.0 + jnp.exp(-cond))

    quart = L // 4
    cut = (quart // 2 + 15) // 16 * 16

    def wo_part(xx, first, count):
        return pl.ds(al((xx * 2 + c) * quart + first, 16), count)

    wo_cuts = ((0, cut), (cut, quart - cut))
    pl.semaphore_wait(barrier, 5)
    cp_wo, cp_wx = [], []

    def send_wo(n):
        rows = wo_part(x, *wo_cuts[n])
        cp_wo.append(remote(wo_h.at[rows], wo.at[tp, rows], dev_y))
        cp_wo[n].start()

    def pass_wo(n):
        cp_wo[n].wait()
        ref = wo.at[1 - tp, wo_part(x, *wo_cuts[n])]
        cp_wx.append(remote(ref, ref, dev_x))
        cp_wx[n].start()

    send_wo(0)

    silu = cond * gate
    silu_all[me] = silu.astype(BF16).astype(F32)
    silu_low = jnp.concatenate([silu, jnp.zeros((6, D), F32)], axis=0).astype(BF16)
    for k in range(NA):
        ld_ada[k].wait()
        part = dot_nn(silu_low, big[k])[0:2] + adab_r[pl.ds(PW * k, PW)].reshape(1, PW)
        modb[tp, :, PW * k : PW * (k + 1)] = part
    cp_mod = remote(modb.at[tp], modb.at[tp], dev_y)
    cp_mod.start()
    send_wo(1)
    credit(0, dev_c)

    def spread(ref, k):
        width = 1 << k
        span = pl.ds((me // width) * width, width)
        cp = remote(ref.at[span], ref.at[span], dp_devs[k])
        cp.start()
        return cp

    cp_silu = spread(silu_all, 0)
    ld_cot = load(cot_h, cot)
    ld_wo = load(wo_h, wo.at[tp, 0:L])
    ld_w1 = load(w1_h, w1)
    ld_w2 = load(w2_h, w2)
    ld_tok.wait()
    cp_mod.wait()

    def mvec(which, img):
        return modb[which // 3, img : img + 1, (which % 3) * D : (which % 3 + 1) * D]

    def rows_loop(img, body, init=None, step=RC):
        base = img * SEQ

        def one(r, carry):
            return body(pl.ds(al(base + r * step, step), step), carry)

        return lax.fori_loop(0, SEQ // step, one, init)

    def zeros8(n):
        return tuple(jnp.zeros((8, D), F32) for _ in range(n))

    def image(img):
        return slice(img * SEQ, (img + 1) * SEQ)

    for img in range(2):
        shift, sc = mvec(0, img), 1.0 + mvec(1, img)

        def body(rows, carry):
            normed, _ = norm_parts(tok[rows, :].astype(F32))
            ia[rows, :] = (normed * sc + shift).astype(BF16)
            return carry

        rows_loop(img, body, 0, 16)
    cp_silu.wait()
    cp_silu = spread(silu_all, 1)

    for j in range(3):
        ld_w3[j].wait()

    def project_in(img):
        rows = image(img)
        for j in range(3):
            out = dot_nt(ia[rows, :], w3[j])
            if j != 1:
                bias_j = qvb_r[j // 2 : j // 2 + 1, :]
                qkv[j, rows, 0:L] = (out[:, 0:L] + bias_j).astype(BF16)
                qkv[j, rows, L:LP] = jnp.zeros((SEQ, LP - L), BF16)
            else:
                qkv[j, rows, :] = out.astype(BF16)

    lane = lax.broadcasted_iota(jnp.int32, (1, 256), 1)

    def head_mask(j, e):
        lo = 16 * j + HEAD_DIM * e
        return jnp.where((lane >= lo) & (lane < lo + HEAD_DIM), 1.0, 0.0).astype(BF16)

    def keep_low(j, old, new):
        full = lax.broadcasted_iota(jnp.int32, new.shape, 1)
        return jnp.where(full < 16 * j, old.astype(F32), new).astype(BF16)

    def attend(img):
        rows = image(img)
        for j in range(4):
            win = slice(128 * j, 128 * j + 256)
            q, k, v = qkv[0, rows, win], qkv[1, rows, win], qkv[2, rows, win]
            mixed = None
            for e in range(2):
                mask = head_mask(j, e)
                s = dot_nt(q * mask, k) * score_scale
                p = jnp.exp(s - jnp.max(s, axis=-1, keepdims=True))
                p = p * (1.0 / jnp.sum(p, axis=-1, keepdims=True))
                low = p.astype(BF16)
                prob[img * 8 + 2 * j + e] = low
                part = dot_nn(low, v * mask)
                mixed = part if mixed is None else mixed + part
            if j:
                mixed = keep_low(j, g4[3, rows, win], mixed)
            g4[3, rows, win] = mixed.astype(BF16)
        att[tp, rows, :] = g4[3, rows, :]
        cp = remote(att.at[tp, rows], att.at[tp, rows], dev_y)
        cp.start()
        return cp

    project_in(0)
    pass_wo(0)
    cp_silu.wait()
    cp_silu = spread(silu_all, 2)
    cp_att = [attend(0)]
    pass_wo(1)
    own_rows = wo.at[1 - tp, wo_part(x, 0, quart)]
    cp_wc = [remote(own_rows, own_rows, dev_c)]
    cp_wc[0].start()
    project_in(1)
    cp_silu.wait()
    cp_silu = spread(silu_all, 3)
    cp_att.append(attend(1))

    for cp in cp_wx:
        cp.wait()
    far_rows = wo.at[1 - tp, wo_part(1 - x, 0, quart)]
    cp_wc.append(remote(far_rows, far_rows, dev_c))
    cp_wc[1].start()

    O1, OO, O2, OQ = 0, F, F + D, F + 2 * D

    def branch_grad():
        ld_cot.wait()
        acc = zeros8(1)[0]
        for img in range(2):
            gate_b = mvec(5, img)

            def body(rows, carry):
                dy = cot[rows, :].astype(F32)
                low = (dy * gate_b).astype(BF16)
                gb[rows, :] = low
                return (carry[0] + fold_rows(low.astype(F32)), carry[1] + fold_rows(dy))

            acc, dy_sum = rows_loop(img, body, (acc, zeros8(1)[0]), 16)
            dysum[img : img + 1, :] = total(dy_sum)
        bias[0, :, O2 : O2 + D] = total(acc)

    cp_silu.wait()
    for i in range(16):
        silu_2d[2 * i : 2 * i + 2, :] = silu_all[i]
    ld_wo.wait()
    ld_w1.wait()
    ld_w2.wait()

    def project(img):
        rows = image(img)
        cp_att[img].wait()
        attn[rows, :] = (
            dot_nn(att[0, rows, :], wo[0]) + dot_nn(att[1, rows, :], wo[1])
        ) + ob_r[...].reshape(1, D)
        gate_a, shift_b, sc_b = mvec(2, img), mvec(3, img), 1.0 + mvec(4, img)

        def body(r, carry):
            m = tok[r, :].astype(F32) + gate_a * attn[r, :]
            mid[r, :] = m
            normed, _ = norm_parts(m)
            ib[r, :] = (normed * sc_b + shift_b).astype(BF16)
            return carry

        rows_loop(img, body, 0)

    def hidden(h, first, count):
        def one(n, carry):
            cols = pl.ds(al(h * FH + n * PW, 128), PW)
            pre = dot_nn(ib[...], w1[:, cols]) + b1_r[cols].reshape(1, PW)
            gh = dot_nt(gb[...], w2[cols, :])
            sq = pre * pre
            th = jnp.tanh(gelu_coef * pre * (1.0 + GELU_CUBE * sq))
            hp = 0.5 + 0.5 * th
            hid[:, cols] = (pre * hp).astype(BF16)
            bend = (0.5 * gelu_coef) * pre * (1.0 - th * th) * (1.0 + (3.0 * GELU_CUBE) * sq)
            low = (gh * (hp + bend)).astype(BF16)
            gpre[:, cols] = low
            bias[0, :, cols] = jnp.sum(low.astype(F32), axis=0, keepdims=True)
            return carry

        lax.fori_loop(first, first + count + dp // 16, one, 0)

    def back(img):
        rows = image(img)
        gibs[rows, :] = dot_nt(gpre[rows, :], w1[...]).astype(BF16)
        cp = remote(gibs.at[rows], gibr.at[rows], dev_y)
        cp.start()
        return cp

    cp_c, cp_a, cp_b, cp_w, cp_f, cp_o = {}, {}, {}, {}, {}, {}
    sent, staged = set(), []

    devs = {"x": dev_x, "z": dev_z, "w": dev_w}

    def bits(mode, zz, xx):
        def one(axis):
            if axis == "x":
                return xx
            if axis == "w":
                return zz // 2
            return zz % 2

        return [one(axis) for axis in mode]

    def place(p, s):
        b = bits(MODES[p], s // 2, s % 2)
        return (b[0] * 4 + b[1] * 2 + b[2]) * blk

    def product(p, count, h, m):
        feats = slice(m * MR, (m + 1) * MR)
        if p < 2 * NP:
            cols = pl.ds(al(h * FH + PW * (p % NP), 128), PW * count)
            return dot_tn((gb if p < NP else ib)[:, feats], (hid if p < NP else gpre)[:, cols])
        if p == 2 * NP:
            return dot_tn(ia[:, feats], g4[2 * h])
        return dot_tn(act[h, :, feats], g4[2 * h + 1])

    def product_blocks(p, count, h, put):
        for m in range(D // MR):
            res = product(p, count, h, m)
            for s in range(8):
                lo, hi = max(m * MR, s * blk), min((m + 1) * MR, (s + 1) * blk)
                if lo < hi:
                    for i in range(count):
                        width = res.shape[1] // count
                        base = place(p + i, s) + lo - s * blk
                        put(
                            p + i, slice(base, base + hi - lo),
                            res[lo - m * MR : hi - m * MR, i * width : (i + 1) * width],
                        )

    def land_c(p):
        if p < 2 * NP:
            return big.at[p]
        return w1.at[:, (p - 2 * NP) * LP : (p - 2 * NP + 1) * LP]

    def land_a(p):
        if p < 2 * NP:
            return rx.at[p]
        q = p - 2 * NP
        return w1.at[q * 4 * blk : (q + 1) * 4 * blk, 2 * LP : 3 * LP]

    def land_b(p):
        if p < 2 * NP:
            return rz.at[p]
        q = D + T + (p - 2 * NP) * 2 * blk
        return w2.at[q : q + 2 * blk, 0:LP]

    def land_w(p):
        return ry.at[p] if p < 2 * NP else ry3.at[p - 2 * NP]

    def slot_c(p):
        if p < 2 * NP:
            return [big.at[6 + p % NP]]
        if p == 2 * NP:
            return [w2.at[0:D, 0:LP]]
        return [w2.at[0:D, LP:D], w1.at[:, 3 * LP : 4 * LP + LP - D]]

    def theirs(p, count=1):
        for cur in range(p, p + count):
            old = cur - NP if NP <= cur < 2 * NP else None
            if old is not None:
                for cp in cp_c[old]:
                    cp.wait_send()
                sent.add(old)

        def put(cur, rows, values):
            values = values.astype(BF16)
            at = 0
            for slot in slot_c(cur):
                width = slot.shape[1]
                slot[rows, :] = values[:, at : at + width]
                at += width

        product_blocks(p, count, 1 - c, put)
        for cur in range(p, p + count):
            if len(cp_c) == 0:
                await_credit(0)
            if cur >= 2 * NP and not {2 * NP, 2 * NP + 1} & set(cp_c):
                await_credit(1)
            cp_c[cur] = []
            at = 0
            for slot in slot_c(cur):
                width = slot.shape[1]
                cp = remote(slot, land_c(cur).at[:, at : at + width], dev_c)
                cp.start()
                cp_c[cur].append(cp)
                at += width

    def mine(p, count=1):
        for cur in range(p, p + count):
            for cp in cp_c[cur]:
                cp.wait_recv()

        def put(cur, rows, values):
            ref = land_c(cur)
            ref[rows, :] = (values + ref[rows, :].astype(F32)).astype(BF16)

        product_blocks(p, count, c, put)
        for cur in range(p, p + count):
            mode = MODES[cur]
            b = bits(mode, z, x)
            rows = pl.ds(al((1 - b[0]) * 4 * blk, 16), 4 * blk)
            cp_a[cur] = remote(land_c(cur).at[rows], land_a(cur), devs[mode[0]])
            if cur >= 2 * NP:
                await_credit(cur - 2 * NP + 2)
            cp_a[cur].start()

    def merge(p, base, arrived, count):
        ref = land_c(p)

        def body(i, carry):
            rows = pl.ds(al(base + i * blk, 16), blk)
            got = arrived[pl.ds(al(i * blk, 16), blk), :].astype(F32)
            ref[rows, :] = (ref[rows, :].astype(F32) + got).astype(BF16)
            return carry

        lax.fori_loop(0, count, body, 0)

    def step_a(p):
        cp_a[p].wait_recv()
        b = bits(MODES[p], z, x)
        base = b[0] * 4 * blk
        merge(p, base, land_a(p), 4)
        rows = pl.ds(al(base + (1 - b[1]) * 2 * blk, 16), 2 * blk)
        cp_b[p] = remote(land_c(p).at[rows], land_b(p), devs[MODES[p][1]])
        if p >= 2 * NP:
            await_credit(p - 2 * NP + 4)
        cp_b[p].start()

    def step_b(p):
        cp_b[p].wait_recv()
        b = bits(MODES[p], z, x)
        base = (b[0] * 4 + b[1] * 2) * blk
        merge(p, base, land_b(p), 2)
        rows = pl.ds(al(base + (1 - b[2]) * blk, 16), blk)
        cp_w[p] = remote(land_c(p).at[rows], land_w(p), devs[MODES[p][2]])
        cp_w[p].start()

    def drain(p):
        cp_o[p].wait()
        cp_f[p].wait_send()

    hb = blk // 2
    keep, give = pl.ds(al(c * hb, 8), hb), pl.ds(al((1 - c) * hb, 8), hb)

    def step_w(p):
        cp_w[p].wait_recv()
        b = bits(MODES[p], z, x)
        base = (b[0] * 4 + b[1] * 2 + b[2]) * blk
        both = land_c(p)[pl.ds(al(base, 16), blk), :].astype(F32)
        both = (both + land_w(p)[...].astype(F32)) * factor
        if p < 2 * NP:
            n = len(staged)
            if n >= 2:
                drain(staged[n - 2])
            staged.append(p)
            stage = fin.at[n % 2]
            stage[...] = both
            cols = pl.ds(al(c * FH + PW * (p % NP), 128), PW)
            targets = [(g2_h if p < NP else g1_h).at[:, cols]]
        else:
            stage = fin3.at[p - 2 * NP]
            stage[...] = both[:, 0:L]
            targets = [gq_h.at[2 * c]] if p == 2 * NP else [gq_h.at[1], go_h]
        k = counter[0]
        for n, dst in enumerate(targets):
            counter[0] = k
            cp_o[p] = pltpu.make_async_copy(stage.at[keep], dst, out_sem.at[8 + p])
            cp_f[p] = remote(stage.at[give], dst, dev_c)

            def go(local=cp_o[p], far=cp_f[p]):
                local.start()
                far.start()

            if len(targets) == 1:
                go()
            else:
                pl.when(c == n)(go)

    def branch():
        out = dot_nn(hid[...], w2[...])
        for img in range(2):
            rows = image(img)
            dy = cot[rows, :].astype(F32)
            part_s[img, 2:3, :] = jnp.sum(dy * out[rows], axis=0, keepdims=True)
        hid[:, 0:D] = out.astype(BF16)

    def norm_b_back(img):
        cp_gib[img].wait()
        gate_a, sc_b = mvec(2, img), 1.0 + mvec(4, img)

        def body(r, carry):
            s_shift, s_scale, s_gate, s_bias = carry
            g = gibs[r, :].astype(F32) + gibr[r, :].astype(F32)
            normed, inv = norm_parts(mid[r, :])
            s_shift += fold_rows(g)
            s_scale += fold_rows(g * normed)
            u = g * sc_b
            m1 = jnp.mean(u, axis=-1, keepdims=True)
            m2 = jnp.mean(u * normed, axis=-1, keepdims=True)
            gm = cot[r, :].astype(F32) + inv * (u - m1 - normed * m2)
            s_gate += fold_rows(gm * attn[r, :])
            low = (gm * gate_a).astype(BF16)
            gb[r, :] = low
            s_bias += fold_rows(low.astype(F32))
            attn[r, :] = gm
            return (s_shift, s_scale, s_gate, s_bias)

        sums = rows_loop(img, body, zeros8(4))
        credit(6 + img, dev_y)
        gmod[1, img : img + 1, 0:D] = total(sums[0])
        gmod[1, img : img + 1, D : 2 * D] = total(sums[1])
        gmod[0, img : img + 1, 2 * D : 3 * D] = total(sums[2])
        cur = total(sums[3])
        bias[0, :, OO : OO + D] = cur if img == 0 else bias[0, :, OO : OO + D] + cur

    def attend_back(img):
        rows = image(img)
        g_all = dot_nt(gb[rows, :], wo[tp]).astype(BF16)
        for j in range(4):
            win = slice(128 * j, 128 * j + 256)
            q, k, v = qkv[0, rows, win], qkv[1, rows, win], qkv[2, rows, win]
            g = g_all[:, win]
            gq = gk = gv = None
            for e in range(2):
                mask = head_mask(j, e)
                gm = g * mask
                low = prob[img * 8 + 2 * j + e]
                p = low.astype(F32)
                gp = dot_nt(gm, v)
                ds = (p * (gp - jnp.sum(p * gp, axis=-1, keepdims=True))).astype(BF16)
                parts = dot_nn(ds, k * mask), dot_tn(ds, q * mask), dot_tn(low, gm)
                if gq is None:
                    gq, gk, gv = parts
                else:
                    gq, gk, gv = gq + parts[0], gk + parts[1], gv + parts[2]
            for i, got in enumerate((gq * score_scale, gk * score_scale, gv)):
                if j:
                    got = keep_low(j, g4[i, rows, win], got)
                g4[i, rows, win] = got.astype(BF16)
        for n, which in enumerate((0, 2)):
            cur = jnp.sum(g4[which, rows, :].astype(F32), axis=0, keepdims=True)
            at = slice(OQ + n * LP, OQ + (n + 1) * LP)
            bias[0, :, at] = cur if img == 0 else bias[0, :, at] + cur
        part = dot_nn(g4[0, rows, :], w3[0])
        part += dot_nn(g4[1, rows, :], w3[1])
        part += dot_nn(g4[2, rows, :], w3[2])
        gibs[rows, :] = part.astype(BF16)
        await_credit(6 + img)
        cp = remote(gibs.at[rows], gibr.at[rows], dev_y)
        cp.start()

        def body(r, carry):
            g = gibs[r, :].astype(F32)
            normed, _ = norm_parts(tok[r, :].astype(F32))
            return (carry[0] + fold_rows(g), carry[1] + fold_rows(g * normed))

        sums = rows_loop(img, body, zeros8(2), 32)
        part_s[img, 0:1, :] = total(sums[0])
        part_s[img, 1:2, :] = total(sums[1])
        return cp

    tails = []

    def norm_a_back(img, cp):
        cp.wait()
        sc_a = 1.0 + mvec(1, img)

        def body(r, carry):
            u = (gibs[r, :].astype(F32) + gibr[r, :].astype(F32)) * sc_a
            normed, inv = norm_parts(tok[r, :].astype(F32))
            m1 = jnp.mean(u, axis=-1, keepdims=True)
            m2 = jnp.mean(u * normed, axis=-1, keepdims=True)
            gibr[r, :] = (attn[r, :] + inv * (u - m1 - normed * m2)).astype(BF16)
            return carry

        rows_loop(img, body, 0)
        rows = image(img)
        tails.append(store(gibr.at[rows], gt_h.at[rows]))

    def finish(img):
        gate_b = mvec(5, img)
        base2 = b2_r[...].reshape(1, D)

        def body(r, carry):
            br = hid[r, 0:D].astype(F32) + w2[pl.ds(al(D + r.start, 16), RC), :].astype(F32)
            ia[r, :] = (mid[r, :] + gate_b * (br + base2)).astype(BF16)
            return carry

        rows_loop(img, body, 0)
        rows = image(img)
        tails.append(store(ia.at[rows], out_h.at[rows]))

    mod_cp = []

    def spread_mod(k):
        if k:
            for cp in mod_cp[-1]:
                cp.wait()
            bias[k] = bias[k - 1] + bias_r[k - 1]
        if k < 4:
            cp = remote(bias.at[k], bias_r.at[k], dp_devs[k])
            cp.start()
            mod_cp.append((spread(mod_all, k), cp))

    def ada_out():
        for i in range(16):
            mod_2d[2 * i : 2 * i + 2, :] = mod_all[i]
        row = lax.broadcasted_iota(jnp.int32, (hb, D), 0)
        col = lax.broadcasted_iota(jnp.int32, (hb, D), 1)
        chosen = jnp.where(col == dp * hb + row, 1.0, 0.0).astype(BF16)
        picked = dot_nt(chosen, silu_2d[...].astype(BF16)).astype(BF16)
        for t in range(3):
            cols = slice(D * t, D * (t + 1))
            whole = mod_2d[:, cols]
            coarse = whole.astype(BF16)
            fine = (whole - coarse.astype(F32)).astype(BF16)
            rows = slice(hb * t, hb * (t + 1))
            mid[rows, :] = (dot_nn(picked, coarse) + dot_nn(picked, fine)) * factor
            tails.append(store(mid.at[rows], gada_h.at[:, cols]))
        gadab_o[...] = (total(mod_2d[...]) * factor).reshape(A)
        sums = bias[4] * factor
        gb1_o[...] = sums[:, O1 : O1 + F].reshape(F)
        gob_o[...] = sums[:, OO : OO + D].reshape(D)
        gb2_o[...] = sums[:, O2 : O2 + D].reshape(D)
        gqvb_o[0:1, :] = sums[:, OQ : OQ + L]
        gqvb_o[1:2, :] = sums[:, OQ + LP : OQ + LP + L]

    for cp in cp_wc:
        cp.wait()
    project(0)
    branch_grad()
    project(1)
    hidden(1 - c, 0, 1)
    cp_gib, cp_gia, cp_later, done = {}, {}, {}, set()
    back_refs = [wo.at[0, 0:T], wo.at[1, 0:T], hid.at[:, D : 2 * D]]

    def do_back(img):
        cp_gib[img] = back(img)
        if img:
            credit(1, dev_c)
            credit(2, devs[MODES[6][0]])
            credit(3, devs[MODES[7][0]])

    def do_branch():
        branch()
        credit(4, devs[MODES[6][1]])
        credit(5, devs[MODES[7][1]])
        credit(8, dev_y)
        send_part("branch")
        await_credit(8)
        cp_later["br"] = remote(hid.at[:, 0:D], w2.at[D : D + T], dev_y)
        cp_later["br"].start()

    def send_part(name):
        done.add(name)
        if {"ab1", "branch"} <= done:
            cp_later["part"] = remote(part_s, part_r, dev_y)
            cp_later["part"].start()
            cp_later["ada"] = [
                load(ada_h.at[0:LP, D * t : D * (t + 1)], w3.at[t]) for t in range(3)
            ] + [load(ada_h.at[LP:D, D * t : D * (t + 1)], back_refs[t]) for t in range(3)]

    def do_gmod():
        cp_later["part"].wait()
        for img in range(2):
            both = part_s[img] + part_r[img]
            gmod[0, img : img + 1, 0:D] = both[0:1]
            gmod[0, img : img + 1, D : 2 * D] = both[1:2]
            gmod[1, img : img + 1, 2 * D : 3 * D] = (
                both[2:3] + dysum[img : img + 1, :] * b2_r[...].reshape(1, D)
            )
        mod_all[me] = gmod[tp]
        spread_mod(0)

    def do_silu():
        for cp in cp_later["ada"]:
            cp.wait()
        gm = gmod[tp]
        gm_hi = gm.astype(BF16).astype(F32)
        gm_two = jnp.concatenate([gm_hi, gm - gm_hi, jnp.zeros((4, A), F32)], axis=0)
        gm_two = gm_two.astype(BF16)
        top = sum(dot_nt(gm_two[:, D * t : D * (t + 1)], w3[t]) for t in range(3))
        rest = sum(dot_nt(gm_two[:, D * t : D * (t + 1)], back_refs[t][...]) for t in range(3))
        cpart[tp, :, 0:LP] = top[0:2] + top[2:4]
        cpart[tp, :, LP:D] = rest[0:2] + rest[2:4]
        cp_later["cond"] = remote(cpart.at[tp], cpart.at[tp], dev_y)
        cp_later["cond"].start()

    def do_cond():
        cp_later["cond"].wait()
        gcond_o[...] = (cpart[0] + cpart[1]) * (gate * (1.0 + cond * (1.0 - gate)))

    def do_finish():
        cp_later["br"].wait()
        finish(0)
        finish(1)

    def do_ada():
        spread_mod(4)
        ada_out()

    def attend_back_of(img):
        cp_gia[img] = attend_back(img)
        if img:
            send_part("ab1")

    steps = {
        "hB0": lambda: hidden(c, 0, 1), "hA1": lambda: hidden(1 - c, 1, NP - 1),
        "hB1": lambda: hidden(c, 1, NP - 1), "branch": do_branch, "gmod": do_gmod, "silu": do_silu,
        "gc": do_cond, "fin": do_finish, "ada": do_ada,
    }
    for n in range(2):
        steps[f"back{n}"] = functools.partial(do_back, n)
        steps[f"nb{n}"] = functools.partial(norm_b_back, n)
        steps[f"ab{n}"] = functools.partial(attend_back_of, n)
        steps[f"na{n}"] = lambda n=n: norm_a_back(n, cp_gia[n])
    for n in range(1, 4):
        steps[f"sp{n}"] = functools.partial(spread_mod, n)
    for p in range(2 * NP + 2):
        steps[f"T{p}"] = functools.partial(theirs, p, GROUPS.get(p))
        steps[f"M{p}"] = functools.partial(mine, p, GROUPS.get(p))
        steps[f"A{p}"] = functools.partial(step_a, p)
        steps[f"B{p}"] = functools.partial(step_b, p)
        steps[f"W{p}"] = functools.partial(step_w, p)
    for name in SCHEDULE:
        steps[name]()
    for p in range(2 * NP + 2):
        if p not in sent:
            for cp in cp_c[p]:
                cp.wait_send()
        cp_a[p].wait_send()
        cp_b[p].wait_send()
        cp_w[p].wait_send()
        if p >= 2 * NP or p in staged[-2:]:
            drain(p)
        cp_f[p].wait_recv()
    for cp in tails:
        cp.wait()


VMEM_BYTES = 66977792

def copy_kernel(count, *refs):
    source, target, held = refs[:count], refs[count : 2 * count], refs[2 * count : 3 * count]
    sems = refs[3 * count]
    into = [pltpu.make_async_copy(source[k], held[k], sems.at[0, k]) for k in range(count)]
    out = [pltpu.make_async_copy(held[k], target[k], sems.at[1, k]) for k in range(count)]
    for cp in into:
        cp.start()
    for k in range(count):
        into[k].wait()
        out[k].start()
    for cp in out:
        cp.wait()


def fused(
    tokens, condition, noise_times, cotangent, ada_weight, ada_bias, qkv_weight, qv_bias,
    out_weight, out_bias, fc1_weight, fc1_bias, fc2_weight, fc2_bias,
):
    T, width = tokens.shape
    L, F, A = qkv_weight.shape[2], fc1_weight.shape[1], ada_weight.shape[1]
    LP = -(-L // 128) * 128
    n_dp = lax.axis_size("dp")
    blk = width // 8
    rows = width // n_dp
    sums = F + 2 * width + 2 * LP
    factor = 1.0 / math.sqrt(T * n_dp)
    w3 = jnp.transpose(qkv_weight, (1, 2, 0))
    hbm, vmem = pl.BlockSpec(memory_space=pl.ANY), pl.BlockSpec(memory_space=pltpu.VMEM)
    sds = jax.ShapeDtypeStruct
    low, full = lambda *shape: pltpu.VMEM(shape, BF16), lambda *shape: pltpu.VMEM(shape, F32)
    results = pl.pallas_call(
        functools.partial(block_kernel, factor),
        out_shape=(
            sds((T, width), BF16), sds((T, width), BF16),
            sds((rows, F), F32), sds((rows, F), F32),
            sds((3, rows, L), F32), sds((rows, L), F32), sds((rows, A), F32),
            sds((2, width), F32), sds((A,), F32), sds((2, L), F32), sds((width,), F32),
            sds((F,), F32), sds((width,), F32),
        ),
        in_specs=[hbm] * 7 + [vmem] * 6,
        out_specs=(hbm,) * 7 + (vmem,) * 6,
        scratch_shapes=[
            low(A // PW, width, PW),
            low(3, LP, width),
            low(2, LP, width),
            low(width, F),
            low(F, width),
            low(T, width),
            low(T, width),
            low(2, T, width),
            low(T, width),
            low(3, T, LP),
            low(16, T // 2, T // 2),
            low(2, T, LP),
            full(T, width),
            full(T, width),
            low(T, F),
            low(T, F),
            low(T, width),
            low(T, width),
            low(4, T, LP),
            low(6, 4 * blk, PW),
            low(6, 2 * blk, PW),
            low(6, blk, PW),
            low(2, blk, LP),
            full(2, blk, PW),
            full(2, blk, L),
            full(2, 2, A),
            full(2, 2, A),
            full(2, width),
            full(2, 3, width),
            full(2, 3, width),
            full(16, 2, width),
            full(32, width),
            full(16, 2, A),
            full(32, A),
            full(5, 1, sums),
            full(4, 1, sums),
            full(2, 2, width),
            pltpu.SemaphoreType.DMA((24,)),
            pltpu.SemaphoreType.DMA((16,)),
            pltpu.SemaphoreType.DMA((72,)),
            pltpu.SemaphoreType.DMA((72,)),
            pltpu.SemaphoreType.REGULAR((9,)),
        ],
        compiler_params=pltpu.CompilerParams(
            collective_id=0, has_side_effects=True, vmem_limit_bytes=VMEM_BYTES
        ),
        name="block",
    )(
        tokens, cotangent, ada_weight, w3, out_weight, fc1_weight, fc2_weight,
        condition + time_features(noise_times), ada_bias, qv_bias, out_bias, fc1_bias, fc2_bias,
    )
    count = len(results)
    results = pl.pallas_call(
        functools.partial(copy_kernel, count),
        out_shape=tuple(sds(r.shape, r.dtype) for r in results),
        in_specs=[hbm] * count,
        out_specs=(hbm,) * count,
        scratch_shapes=[pltpu.VMEM(r.shape, r.dtype) for r in results]
        + [pltpu.SemaphoreType.DMA((2, count))],
        compiler_params=pltpu.CompilerParams(vmem_limit_bytes=VMEM_BYTES),
        name="results",
    )(*results)
    (
        output, grad_tokens, g2, g1, gqkv, gout, gada, gcond, gada_b, gqv_b, gout_b, g1_b, g2_b,
    ) = results
    return (
        output, grad_tokens, gcond, gada, gada_b, jnp.transpose(gqkv, (1, 0, 2)), gqv_b,
        gout.T, gout_b, g1, g1_b, g2.T, g2_b,
    )


def local(*args):
    tokens, condition, qkv_weight, fc1_weight = args[0], args[1], args[6], args[10]
    fits = (
        lax.axis_size("tp") == 2 and lax.axis_size("dp") == 16
        and condition.shape[0] == 2 and tokens.shape[0] == 2 * SEQ
        and qkv_weight.shape[2] == D // 2 and fc1_weight.shape[1] == 2 * D
    )
    return fused(*args) if fits else plain(*args)


def solution(mesh):
    return jax.shard_map(
        local,
        mesh=mesh,
        in_specs=(
            P("dp", None),
            P("dp", None),
            P("dp"),
            P("dp", None),
            P(None, "tp"),
            P("tp"),
            P(None, None, "tp"),
            P(None, "tp"),
            P("tp", None),
            P(),
            P(None, "tp"),
            P("tp"),
            P("tp", None),
            P(),
        ),
        out_specs=(
            P("dp", None),
            P("dp", None),
            P("dp", None),
            P("dp", "tp"),
            P("tp"),
            P("dp", None, "tp"),
            P(None, "tp"),
            P("tp", "dp"),
            P(),
            P("dp", "tp"),
            P("tp"),
            P("tp", "dp"),
            P(),
        ),
        check_vma=False,
    )
```
